32 devices in a mesh: seq: 8 (over y, x, core), ch: 4 (over z).
Axes of the slice: x: 2, y: 2, z: 4, core: 2. Of those that a mesh axis runs over, the one named last changes fastest.
Arguments:
- token_ids: int32 [1024], P('seq'), may hold values from 0 to 511
- embedding: bfloat16 [512, 4096], P(None, 'ch'), may hold values from -6 to 6
- short_filter: float32 [7, 4096], P(None, 'ch'), may hold values from -2 to 2
- medium_filter: float32 [128, 4096], P(None, 'ch'), may hold values from -0.5 to 0.5
- long_residue: float32 [16, 4096], P(None, 'ch'), may hold values from -10.5 to 10.5, as said below
- long_rate: float32 [16, 4096], P(None, 'ch'), may hold values from 1e-05 to 0.05
- query_gain: float32 [4096], P('ch'), may hold values from -14 to 14
- key_gain: float32 [4096], P('ch'), may hold values from -14 to 14
Outputs:
- hyena_out: bfloat16 [1024, 4096], P('seq', 'ch')
- attended: bfloat16 [1024, 4096], P('seq', 'ch')
The draws below stay inside these ranges and needn't reach their ends.
Inputs may be any that keep to these rules, and one draw needn't show every extreme that they name: `long_residue`: residues of the long filter's modes.
All inputs are finite; a program needn't handle non-finite values.
Results may differ from the reference program's by a relative error of at most 0.0095.
The reference program's roundings to bfloat16 on the way count: a program that leaves them out, or rounds other values in their place, can miss the bound.
Values may be sent and summed in bfloat16 or wider, within the bound.
No kernel may reach another device: no remote copies, remote signals or barrier semaphores. Data moves between devices by JAX's collectives and lax.ppermute only.
A program may use at most 64 MiB of HBM per device.

```python
import math
import jax
import jax.numpy as jnp
import numpy as np
from jax import lax

C = 4096
HEAD = 128
VOCAB = 512
SHORT = 7
MEDIUM = 128
ORDER = 16
HEADS = 32
LENGTH = 1024


def draw_long_rate(key, part):
    fraction = jax.random.uniform(key, (ORDER, C), jnp.float32)
    log_low = math.log(1e-05)
    log_high = math.log(0.05)
    return jnp.exp(log_low + fraction * (log_high - log_low))


def draw_long_residue(key, part):
    channel_ramp = 1.0 + 0.75 * jnp.arange(C, dtype=jnp.float32) / C
    entries = jnp.clip(jax.random.normal(key, (ORDER, C), jnp.float32), -6.0, 6.0)
    return entries * channel_ramp[None, :]


def gain_pair(key):
    folded = jax.random.fold_in(key, 11)
    key_one, key_two = jax.random.split(folded, 2)
    query_draw = jnp.clip(1.4 * jax.random.normal(key_one, (C,), jnp.float32), -14.0, 14.0)
    key_draw = jnp.clip(1.4 * jax.random.normal(key_two, (C,), jnp.float32), -14.0, 14.0)
    return (query_draw, key_draw)


def draw_query_gain(key, part):
    return gain_pair(key)[0]


def draw_key_gain(key, part):
    return gain_pair(key)[1]


def with_ends(values, stream_key, least, high):
    place = [jax.random.randint(jax.random.fold_in(stream_key, axis), (), 0, length) for axis, length in enumerate(values.shape)]
    widest = values.shape.index(max(values.shape))
    neighbour = place[:widest] + [(place[widest] + 1) % values.shape[widest]] + place[widest + 1:]
    return values.at[tuple(place)].set(least).at[tuple(neighbour)].set(high)


def levels(stream_key, dims, cuts, low, top_value):
    gain = 1.0
    for position, shards_of in cuts:
        steps = jax.random.uniform(jax.random.fold_in(jax.random.fold_in(stream_key, 6), position), (shards_of,), jnp.float32, low / len(cuts), top_value / len(cuts))
        gain = gain * jnp.repeat(jnp.exp(steps), dims[position] // shards_of).reshape((-1,) + (1,) * (len(dims) - 1 - position))
    return gain


def cumulative_ranks(amount, skew):
    loads = [(1 << 20) // math.isqrt(standing ** skew) + 1 for standing in range(1, amount + 1)]
    spread = 1 + sum(loads) // (1 << 30)
    return np.cumsum(np.array([max(1, weight // spread) for weight in loads]))


def skewed_ids(rng, shape, amount, slope):
    grid = cumulative_ranks(amount, slope)
    pick = jax.random.randint(jax.random.fold_in(rng, 1), shape, 0, int(grid[amount - 1]))
    grade = jnp.searchsorted(jnp.asarray(grid, jnp.int32), pick, side="right")
    return jax.random.permutation(jax.random.fold_in(rng, 2), amount)[grade].astype(jnp.int32)


def gaussian(key, dims, width, reach, pieces=(), kind=jnp.bfloat16):
    drawn = jax.random.normal(key, dims, jnp.float32) * width
    if len(pieces) > 0:
        drawn = levels(key, dims, pieces, -0.22, 0.18) * drawn
    return jnp.clip(drawn, min=-reach, max=reach).astype(kind)


def setup_inputs(seed: int = 0) -> dict:
    seeds = jax.random.split(jax.random.key(seed), 9)
    return {
        "token_ids": with_ends(skewed_ids(seeds[0], (LENGTH,), VOCAB, 2), jax.random.fold_in(seeds[0], 3), 0, VOCAB - 1).astype(jnp.int32),
        "embedding": gaussian(seeds[1], (VOCAB, C), 1.0, 6.0, ((1, 4),)),
        "short_filter": gaussian(seeds[2], (SHORT, C), SHORT ** -0.5, 2.0, ((1, 4),), jnp.float32),
        "medium_filter": gaussian(seeds[3], (MEDIUM, C), MEDIUM ** -0.5, 0.5, ((1, 4),), jnp.float32),
        "long_residue": draw_long_residue(jax.random.fold_in(seeds[8], 71), 0),
        "long_rate": draw_long_rate(jax.random.fold_in(seeds[8], 71), 0),
        "query_gain": draw_query_gain(jax.random.fold_in(seeds[8], 71), 0),
        "key_gain": draw_key_gain(jax.random.fold_in(seeds[8], 71), 0),
    }


def rounded(value):
    return lax.optimization_barrier(value.astype(jnp.bfloat16))

def depthwise_conv(signal, tap_weights):
    tap_count = tap_weights.shape[0]
    row_count = signal.shape[0]
    padded = jnp.pad(signal, ((tap_count - 1, 0), (0, 0)))

    def add_tap(tap_index, running):
        start_row = (tap_count - 1 - tap_index).astype(jnp.int32)
        window = lax.dynamic_slice_in_dim(padded, start_row, row_count, 0)
        return running + tap_weights[tap_index] * window
    return lax.fori_loop(0, tap_count, add_tap, jnp.zeros(signal.shape, jnp.float32))

def long_kernel(long_residue, long_rate, length):
    positions = jnp.arange(length, dtype=jnp.int32).astype(jnp.float32)

    def add_mode(mode_index, running):
        decay_rate = long_rate[mode_index]
        mode_weight = long_residue[mode_index] * jnp.sqrt(-jnp.expm1(-2.0 * decay_rate)) / math.sqrt(ORDER)
        return running + mode_weight[None, :] * jnp.exp(-decay_rate[None, :] * positions[:, None])
    return lax.fori_loop(0, ORDER, add_mode, jnp.zeros((length, long_rate.shape[1]), jnp.float32))

def attend_head(operands):
    query_rows, key_rows, value_rows = operands
    length = query_rows.shape[0]
    block_rows = math.gcd(length, 1024)
    score_scale = HEAD ** (-0.5)
    key_index = jnp.arange(length, dtype=jnp.int32)

    def one_block(block_index):
        start_row = block_index * block_rows
        query_part = lax.dynamic_slice_in_dim(query_rows, start_row, block_rows, 0)
        scores = jnp.dot(query_part, key_rows.T, preferred_element_type=jnp.float32) * score_scale
        query_index = start_row + jnp.arange(block_rows, dtype=jnp.int32)
        scores = jnp.where(key_index[None, :] <= query_index[:, None], scores, -1e+30)
        row_peak = lax.optimization_barrier(jnp.max(scores, axis=1, keepdims=True))
        weights = jnp.exp(scores - row_peak)
        row_total = lax.optimization_barrier(jnp.sum(weights, axis=1, keepdims=True))
        blended = jnp.dot(weights.astype(jnp.bfloat16), value_rows, preferred_element_type=jnp.float32)
        return blended / row_total
    outputs = lax.map(one_block, jnp.arange(length // block_rows, dtype=jnp.int32))
    return outputs.reshape(length, value_rows.shape[1])

def reference(token_ids, embedding, short_filter, medium_filter, long_residue, long_rate, query_gain, key_gain):
    embedded = embedding[token_ids]
    embed_float = embedded.astype(jnp.float32)
    short_gated = rounded(embed_float * depthwise_conv(embed_float, short_filter))
    gated_float = short_gated.astype(jnp.float32)
    medium_gated = rounded(gated_float * depthwise_conv(gated_float, medium_filter))
    medium_float = medium_gated.astype(jnp.float32)
    kernel = long_kernel(long_residue, long_rate, LENGTH)
    full_size = 2 * LENGTH
    spectrum = jnp.fft.rfft(medium_float, n=full_size, axis=0) * jnp.fft.rfft(kernel, n=full_size, axis=0)
    long_part = jnp.fft.irfft(spectrum, n=full_size, axis=0)[:LENGTH]
    hyena_out = rounded(medium_float * long_part)
    hyena_float = hyena_out.astype(jnp.float32)
    inverse_scale = lax.rsqrt(lax.optimization_barrier(jnp.sum(hyena_float * hyena_float, axis=1)) / C + 1e-05)
    normed = hyena_float * inverse_scale[:, None]
    values = normed.astype(jnp.bfloat16)
    queries = (normed * query_gain[None, :]).astype(jnp.bfloat16)
    key_rows = (normed * key_gain[None, :]).astype(jnp.bfloat16)
    query_heads = queries.reshape(LENGTH, HEADS, HEAD).transpose(1, 0, 2)
    key_heads = key_rows.reshape(LENGTH, HEADS, HEAD).transpose(1, 0, 2)
    value_heads = values.reshape(LENGTH, HEADS, HEAD).transpose(1, 0, 2)
    outputs = lax.map(attend_head, (query_heads, key_heads, value_heads))
    attended = outputs.transpose(1, 0, 2).reshape(LENGTH, C).astype(jnp.bfloat16)
    return (hyena_out, attended)
```

```python
import functools
import math

import jax
import jax.numpy as jnp
import ml_dtypes
import numpy as np
from jax import lax
from jax.experimental import pallas as pl
from jax.experimental.pallas import tpu as pltpu
from jax.sharding import PartitionSpec as P

C = 4096
HEAD = 128


def shifted(value, axis, steps):
    count = lax.axis_size(axis)
    leading, last = (max(0, -steps), min(count, count - steps))
    return lax.ppermute(value, axis, [(source, source + steps) for source in range(leading, last)])


def swapped(shard, axis, apart):
    return lax.ppermute(shard, axis, [(i, i ^ 1 << apart) for i in range(lax.axis_size(axis))])


def from_behind(shard, axis, by):
    size = lax.axis_size(axis)
    return lax.ppermute(shard, axis, [(i, (i + by) % size) for i in range(size)])


def rounded(value):
    return lax.optimization_barrier(value.astype(jnp.bfloat16))


def depthwise_conv(widened, tap_weights, row_count):
    tap_count = tap_weights.shape[0]

    def add_tap(tap_index, running):
        window = lax.dynamic_slice_in_dim(widened, tap_count - 1 - tap_index, row_count, 0)
        return running + tap_weights[tap_index] * window.astype(jnp.float32)

    return lax.fori_loop(
        0, tap_count, add_tap, jnp.zeros((row_count, widened.shape[1]), jnp.float32)
    )


def long_kernel_rows(residue_mine, rate_mine, length):
    positions = jnp.arange(length, dtype=jnp.int32).astype(jnp.float32)
    mode_total = rate_mine.shape[0]

    def add_mode(mode_index, running):
        decay_rate = rate_mine[mode_index]
        mode_weight = (
            residue_mine[mode_index]
            * jnp.sqrt(-jnp.expm1(-2.0 * decay_rate))
            / math.sqrt(mode_total)
        )
        return running + mode_weight[:, None] * jnp.exp(-decay_rate[:, None] * positions[None, :])

    return lax.fori_loop(
        0, mode_total, add_mode, jnp.zeros((rate_mine.shape[1], length), jnp.float32)
    )


def dft_tables(row_size, column_size, period_size):
    row_index = lax.broadcasted_iota(jnp.int32, (row_size, column_size), 0)
    column_index = lax.broadcasted_iota(jnp.int32, (row_size, column_size), 1)
    angles = (row_index * column_index % period_size).astype(jnp.float32) * (
        2.0 * math.pi / period_size
    )
    return (jnp.cos(angles), jnp.sin(angles))


def forward_dft(signal, outer_size, inner_size):
    highest = lax.Precision.HIGHEST
    cos_outer, sin_outer = dft_tables(outer_size // 2, outer_size, outer_size)
    twiddle_cos, twiddle_sin = dft_tables(outer_size, inner_size, outer_size * inner_size)
    cos_inner, sin_inner = dft_tables(inner_size, inner_size, inner_size)
    step_real = jnp.einsum("pab,ak->pkb", signal, cos_outer, precision=highest)
    step_imag = -jnp.einsum("pab,ak->pkb", signal, sin_outer, precision=highest)
    turned_real = step_real * twiddle_cos + step_imag * twiddle_sin
    turned_imag = step_imag * twiddle_cos - step_real * twiddle_sin
    spec_real = jnp.einsum("pkb,bm->pkm", turned_real, cos_inner, precision=highest) + jnp.einsum(
        "pkb,bm->pkm", turned_imag, sin_inner, precision=highest
    )
    spec_imag = jnp.einsum("pkb,bm->pkm", turned_imag, cos_inner, precision=highest) - jnp.einsum(
        "pkb,bm->pkm", turned_real, sin_inner, precision=highest
    )
    return (spec_real, spec_imag)


def inverse_dft(spec_real, spec_imag, outer_size, inner_size):
    highest = lax.Precision.HIGHEST
    cos_outer, sin_outer = dft_tables(outer_size // 2, outer_size, outer_size)
    twiddle_cos, twiddle_sin = dft_tables(outer_size, inner_size, outer_size * inner_size)
    cos_inner, sin_inner = dft_tables(inner_size, inner_size, inner_size)
    back_real = jnp.einsum("pkm,mb->pkb", spec_real, cos_inner, precision=highest) - jnp.einsum(
        "pkm,mb->pkb", spec_imag, sin_inner, precision=highest
    )
    back_imag = jnp.einsum("pkm,mb->pkb", spec_real, sin_inner, precision=highest) + jnp.einsum(
        "pkm,mb->pkb", spec_imag, cos_inner, precision=highest
    )
    turned_real = back_real * twiddle_cos - back_imag * twiddle_sin
    turned_imag = back_real * twiddle_sin + back_imag * twiddle_cos
    signal = jnp.einsum("pkb,ak->pab", turned_real, cos_outer, precision=highest) - jnp.einsum(
        "pkb,ak->pab", turned_imag, sin_outer, precision=highest
    )
    return signal / (outer_size * inner_size)


def attend_block(query_rows, query_index, key_block, value_block, key_start, running, score_scale):
    row_peak, row_total, blended = running
    scores = (
        jnp.einsum("qhd,khd->hqk", query_rows, key_block, preferred_element_type=jnp.float32)
        * score_scale
    )
    key_index = key_start + jnp.arange(key_block.shape[0], dtype=jnp.int32)
    scores = jnp.where(key_index[None, None, :] <= query_index[None, :, None], scores, -1e30)
    new_peak = jnp.maximum(row_peak, jnp.max(scores, axis=2))
    weights = jnp.exp(scores - new_peak[:, :, None])
    rescale = jnp.exp(row_peak - new_peak)
    row_total = row_total * rescale + jnp.sum(weights, axis=2)
    blended = blended * rescale[:, :, None] + jnp.einsum(
        "hqk,khd->hqd",
        weights.astype(jnp.bfloat16),
        value_block,
        preferred_element_type=jnp.float32,
    )
    return (new_peak, row_total, blended)


def merge_partials(first_part, second_part):
    peak_one, total_one, blend_one = first_part
    peak_two, total_two, blend_two = second_part
    new_peak = jnp.maximum(peak_one, peak_two)
    scale_one = jnp.exp(peak_one - new_peak)
    scale_two = jnp.exp(peak_two - new_peak)
    new_total = total_one * scale_one + total_two * scale_two
    new_blend = blend_one * scale_one[..., None] + blend_two * scale_two[..., None]
    return (new_peak, new_total, new_blend)


def split_halves(stacked_part, half_size, upper_side):
    lower_half = stacked_part[:, :half_size]
    upper_half = stacked_part[:, half_size:]
    keep_half = jnp.where(upper_side == 1, upper_half, lower_half)
    send_half = jnp.where(upper_side == 1, lower_half, upper_half)
    return (keep_half, send_half)


def by_position(
    token_ids, embedding, short_filter, medium_filter, long_residue, long_rate, query_gain, key_gain
):
    tok_count = token_ids.shape[0]
    vocab_size = embedding.shape[0]
    width_dev = embedding.shape[1]
    seq_count = lax.axis_size("seq")
    seq_index = lax.axis_index("seq")
    one_hot = (
        token_ids[:, None] == lax.broadcasted_iota(jnp.int32, (tok_count, vocab_size), 1)
    ).astype(jnp.bfloat16)
    embedded = jnp.dot(one_hot, embedding, preferred_element_type=jnp.float32).astype(jnp.bfloat16)
    short_taps = short_filter.shape[0]
    rim_rows = shifted(embedded[tok_count - (short_taps - 1) :], "seq", 1)
    widened = jnp.concatenate([rim_rows, embedded], axis=0)
    short_part = depthwise_conv(widened, short_filter, tok_count)
    short_gated = rounded(embedded.astype(jnp.float32) * short_part)
    medium_taps = medium_filter.shape[0]
    upper_rows = shifted(short_gated[tok_count - (medium_taps - 1) :], "seq", 1)
    widened_two = jnp.concatenate([upper_rows, short_gated], axis=0)
    medium_part = depthwise_conv(widened_two, medium_filter, tok_count)
    medium_gated = rounded(short_gated.astype(jnp.float32) * medium_part)
    per_dev = width_dev // seq_count
    length = tok_count * seq_count
    grouped = medium_gated.T.reshape(seq_count, per_dev, tok_count)
    spread = lax.all_to_all(grouped, "seq", split_axis=0, concat_axis=2, tiled=True).reshape(
        per_dev, length
    )
    rate_mine = lax.dynamic_slice_in_dim(long_rate, seq_index * per_dev, per_dev, 1)
    residue_mine = lax.dynamic_slice_in_dim(long_residue, seq_index * per_dev, per_dev, 1)
    kernel = long_kernel_rows(residue_mine, rate_mine, length)
    outer_size = 128
    inner_size = 2 * length // outer_size
    spread_float = spread.astype(jnp.float32)
    data_real, data_imag = forward_dft(
        spread_float.reshape(per_dev, outer_size // 2, inner_size), outer_size, inner_size
    )
    kernel_real, kernel_imag = forward_dft(
        kernel.reshape(per_dev, outer_size // 2, inner_size), outer_size, inner_size
    )
    product_real = data_real * kernel_real - data_imag * kernel_imag
    product_imag = data_real * kernel_imag + data_imag * kernel_real
    long_part = inverse_dft(product_real, product_imag, outer_size, inner_size).reshape(
        per_dev, length
    )
    channel_out = (spread_float * long_part).astype(jnp.bfloat16)
    returned = lax.all_to_all(channel_out[None], "seq", split_axis=2, concat_axis=0, tiled=True)
    hyena_out = returned.reshape(width_dev, tok_count).T
    head_count = width_dev // HEAD
    hyena_float = hyena_out.astype(jnp.float32)
    square_sums = jnp.sum(hyena_float * hyena_float, axis=1)
    total_sums = lax.psum(square_sums, "ch")
    inverse_scale = lax.rsqrt(total_sums / C + 1e-05)
    normed = hyena_float * inverse_scale[:, None]
    values = normed.astype(jnp.bfloat16).reshape(tok_count, head_count, HEAD)
    queries = (
        (normed * query_gain[None, :]).astype(jnp.bfloat16).reshape(tok_count, head_count, HEAD)
    )
    key_rows = (
        (normed * key_gain[None, :]).astype(jnp.bfloat16).reshape(tok_count, head_count, HEAD)
    )
    group_size = 2
    level_count = group_size.bit_length() - 1
    seq_bits = seq_count.bit_length() - 1
    base_bit = seq_bits - level_count
    stride = seq_count // group_size
    stacked = queries[None]
    level = 0
    bit_number = base_bit + level
    partner_rows = swapped(stacked, "seq", bit_number)
    upper_side = seq_index >> bit_number & 1
    stacked = jnp.where(
        upper_side == 1,
        jnp.concatenate([partner_rows, stacked], axis=0),
        jnp.concatenate([stacked, partner_rows], axis=0),
    )
    query_rows = stacked.reshape(group_size * tok_count, head_count, HEAD)
    group_first = seq_index % stride
    block_numbers = group_first + stride * jnp.arange(group_size, dtype=jnp.int32)
    query_index = (
        block_numbers[:, None] * tok_count + jnp.arange(tok_count, dtype=jnp.int32)[None, :]
    ).reshape(group_size * tok_count)
    score_scale = HEAD ** (-0.5)
    partial_state = (
        jnp.full((head_count, group_size * tok_count), -1e30, jnp.float32),
        jnp.zeros((head_count, group_size * tok_count), jnp.float32),
        jnp.zeros((head_count, group_size * tok_count, HEAD), jnp.float32),
    )

    def cycle_step(turn_number, carried):
        key_block, value_block, running = carried
        key_block, value_block = from_behind((key_block, value_block), "seq", -1)
        source_block = jnp.remainder(seq_index + turn_number, seq_count)
        running = attend_block(
            query_rows,
            query_index,
            key_block,
            value_block,
            source_block * tok_count,
            running,
            score_scale,
        )
        return (key_block, value_block, running)

    carried = lax.fori_loop(1, stride + 1, cycle_step, (key_rows, values, partial_state))
    row_peak, row_total, blended = carried[2]
    row_peak = row_peak.reshape(head_count, group_size, tok_count)
    row_total = row_total.reshape(head_count, group_size, tok_count)
    blended = blended.reshape(head_count, group_size, tok_count, HEAD)
    for level in reversed(range(level_count)):
        bit_number = base_bit + level
        half_size = row_peak.shape[1] // 2
        upper_side = seq_index >> bit_number & 1
        keep_peak, send_peak = split_halves(row_peak, half_size, upper_side)
        keep_total, send_total = split_halves(row_total, half_size, upper_side)
        keep_blend, send_blend = split_halves(blended, half_size, upper_side)
        got_peak, got_total, got_blend = swapped(
            (send_peak, send_total, send_blend), "seq", bit_number
        )
        row_peak, row_total, blended = merge_partials(
            (keep_peak, keep_total, keep_blend), (got_peak, got_total, got_blend)
        )
    normalized = blended[:, 0] / row_total[:, 0][:, :, None]
    attended = normalized.transpose(1, 0, 2).reshape(tok_count, width_dev).astype(jnp.bfloat16)
    return (hyena_out, attended)


def transform_tables(block):
    size = 2 * block
    step = 2.0 * np.pi / size
    freq = (np.arange(block) + 0.5)[:, None]
    angle = freq * np.arange(size)[None, :] * step
    forward = np.concatenate([np.cos(angle), -np.sin(angle)], axis=0)
    angle = (np.arange(block)[:, None] + block) * freq.T * step
    backward = np.concatenate([np.cos(angle), -np.sin(angle)], axis=1) * (2.0 / size)

    def parts(table):
        kept = []
        for _ in range(3):
            kept.append(table.astype(np.float32).astype(ml_dtypes.bfloat16))
            table = table - kept[-1].astype(np.float64)
        return np.concatenate(kept, axis=0)

    return parts(forward), parts(backward)


def split_pair(value):
    upper = value.astype(jnp.bfloat16)
    return upper, (value - upper.astype(jnp.float32)).astype(jnp.bfloat16)


def split_three(value):
    upper = value.astype(jnp.bfloat16)
    rest = value - upper.astype(jnp.float32)
    middle = rest.astype(jnp.bfloat16)
    return upper, middle, (rest - middle.astype(jnp.float32)).astype(jnp.bfloat16)


def minus_expm1(value):
    term = value
    series = value
    for order in range(2, 11):
        term = term * value * (-1.0 / order)
        series = series + term
    return jnp.where(value < 0.5, series, 1.0 - jnp.exp(-value))


def dot32(left, right):
    return jnp.dot(left, right, preferred_element_type=jnp.float32)


def own_lanes(width):
    return pl.ds(pl.multiple_of(lax.axis_index("seq") * width, width), width)


def filter_kernel(
    residue, rate, medium, forward, medium_out, long_out, residues, rates, taps, table, modes, sems
):
    block, width = taps.shape
    size = 2 * block
    copies = [
        pltpu.make_async_copy(rate.at[:, own_lanes(width)], rates, sems.at[0]),
        pltpu.make_async_copy(residue.at[:, own_lanes(width)], residues, sems.at[1]),
        pltpu.make_async_copy(medium.at[:, own_lanes(width)], taps, sems.at[2]),
        pltpu.make_async_copy(forward.at[:, 0:block], table, sems.at[3]),
    ]
    for copy in copies:
        copy.start()
    for copy in copies[:2]:
        copy.wait()
    mode_total = rate.shape[0]
    block_total = long_out.shape[1] // width
    decays = rates[...]
    weights = residues[...] * jnp.sqrt(minus_expm1(2.0 * decays)) / math.sqrt(mode_total)
    for part in range(block_total):
        modes[part] = weights * jnp.exp(-decays * float(part * block))
    place = lax.broadcasted_iota(jnp.int32, (block, width), 0).astype(jnp.float32)
    rows = 32
    for first in range(0, block, rows):
        sums = [jnp.zeros((rows, width), jnp.float32) for _ in range(block_total)]
        for mode in range(mode_total):
            shape = jnp.exp(-decays[mode : mode + 1, :] * place[first : first + rows])
            for part in range(block_total):
                sums[part] = sums[part] + modes[part, mode : mode + 1, :] * shape
        for part in range(block_total):
            long_out[first : first + rows, part * width : (part + 1) * width] = sums[part]
    for copy in copies[2:]:
        copy.wait()

    def transformed(signal):
        up, middle, low = split_three(signal)
        return (
            dot32(table[0:size, :], up)
            + dot32(table[size : 2 * size, :], up)
            + dot32(table[0:size, :], middle)
            + dot32(table[2 * size : 3 * size, :], up)
            + dot32(table[size : 2 * size, :], middle)
            + dot32(table[0:size, :], low)
        )

    medium_out[...] = transformed(taps[...])
    long_out[...] = transformed(long_out[0:block, :])


def conv_kernel(
    *refs, piece_count
):
    pieces = refs[:piece_count]
    (embedding, short, medium_resp, long_resp, forward, backward) = refs[piece_count : piece_count + 6]
    (hyena, sums) = refs[piece_count + 6 : piece_count + 8]
    ids, ordered, padded, gated, windows, spectrum, prod_up, prod_mid, prod_low = refs[piece_count + 8 :]
    width = gated.shape[1]
    block = width
    size = 2 * block
    length = hyena.shape[0]
    count = length // block
    me = lax.axis_index("seq")
    for i, piece in enumerate(pieces):
        ids[2 * i : 2 * i + 2, :] = piece[...]
    for b in range(count):
        ordered[b : b + 1, :] = ids[pl.ds(lax.bitwise_xor(me, b), 1), :]
    across = jnp.transpose(ordered[...].astype(jnp.float32), (1, 0)).astype(jnp.int32)
    padded[0:8, :] = jnp.zeros((8, width), jnp.float32)
    windows[0:block, 0:width] = jnp.zeros((block, width), jnp.bfloat16)
    table = embedding[:, own_lanes(width)]
    short_taps = short[:, own_lanes(width)]
    vocab = table.shape[0]
    entries = lax.broadcasted_iota(jnp.int32, (block, vocab), 1)
    for b in range(count):
        chosen = jnp.where(across[:, b : b + 1] == entries, 1.0, 0.0).astype(jnp.bfloat16)
        padded[8 + b * block : 8 + (b + 1) * block, :] = dot32(chosen, table)

    def enter(b, signal):
        windows[block:size, b * width : (b + 1) * width] = signal
        if b + 1 < count:
            windows[0:block, (b + 1) * width : (b + 2) * width] = signal

    tap_count = short_taps.shape[0]
    for b in range(count):
        running = jnp.zeros((block, width), jnp.float32)
        for j in range(tap_count):
            running = running + short_taps[j : j + 1, :] * padded[8 + b * block - j : 8 + (b + 1) * block - j, :]
        signal = (padded[8 + b * block : 8 + (b + 1) * block, :] * running).astype(jnp.bfloat16)
        gated[b * block : (b + 1) * block, :] = signal
        enter(b, signal)

    def analyse():
        signal = windows[...]
        spectrum[...] = (
            dot32(forward[0:size, :], signal)
            + dot32(forward[size : 2 * size, :], signal)
            + dot32(forward[2 * size : 3 * size, :], signal)
        )

    def enter_product(real, imag, rows, lanes):
        for offset, part in ((0, real), (block, imag)):
            for kept, piece in zip((prod_up, prod_mid, prod_low), split_three(part)):
                kept[pl.ds(offset + rows[0], rows[1]), lanes] = piece

    def synthesise():
        up, middle = prod_up[...], prod_mid[...]
        return (
            dot32(backward[0:block, :], up)
            + dot32(backward[block : 2 * block, :], up)
            + dot32(backward[0:block, :], middle)
            + dot32(backward[2 * block : 3 * block, :], up)
            + dot32(backward[block : 2 * block, :], middle)
            + dot32(backward[0:block, :], prod_low[...])
        )

    analyse()
    rows = 16
    for first in range(0, block, rows):
        filt_real = medium_resp[first : first + rows, :]
        filt_imag = medium_resp[block + first : block + first + rows, :]
        for b in range(count):
            lanes = pl.ds(b * width, width)
            real = spectrum[first : first + rows, lanes]
            imag = spectrum[block + first : block + first + rows, lanes]
            enter_product(
                real * filt_real - imag * filt_imag, real * filt_imag + imag * filt_real, (first, rows), lanes
            )
    out = synthesise()
    for b in range(count):
        past = gated[b * block : (b + 1) * block, :].astype(jnp.float32)
        signal = (past * out[:, b * width : (b + 1) * width]).astype(jnp.bfloat16)
        gated[b * block : (b + 1) * block, :] = signal
        enter(b, signal)
    analyse()

    def long_rows(step, _):
        first = pl.multiple_of(step * rows, rows)
        for b in range(count):
            total_real = jnp.zeros((rows, width), jnp.float32)
            total_imag = jnp.zeros((rows, width), jnp.float32)
            for part in range(b + 1):
                lanes = pl.ds((b - part) * width, width)
                resp = pl.ds(part * width, width)
                real = spectrum[pl.ds(first, rows), lanes]
                imag = spectrum[pl.ds(block + first, rows), lanes]
                filt_real = long_resp[pl.ds(first, rows), resp]
                filt_imag = long_resp[pl.ds(block + first, rows), resp]
                total_real = total_real + (real * filt_real - imag * filt_imag)
                total_imag = total_imag + (real * filt_imag + imag * filt_real)
            enter_product(total_real, total_imag, (first, rows), pl.ds(b * width, width))
        return 0

    lax.fori_loop(0, block // rows, long_rows, 0)
    out = synthesise()
    ones = jnp.ones((8, width), jnp.bfloat16)
    spot = lax.broadcasted_iota(jnp.int32, (count, block), 0)
    total = jnp.zeros((count, block), jnp.float32)
    contract = (((1,), (1,)), ((), ()))
    for b in range(count):
        past = gated[b * block : (b + 1) * block, :].astype(jnp.float32)
        result = (past * out[:, b * width : (b + 1) * width]).astype(jnp.bfloat16)
        hyena[b * block : (b + 1) * block, :] = result
        wide = result.astype(jnp.float32)
        up, low = split_pair(wide * wide)
        row = lax.dot_general(ones, up, contract, preferred_element_type=jnp.float32) + lax.dot_general(
            ones, low, contract, preferred_element_type=jnp.float32
        )
        total = jnp.where(spot == b, row[0:1, :], total)
    sums[...] = total


def attend_kernel(own, other, sums, query_gain, key_gain, out, queries, keys, values, *, channel_count):
    length, width = own.shape
    count = sums.shape[1]
    block = length // count
    me = lax.axis_index("seq")
    core = lax.rem(me, 2)
    chip = me // 2
    total = jnp.sum(sums[...], axis=0)
    inverse = lax.rsqrt(total / channel_count + 1e-05)
    inverse = jnp.transpose(inverse, (1, 0))
    contract = (((1,), (1,)), ((), ()))
    for side, signal in ((0, own), (1, other)):
        head = lax.bitwise_xor(me, side)
        lanes = pl.ds(pl.multiple_of(head * width, width), width)
        gain_q = query_gain[0:1, lanes]
        gain_k = key_gain[0:1, lanes]
        for b in range(count):
            spans = slice(b * block, (b + 1) * block)
            normed = signal[spans, :].astype(jnp.float32) * inverse[:, b : b + 1]
            values[side, spans, :] = normed.astype(jnp.bfloat16)
            keys[side, spans, :] = (normed * gain_k).astype(jnp.bfloat16)
            queries[side, spans, :] = (normed * gain_q).astype(jnp.bfloat16)
    row_index = lax.broadcasted_iota(jnp.int32, (block, 2 * block), 0) + core * block
    column_index = lax.broadcasted_iota(jnp.int32, (block, 2 * block), 1)
    allowed = column_index <= row_index
    for i in range(count // 2):
        reach = (i + 1) * 2 * block
        start = pl.multiple_of((2 * i + core) * block, block)
        place = lax.bitwise_xor(chip, i)
        for side, signal in ((0, own), (1, other)):
            rows = queries[side, pl.ds(start, block), :]
            scores = lax.dot_general(
                rows, keys[side, 0:reach, :], contract, preferred_element_type=jnp.float32
            ) * (width**-0.5)
            last = jnp.where(allowed, scores[:, reach - 2 * block :], -1e30)
            scores = jnp.concatenate([scores[:, : reach - 2 * block], last], axis=1) if i else last
            peak = jnp.max(scores, axis=1, keepdims=True)
            weights = jnp.exp(scores - peak)
            row_total = jnp.sum(weights, axis=1, keepdims=True)
            blended = dot32(weights.astype(jnp.bfloat16), values[side, 0:reach, :])
            half = lax.bitwise_xor(core, side)
            lanes = pl.ds(pl.multiple_of(half * width, width), width)
            out[place, :, lanes] = (blended / row_total).astype(jnp.bfloat16)
            lanes = pl.ds(pl.multiple_of((2 + half) * width, width), width)
            out[place, :, lanes] = signal[pl.ds(start, block), :]


def place_kernel(*refs):
    blocks, (hyena, attended) = refs[:-2], refs[-2:]
    span = blocks[0].shape[1] // 2
    chip = lax.axis_index("seq") // 2
    for i, block in enumerate(blocks):
        lanes = pl.ds(pl.multiple_of(lax.bitwise_xor(chip, i) * span, span), span)
        attended[:, lanes] = block[:, 0:span]
        hyena[:, lanes] = block[:, span : 2 * span]


def by_head(
    token_ids, embedding, short_filter, medium_filter, long_residue, long_rate, query_gain, key_gain
):
    seq_count = lax.axis_size("seq")
    ch_count = lax.axis_size("ch")
    block = token_ids.shape[0]
    width_dev = embedding.shape[1]
    length = block * seq_count
    width = HEAD
    f32, bf16 = jnp.float32, jnp.bfloat16
    forward, backward = transform_tables(block)
    whole = pl.BlockSpec(memory_space=pltpu.VMEM)
    params = pltpu.CompilerParams(vmem_limit_bytes=24 * 1024 * 1024)

    def exchange(value, apart):
        return lax.ppermute(value, "seq", [(i, i ^ apart) for i in range(seq_count)])

    chip_ids = jnp.stack([token_ids, exchange(token_ids, 1)])
    pieces = [chip_ids] + [exchange(chip_ids, apart) for apart in range(2, seq_count, 2)]

    mode_total = long_rate.shape[0]
    in_hbm = pl.BlockSpec(memory_space=pltpu.HBM)

    def fetched(value):
        return pltpu.with_memory_space_constraint(value, pltpu.HBM)

    medium_resp, long_resp = pl.pallas_call(
        filter_kernel,
        out_shape=[
            jax.ShapeDtypeStruct((2 * block, width), f32),
            jax.ShapeDtypeStruct((2 * block, length), f32),
        ],
        in_specs=[in_hbm] * 4,
        out_specs=[whole] * 2,
        scratch_shapes=[
            pltpu.VMEM((mode_total, width), f32),
            pltpu.VMEM((mode_total, width), f32),
            pltpu.VMEM((block, width), f32),
            pltpu.VMEM((forward.shape[0], block), bf16),
            pltpu.VMEM((seq_count, mode_total, width), f32),
            pltpu.SemaphoreType.DMA((4,)),
        ],
        compiler_params=params,
        cost_estimate=pl.CostEstimate(flops=8 * 10**8, bytes_accessed=2 * 10**6, transcendentals=3 * 10**5),
        name="filter_responses",
    )(*[fetched(value) for value in (long_residue, long_rate, medium_filter, jnp.asarray(forward))])

    hyena, square_sums = pl.pallas_call(
        functools.partial(conv_kernel, piece_count=len(pieces)),
        out_shape=[
            jax.ShapeDtypeStruct((length, width), bf16),
            jax.ShapeDtypeStruct((seq_count, block), f32),
        ],
        in_specs=[whole] * (len(pieces) + 6),
        out_specs=[whole, whole],
        scratch_shapes=[
            pltpu.VMEM((seq_count, block), jnp.int32),
            pltpu.VMEM((seq_count, block), jnp.int32),
            pltpu.VMEM((8 + length, width), f32),
            pltpu.VMEM((length, width), bf16),
            pltpu.VMEM((2 * block, length), bf16),
            pltpu.VMEM((2 * block, length), f32),
            pltpu.VMEM((2 * block, length), bf16),
            pltpu.VMEM((2 * block, length), bf16),
            pltpu.VMEM((2 * block, length), bf16),
        ],
        compiler_params=params,
        cost_estimate=pl.CostEstimate(flops=2 * 10**9, bytes_accessed=2 * 10**6, transcendentals=0),
        name="gated_convolutions",
    )(*pieces, embedding, short_filter, medium_resp, long_resp, forward, backward)

    other = exchange(hyena, 1)
    devices = seq_count * ch_count
    all_sums = lax.all_to_all(
        jnp.broadcast_to(square_sums[None], (devices, seq_count, block)), ("seq", "ch"), 0, 0, tiled=True
    )
    outgoing = pl.pallas_call(
        functools.partial(attend_kernel, channel_count=width_dev * ch_count),
        out_shape=jax.ShapeDtypeStruct((seq_count // 2, block, 4 * width), bf16),
        in_specs=[whole] * 5,
        out_specs=whole,
        scratch_shapes=[pltpu.VMEM((2, length, width), bf16)] * 3,
        compiler_params=params,
        cost_estimate=pl.CostEstimate(flops=5 * 10**9, bytes_accessed=10**6, transcendentals=10**6),
        name="attention",
    )(hyena, other, all_sums, query_gain.reshape(1, width_dev), key_gain.reshape(1, width_dev))
    blocks = [outgoing[0]] + [exchange(outgoing[i], 2 * i) for i in range(1, seq_count // 2)]
    return pl.pallas_call(
        place_kernel,
        out_shape=[jax.ShapeDtypeStruct((block, width_dev), bf16)] * 2,
        in_specs=[whole] * len(blocks),
        out_specs=[whole, whole],
        compiler_params=params,
        name="placed_blocks",
    )(*blocks)


def on_device(*operands):
    seq_count = lax.axis_size("seq")
    token_ids, embedding, _, medium_filter = operands[:4]
    block = token_ids.shape[0]
    fits = (
        embedding.shape[1] == seq_count * HEAD
        and block == HEAD
        and medium_filter.shape[0] == block
        and seq_count % 8 == 0
        and seq_count & (seq_count - 1) == 0
    )
    return by_head(*operands) if fits else by_position(*operands)


def solution(mesh):
    in_specs = (
        P("seq"),
        P(None, "ch"),
        P(None, "ch"),
        P(None, "ch"),
        P(None, "ch"),
        P(None, "ch"),
        P("ch"),
        P("ch"),
    )
    out_specs = (P("seq", "ch"), P("seq", "ch"))
    return jax.shard_map(
        on_device, mesh=mesh, in_specs=in_specs, out_specs=out_specs, check_vma=False
    )
```

```python
import functools
import math

import jax
import jax.numpy as jnp
import ml_dtypes
import numpy as np
from jax import lax
from jax.experimental import pallas as pl
from jax.experimental.pallas import tpu as pltpu
from jax.sharding import PartitionSpec as P

C = 4096
HEAD = 128


def shifted(value, axis, steps):
    count = lax.axis_size(axis)
    leading, last = (max(0, -steps), min(count, count - steps))
    return lax.ppermute(value, axis, [(source, source + steps) for source in range(leading, last)])


def swapped(shard, axis, apart):
    return lax.ppermute(shard, axis, [(i, i ^ 1 << apart) for i in range(lax.axis_size(axis))])


def from_behind(shard, axis, by):
    size = lax.axis_size(axis)
    return lax.ppermute(shard, axis, [(i, (i + by) % size) for i in range(size)])


def rounded(value):
    return lax.optimization_barrier(value.astype(jnp.bfloat16))


def depthwise_conv(widened, tap_weights, row_count):
    tap_count = tap_weights.shape[0]

    def add_tap(tap_index, running):
        window = lax.dynamic_slice_in_dim(widened, tap_count - 1 - tap_index, row_count, 0)
        return running + tap_weights[tap_index] * window.astype(jnp.float32)

    return lax.fori_loop(
        0, tap_count, add_tap, jnp.zeros((row_count, widened.shape[1]), jnp.float32)
    )


def long_kernel_rows(residue_mine, rate_mine, length):
    positions = jnp.arange(length, dtype=jnp.int32).astype(jnp.float32)
    mode_total = rate_mine.shape[0]

    def add_mode(mode_index, running):
        decay_rate = rate_mine[mode_index]
        mode_weight = (
            residue_mine[mode_index]
            * jnp.sqrt(-jnp.expm1(-2.0 * decay_rate))
            / math.sqrt(mode_total)
        )
        return running + mode_weight[:, None] * jnp.exp(-decay_rate[:, None] * positions[None, :])

    return lax.fori_loop(
        0, mode_total, add_mode, jnp.zeros((rate_mine.shape[1], length), jnp.float32)
    )


def dft_tables(row_size, column_size, period_size):
    row_index = lax.broadcasted_iota(jnp.int32, (row_size, column_size), 0)
    column_index = lax.broadcasted_iota(jnp.int32, (row_size, column_size), 1)
    angles = (row_index * column_index % period_size).astype(jnp.float32) * (
        2.0 * math.pi / period_size
    )
    return (jnp.cos(angles), jnp.sin(angles))


def forward_dft(signal, outer_size, inner_size):
    highest = lax.Precision.HIGHEST
    cos_outer, sin_outer = dft_tables(outer_size // 2, outer_size, outer_size)
    twiddle_cos, twiddle_sin = dft_tables(outer_size, inner_size, outer_size * inner_size)
    cos_inner, sin_inner = dft_tables(inner_size, inner_size, inner_size)
    step_real = jnp.einsum("pab,ak->pkb", signal, cos_outer, precision=highest)
    step_imag = -jnp.einsum("pab,ak->pkb", signal, sin_outer, precision=highest)
    turned_real = step_real * twiddle_cos + step_imag * twiddle_sin
    turned_imag = step_imag * twiddle_cos - step_real * twiddle_sin
    spec_real = jnp.einsum("pkb,bm->pkm", turned_real, cos_inner, precision=highest) + jnp.einsum(
        "pkb,bm->pkm", turned_imag, sin_inner, precision=highest
    )
    spec_imag = jnp.einsum("pkb,bm->pkm", turned_imag, cos_inner, precision=highest) - jnp.einsum(
        "pkb,bm->pkm", turned_real, sin_inner, precision=highest
    )
    return (spec_real, spec_imag)


def inverse_dft(spec_real, spec_imag, outer_size, inner_size):
    highest = lax.Precision.HIGHEST
    cos_outer, sin_outer = dft_tables(outer_size // 2, outer_size, outer_size)
    twiddle_cos, twiddle_sin = dft_tables(outer_size, inner_size, outer_size * inner_size)
    cos_inner, sin_inner = dft_tables(inner_size, inner_size, inner_size)
    back_real = jnp.einsum("pkm,mb->pkb", spec_real, cos_inner, precision=highest) - jnp.einsum(
        "pkm,mb->pkb", spec_imag, sin_inner, precision=highest
    )
    back_imag = jnp.einsum("pkm,mb->pkb", spec_real, sin_inner, precision=highest) + jnp.einsum(
        "pkm,mb->pkb", spec_imag, cos_inner, precision=highest
    )
    turned_real = back_real * twiddle_cos - back_imag * twiddle_sin
    turned_imag = back_real * twiddle_sin + back_imag * twiddle_cos
    signal = jnp.einsum("pkb,ak->pab", turned_real, cos_outer, precision=highest) - jnp.einsum(
        "pkb,ak->pab", turned_imag, sin_outer, precision=highest
    )
    return signal / (outer_size * inner_size)


def attend_block(query_rows, query_index, key_block, value_block, key_start, running, score_scale):
    row_peak, row_total, blended = running
    scores = (
        jnp.einsum("qhd,khd->hqk", query_rows, key_block, preferred_element_type=jnp.float32)
        * score_scale
    )
    key_index = key_start + jnp.arange(key_block.shape[0], dtype=jnp.int32)
    scores = jnp.where(key_index[None, None, :] <= query_index[None, :, None], scores, -1e30)
    new_peak = jnp.maximum(row_peak, jnp.max(scores, axis=2))
    weights = jnp.exp(scores - new_peak[:, :, None])
    rescale = jnp.exp(row_peak - new_peak)
    row_total = row_total * rescale + jnp.sum(weights, axis=2)
    blended = blended * rescale[:, :, None] + jnp.einsum(
        "hqk,khd->hqd",
        weights.astype(jnp.bfloat16),
        value_block,
        preferred_element_type=jnp.float32,
    )
    return (new_peak, row_total, blended)


def merge_partials(first_part, second_part):
    peak_one, total_one, blend_one = first_part
    peak_two, total_two, blend_two = second_part
    new_peak = jnp.maximum(peak_one, peak_two)
    scale_one = jnp.exp(peak_one - new_peak)
    scale_two = jnp.exp(peak_two - new_peak)
    new_total = total_one * scale_one + total_two * scale_two
    new_blend = blend_one * scale_one[..., None] + blend_two * scale_two[..., None]
    return (new_peak, new_total, new_blend)


def split_halves(stacked_part, half_size, upper_side):
    lower_half = stacked_part[:, :half_size]
    upper_half = stacked_part[:, half_size:]
    keep_half = jnp.where(upper_side == 1, upper_half, lower_half)
    send_half = jnp.where(upper_side == 1, lower_half, upper_half)
    return (keep_half, send_half)


def by_position(
    token_ids, embedding, short_filter, medium_filter, long_residue, long_rate, query_gain, key_gain
):
    tok_count = token_ids.shape[0]
    vocab_size = embedding.shape[0]
    width_dev = embedding.shape[1]
    seq_count = lax.axis_size("seq")
    seq_index = lax.axis_index("seq")
    one_hot = (
        token_ids[:, None] == lax.broadcasted_iota(jnp.int32, (tok_count, vocab_size), 1)
    ).astype(jnp.bfloat16)
    embedded = jnp.dot(one_hot, embedding, preferred_element_type=jnp.float32).astype(jnp.bfloat16)
    short_taps = short_filter.shape[0]
    rim_rows = shifted(embedded[tok_count - (short_taps - 1) :], "seq", 1)
    widened = jnp.concatenate([rim_rows, embedded], axis=0)
    short_part = depthwise_conv(widened, short_filter, tok_count)
    short_gated = rounded(embedded.astype(jnp.float32) * short_part)
    medium_taps = medium_filter.shape[0]
    upper_rows = shifted(short_gated[tok_count - (medium_taps - 1) :], "seq", 1)
    widened_two = jnp.concatenate([upper_rows, short_gated], axis=0)
    medium_part = depthwise_conv(widened_two, medium_filter, tok_count)
    medium_gated = rounded(short_gated.astype(jnp.float32) * medium_part)
    per_dev = width_dev // seq_count
    length = tok_count * seq_count
    grouped = medium_gated.T.reshape(seq_count, per_dev, tok_count)
    spread = lax.all_to_all(grouped, "seq", split_axis=0, concat_axis=2, tiled=True).reshape(
        per_dev, length
    )
    rate_mine = lax.dynamic_slice_in_dim(long_rate, seq_index * per_dev, per_dev, 1)
    residue_mine = lax.dynamic_slice_in_dim(long_residue, seq_index * per_dev, per_dev, 1)
    kernel = long_kernel_rows(residue_mine, rate_mine, length)
    outer_size = 128
    inner_size = 2 * length // outer_size
    spread_float = spread.astype(jnp.float32)
    data_real, data_imag = forward_dft(
        spread_float.reshape(per_dev, outer_size // 2, inner_size), outer_size, inner_size
    )
    kernel_real, kernel_imag = forward_dft(
        kernel.reshape(per_dev, outer_size // 2, inner_size), outer_size, inner_size
    )
    product_real = data_real * kernel_real - data_imag * kernel_imag
    product_imag = data_real * kernel_imag + data_imag * kernel_real
    long_part = inverse_dft(product_real, product_imag, outer_size, inner_size).reshape(
        per_dev, length
    )
    channel_out = (spread_float * long_part).astype(jnp.bfloat16)
    returned = lax.all_to_all(channel_out[None], "seq", split_axis=2, concat_axis=0, tiled=True)
    hyena_out = returned.reshape(width_dev, tok_count).T
    head_count = width_dev // HEAD
    hyena_float = hyena_out.astype(jnp.float32)
    square_sums = jnp.sum(hyena_float * hyena_float, axis=1)
    total_sums = lax.psum(square_sums, "ch")
    inverse_scale = lax.rsqrt(total_sums / C + 1e-05)
    normed = hyena_float * inverse_scale[:, None]
    values = normed.astype(jnp.bfloat16).reshape(tok_count, head_count, HEAD)
    queries = (
        (normed * query_gain[None, :]).astype(jnp.bfloat16).reshape(tok_count, head_count, HEAD)
    )
    key_rows = (
        (normed * key_gain[None, :]).astype(jnp.bfloat16).reshape(tok_count, head_count, HEAD)
    )
    group_size = 2
    level_count = group_size.bit_length() - 1
    seq_bits = seq_count.bit_length() - 1
    base_bit = seq_bits - level_count
    stride = seq_count // group_size
    stacked = queries[None]
    level = 0
    bit_number = base_bit + level
    partner_rows = swapped(stacked, "seq", bit_number)
    upper_side = seq_index >> bit_number & 1
    stacked = jnp.where(
        upper_side == 1,
        jnp.concatenate([partner_rows, stacked], axis=0),
        jnp.concatenate([stacked, partner_rows], axis=0),
    )
    query_rows = stacked.reshape(group_size * tok_count, head_count, HEAD)
    group_first = seq_index % stride
    block_numbers = group_first + stride * jnp.arange(group_size, dtype=jnp.int32)
    query_index = (
        block_numbers[:, None] * tok_count + jnp.arange(tok_count, dtype=jnp.int32)[None, :]
    ).reshape(group_size * tok_count)
    score_scale = HEAD ** (-0.5)
    partial_state = (
        jnp.full((head_count, group_size * tok_count), -1e30, jnp.float32),
        jnp.zeros((head_count, group_size * tok_count), jnp.float32),
        jnp.zeros((head_count, group_size * tok_count, HEAD), jnp.float32),
    )

    def cycle_step(turn_number, carried):
        key_block, value_block, running = carried
        key_block, value_block = from_behind((key_block, value_block), "seq", -1)
        source_block = jnp.remainder(seq_index + turn_number, seq_count)
        running = attend_block(
            query_rows,
            query_index,
            key_block,
            value_block,
            source_block * tok_count,
            running,
            score_scale,
        )
        return (key_block, value_block, running)

    carried = lax.fori_loop(1, stride + 1, cycle_step, (key_rows, values, partial_state))
    row_peak, row_total, blended = carried[2]
    row_peak = row_peak.reshape(head_count, group_size, tok_count)
    row_total = row_total.reshape(head_count, group_size, tok_count)
    blended = blended.reshape(head_count, group_size, tok_count, HEAD)
    for level in reversed(range(level_count)):
        bit_number = base_bit + level
        half_size = row_peak.shape[1] // 2
        upper_side = seq_index >> bit_number & 1
        keep_peak, send_peak = split_halves(row_peak, half_size, upper_side)
        keep_total, send_total = split_halves(row_total, half_size, upper_side)
        keep_blend, send_blend = split_halves(blended, half_size, upper_side)
        got_peak, got_total, got_blend = swapped(
            (send_peak, send_total, send_blend), "seq", bit_number
        )
        row_peak, row_total, blended = merge_partials(
            (keep_peak, keep_total, keep_blend), (got_peak, got_total, got_blend)
        )
    normalized = blended[:, 0] / row_total[:, 0][:, :, None]
    attended = normalized.transpose(1, 0, 2).reshape(tok_count, width_dev).astype(jnp.bfloat16)
    return (hyena_out, attended)


def transform_tables(block):
    size = 2 * block
    step = 2.0 * np.pi / size
    freq = (np.arange(block) + 0.5)[:, None]
    angle = freq * np.arange(size)[None, :] * step
    forward = np.concatenate([np.cos(angle), -np.sin(angle)], axis=0)
    angle = (np.arange(block)[:, None] + block) * freq.T * step
    backward = np.concatenate([np.cos(angle), -np.sin(angle)], axis=1) * (2.0 / size)

    def parts(table):
        kept = []
        for _ in range(3):
            kept.append(table.astype(np.float32).astype(ml_dtypes.bfloat16))
            table = table - kept[-1].astype(np.float64)
        return np.concatenate(kept, axis=0)

    forward, backward = parts(forward), parts(backward)
    first, second, third = np.split(forward[:, :block], 3)
    taps = np.concatenate([np.concatenate([first, second], axis=1), np.concatenate([first, third], axis=1)], axis=0)
    return forward, backward, taps


def split_pair(value):
    upper = value.astype(jnp.bfloat16)
    return upper, (value - upper.astype(jnp.float32)).astype(jnp.bfloat16)


def split_three(value):
    upper = value.astype(jnp.bfloat16)
    rest = value - upper.astype(jnp.float32)
    middle = rest.astype(jnp.bfloat16)
    return upper, middle, (rest - middle.astype(jnp.float32)).astype(jnp.bfloat16)


def minus_expm1(value):
    term = value
    series = value
    for order in range(2, 11):
        term = term * value * (-1.0 / order)
        series = series + term
    return jnp.where(value < 0.5, series, 1.0 - jnp.exp(-value))


def dot32(left, right):
    return jnp.dot(left, right, preferred_element_type=jnp.float32)


def own_lanes(width):
    return pl.ds(pl.multiple_of(lax.axis_index("seq") * width, width), width)


def fetch_kernel(
    token_ids, residue, rate, medium, table, ids_out, medium_out, table_out, long_out, residues, rates, modes, sems
):
    block, width = medium_out.shape
    lanes = own_lanes(width)
    copies = [
        pltpu.make_async_copy(rate.at[:, lanes], rates, sems.at[0]),
        pltpu.make_async_copy(residue.at[:, lanes], residues, sems.at[1]),
        pltpu.make_async_copy(token_ids, ids_out, sems.at[2]),
        pltpu.make_async_copy(medium.at[:, lanes], medium_out, sems.at[3]),
        pltpu.make_async_copy(table, table_out, sems.at[4]),
    ]
    for copy in copies:
        copy.start()
    for copy in copies[:2]:
        copy.wait()
    mode_total = rate.shape[0]
    block_total = long_out.shape[1] // width
    decays = rates[...]
    weights = residues[...] * jnp.sqrt(minus_expm1(2.0 * decays)) / math.sqrt(mode_total)
    for part in range(block_total):
        modes[part] = weights * jnp.exp(-decays * float(part * block))
    place = lax.broadcasted_iota(jnp.int32, (block, width), 0).astype(jnp.float32)
    rows = 32
    for first in range(0, block, rows):
        sums = [jnp.zeros((rows, width), jnp.float32) for _ in range(block_total)]
        for mode in range(mode_total):
            shape = jnp.exp(-decays[mode : mode + 1, :] * place[first : first + rows])
            for part in range(block_total):
                sums[part] = sums[part] + modes[part, mode : mode + 1, :] * shape
        for part in range(block_total):
            long_out[first : first + rows, part * width : (part + 1) * width] = sums[part]
    for copy in copies[2:]:
        copy.wait()


def response_kernel(medium, long, table, medium_out, long_out):
    size = 2 * medium.shape[0]

    def transformed(signal):
        up, middle, low = split_three(signal)
        return (
            dot32(table[0:size, :], jnp.concatenate([up, up], axis=0))
            + dot32(table[0:size, :], jnp.concatenate([middle, middle], axis=0))
            + dot32(table[size : 2 * size, :], jnp.concatenate([low, up], axis=0))
        )

    medium_out[...] = transformed(medium[...])
    long_out[...] = transformed(long[...])


def conv_kernel(
    *refs, piece_count
):
    pieces = refs[:piece_count]
    (embedding, short, medium_resp, long_resp, forward, backward) = refs[piece_count : piece_count + 6]
    (hyena, sums) = refs[piece_count + 6 : piece_count + 8]
    ids, ordered, padded, gated, windows, spectrum, prod_up, prod_mid, prod_low = refs[piece_count + 8 :]
    width = gated.shape[1]
    block = width
    size = 2 * block
    length = hyena.shape[0]
    count = length // block
    me = lax.axis_index("seq")
    for i, piece in enumerate(pieces):
        ids[2 * i : 2 * i + 2, :] = piece[...]
    for b in range(count):
        ordered[b : b + 1, :] = ids[pl.ds(lax.bitwise_xor(me, b), 1), :]
    across = jnp.transpose(ordered[...].astype(jnp.float32), (1, 0)).astype(jnp.int32)
    padded[0:8, :] = jnp.zeros((8, width), jnp.float32)
    windows[0:block, 0:width] = jnp.zeros((block, width), jnp.bfloat16)
    table = embedding[:, own_lanes(width)]
    short_taps = short[:, own_lanes(width)]
    vocab = table.shape[0]
    entries = lax.broadcasted_iota(jnp.int32, (block, vocab), 1)
    for b in range(count):
        chosen = jnp.where(across[:, b : b + 1] == entries, 1.0, 0.0).astype(jnp.bfloat16)
        padded[8 + b * block : 8 + (b + 1) * block, :] = dot32(chosen, table)

    def enter(b, signal):
        windows[block:size, b * width : (b + 1) * width] = signal
        if b + 1 < count:
            windows[0:block, (b + 1) * width : (b + 2) * width] = signal

    tap_count = short_taps.shape[0]
    for b in range(count):
        running = jnp.zeros((block, width), jnp.float32)
        for j in range(tap_count):
            running = running + short_taps[j : j + 1, :] * padded[8 + b * block - j : 8 + (b + 1) * block - j, :]
        signal = (padded[8 + b * block : 8 + (b + 1) * block, :] * running).astype(jnp.bfloat16)
        gated[b * block : (b + 1) * block, :] = signal
        enter(b, signal)

    def analyse():
        signal = windows[...]
        spectrum[...] = (
            dot32(forward[0:size, :], signal)
            + dot32(forward[size : 2 * size, :], signal)
            + dot32(forward[2 * size : 3 * size, :], signal)
        )

    def enter_product(real, imag, rows, lanes):
        for offset, part in ((0, real), (block, imag)):
            for kept, piece in zip((prod_up, prod_mid, prod_low), split_three(part)):
                kept[pl.ds(offset + rows[0], rows[1]), lanes] = piece

    def synthesise():
        up, middle = prod_up[...], prod_mid[...]
        return (
            dot32(backward[0:block, :], up)
            + dot32(backward[block : 2 * block, :], up)
            + dot32(backward[0:block, :], middle)
            + dot32(backward[2 * block : 3 * block, :], up)
            + dot32(backward[block : 2 * block, :], middle)
            + dot32(backward[0:block, :], prod_low[...])
        )

    analyse()
    rows = 16
    for first in range(0, block, rows):
        filt_real = medium_resp[first : first + rows, :]
        filt_imag = medium_resp[block + first : block + first + rows, :]
        for b in range(count):
            lanes = pl.ds(b * width, width)
            real = spectrum[first : first + rows, lanes]
            imag = spectrum[block + first : block + first + rows, lanes]
            enter_product(
                real * filt_real - imag * filt_imag, real * filt_imag + imag * filt_real, (first, rows), lanes
            )
    out = synthesise()
    for b in range(count):
        past = gated[b * block : (b + 1) * block, :].astype(jnp.float32)
        signal = (past * out[:, b * width : (b + 1) * width]).astype(jnp.bfloat16)
        gated[b * block : (b + 1) * block, :] = signal
        enter(b, signal)
    analyse()

    def long_rows(step, _):
        first = pl.multiple_of(step * rows, rows)
        for b in range(count):
            total_real = jnp.zeros((rows, width), jnp.float32)
            total_imag = jnp.zeros((rows, width), jnp.float32)
            for part in range(b + 1):
                lanes = pl.ds((b - part) * width, width)
                resp = pl.ds(part * width, width)
                real = spectrum[pl.ds(first, rows), lanes]
                imag = spectrum[pl.ds(block + first, rows), lanes]
                filt_real = long_resp[pl.ds(first, rows), resp]
                filt_imag = long_resp[pl.ds(block + first, rows), resp]
                total_real = total_real + (real * filt_real - imag * filt_imag)
                total_imag = total_imag + (real * filt_imag + imag * filt_real)
            enter_product(total_real, total_imag, (first, rows), pl.ds(b * width, width))
        return 0

    lax.fori_loop(0, block // rows, long_rows, 0)
    out = synthesise()
    ones = jnp.ones((8, width), jnp.bfloat16)
    spot = lax.broadcasted_iota(jnp.int32, (count, block), 0)
    total = jnp.zeros((count, block), jnp.float32)
    contract = (((1,), (1,)), ((), ()))
    for b in range(count):
        past = gated[b * block : (b + 1) * block, :].astype(jnp.float32)
        result = (past * out[:, b * width : (b + 1) * width]).astype(jnp.bfloat16)
        hyena[b * block : (b + 1) * block, :] = result
        wide = result.astype(jnp.float32)
        up, low = split_pair(wide * wide)
        row = lax.dot_general(ones, up, contract, preferred_element_type=jnp.float32) + lax.dot_general(
            ones, low, contract, preferred_element_type=jnp.float32
        )
        total = jnp.where(spot == b, row[0:1, :], total)
    sums[...] = total


def attend_rows(chip, core, side, queries, keys, values, allowed):
    block = allowed.shape[0]
    width = keys.shape[2]
    reach = (chip + 1) * 2 * block
    start = pl.multiple_of((2 * chip + core) * block, block)
    scores = lax.dot_general(
        queries[side, pl.ds(start, block), :],
        keys[side, 0:reach, :],
        (((1,), (1,)), ((), ())),
        preferred_element_type=jnp.float32,
    ) * (width**-0.5)
    last = jnp.where(allowed, scores[:, reach - 2 * block :], -1e30)
    scores = jnp.concatenate([scores[:, : reach - 2 * block], last], axis=1) if chip else last
    peak = jnp.max(scores, axis=1, keepdims=True)
    weights = jnp.exp(scores - peak)
    row_total = jnp.sum(weights, axis=1, keepdims=True)
    blended = dot32(weights.astype(jnp.bfloat16), values[side, 0:reach, :])
    return (blended / row_total).astype(jnp.bfloat16)


def fill_block(chip, place, signals, queries, keys, values, out):
    block, width = out.shape[1], keys.shape[2]
    core = lax.rem(lax.axis_index("seq"), 2)
    row_index = lax.broadcasted_iota(jnp.int32, (block, 2 * block), 0) + core * block
    allowed = lax.broadcasted_iota(jnp.int32, (block, 2 * block), 1) <= row_index
    start = pl.multiple_of((2 * chip + core) * block, block)
    for side, signal in enumerate(signals):
        half = lax.bitwise_xor(core, side)
        lanes = pl.ds(pl.multiple_of(half * width, width), width)
        out[place, :, lanes] = attend_rows(chip, core, side, queries, keys, values, allowed)
        lanes = pl.ds(pl.multiple_of((2 + half) * width, width), width)
        out[place, :, lanes] = signal[pl.ds(start, block), :]


def attend_kernel(own, other, sums, query_gain, key_gain, out, queries, keys, values, *, channel_count):
    length, width = own.shape
    count = sums.shape[1]
    block = length // count
    me = lax.axis_index("seq")
    total = jnp.sum(sums[...], axis=0)
    inverse = lax.rsqrt(total / channel_count + 1e-05)
    inverse = jnp.transpose(inverse, (1, 0))
    for side, signal in enumerate((own, other)):
        head = lax.bitwise_xor(me, side)
        lanes = pl.ds(pl.multiple_of(head * width, width), width)
        gain_q = query_gain[0:1, lanes]
        gain_k = key_gain[0:1, lanes]
        for b in range(count):
            spans = slice(b * block, (b + 1) * block)
            normed = signal[spans, :].astype(jnp.float32) * inverse[:, b : b + 1]
            values[side, spans, :] = normed.astype(jnp.bfloat16)
            keys[side, spans, :] = (normed * gain_k).astype(jnp.bfloat16)
            queries[side, spans, :] = (normed * gain_q).astype(jnp.bfloat16)
    for chip in range(count // 2):
        place = lax.bitwise_xor(me // 2, chip)

        @pl.when(place != 0)
        def _():
            fill_block(chip, place - 1, (own, other), queries, keys, values, out)


def attend_own_kernel(own, other, queries, keys, values, out):
    count = own.shape[0] // out.shape[1]
    for chip in range(count // 2):

        @pl.when(lax.axis_index("seq") // 2 == chip)
        def _():
            fill_block(chip, 0, (own, other), queries, keys, values, out)


def place_kernel(*refs):
    blocks, (hyena, attended) = refs[:-2], refs[-2:]
    span = blocks[0].shape[1] // 2
    chip = lax.axis_index("seq") // 2
    for i, block in enumerate(blocks):
        lanes = pl.ds(pl.multiple_of(lax.bitwise_xor(chip, i) * span, span), span)
        attended[:, lanes] = block[:, 0:span]
        hyena[:, lanes] = block[:, span : 2 * span]


def by_head(
    token_ids, embedding, short_filter, medium_filter, long_residue, long_rate, query_gain, key_gain
):
    seq_count = lax.axis_size("seq")
    ch_count = lax.axis_size("ch")
    block = token_ids.shape[0]
    width_dev = embedding.shape[1]
    length = block * seq_count
    width = HEAD
    f32, bf16 = jnp.float32, jnp.bfloat16
    forward, backward, tap_table = transform_tables(block)
    whole = pl.BlockSpec(memory_space=pltpu.VMEM)
    params = pltpu.CompilerParams(vmem_limit_bytes=24 * 1024 * 1024)

    def exchange(value, apart):
        return lax.ppermute(value, "seq", [(i, i ^ apart) for i in range(seq_count)])

    mode_total = long_rate.shape[0]
    in_hbm = pl.BlockSpec(memory_space=pltpu.HBM)

    def fetched(value):
        return pltpu.with_memory_space_constraint(value, pltpu.HBM)

    partner_ids = exchange(token_ids, 1)
    own_ids, medium_taps, taps_table, long_taps = pl.pallas_call(
        fetch_kernel,
        out_shape=[
            jax.ShapeDtypeStruct((block,), jnp.int32),
            jax.ShapeDtypeStruct((block, width), f32),
            jax.ShapeDtypeStruct(tap_table.shape, bf16),
            jax.ShapeDtypeStruct((block, length), f32),
        ],
        in_specs=[in_hbm] * 5,
        out_specs=[whole] * 4,
        scratch_shapes=[
            pltpu.VMEM((mode_total, width), f32),
            pltpu.VMEM((mode_total, width), f32),
            pltpu.VMEM((seq_count, mode_total, width), f32),
            pltpu.SemaphoreType.DMA((5,)),
        ],
        compiler_params=params,
        cost_estimate=pl.CostEstimate(flops=10**9, bytes_accessed=2 * 10**6, transcendentals=3 * 10**5),
        name="long_taps",
    )(*[fetched(value) for value in (token_ids, long_residue, long_rate, medium_filter, jnp.asarray(tap_table))])
    chip_ids = jnp.stack([own_ids, partner_ids])
    pieces = [chip_ids] + [exchange(chip_ids, apart) for apart in range(2, seq_count, 2)]
    medium_resp, long_resp = pl.pallas_call(
        response_kernel,
        out_shape=[
            jax.ShapeDtypeStruct((2 * block, width), f32),
            jax.ShapeDtypeStruct((2 * block, length), f32),
        ],
        in_specs=[whole] * 3,
        out_specs=[whole] * 2,
        compiler_params=params,
        cost_estimate=pl.CostEstimate(flops=8 * 10**8, bytes_accessed=2 * 10**6, transcendentals=0),
        name="filter_responses",
    )(medium_taps, long_taps, taps_table)

    hyena, square_sums = pl.pallas_call(
        functools.partial(conv_kernel, piece_count=len(pieces)),
        out_shape=[
            jax.ShapeDtypeStruct((length, width), bf16),
            jax.ShapeDtypeStruct((seq_count, block), f32),
        ],
        in_specs=[whole] * (len(pieces) + 6),
        out_specs=[whole, whole],
        scratch_shapes=[
            pltpu.VMEM((seq_count, block), jnp.int32),
            pltpu.VMEM((seq_count, block), jnp.int32),
            pltpu.VMEM((8 + length, width), f32),
            pltpu.VMEM((length, width), bf16),
            pltpu.VMEM((2 * block, length), bf16),
            pltpu.VMEM((2 * block, length), f32),
            pltpu.VMEM((2 * block, length), bf16),
            pltpu.VMEM((2 * block, length), bf16),
            pltpu.VMEM((2 * block, length), bf16),
        ],
        compiler_params=params,
        cost_estimate=pl.CostEstimate(flops=2 * 10**9, bytes_accessed=2 * 10**6, transcendentals=0),
        name="gated_convolutions",
    )(*pieces, embedding, short_filter, medium_resp, long_resp, forward, backward)

    other = exchange(hyena, 1)
    devices = seq_count * ch_count
    all_sums = lax.all_to_all(
        jnp.broadcast_to(square_sums[None], (devices, seq_count, block)), ("seq", "ch"), 0, 0, tiled=True
    )
    outgoing, queries, keys, values = pl.pallas_call(
        functools.partial(attend_kernel, channel_count=width_dev * ch_count),
        out_shape=[jax.ShapeDtypeStruct((seq_count // 2 - 1, block, 4 * width), bf16)]
        + [jax.ShapeDtypeStruct((2, length, width), bf16)] * 3,
        in_specs=[whole] * 5,
        out_specs=[whole] * 4,
        compiler_params=params,
        cost_estimate=pl.CostEstimate(flops=2 * 10**9, bytes_accessed=10**6, transcendentals=10**6),
        name="attention",
    )(hyena, other, all_sums, query_gain.reshape(1, width_dev), key_gain.reshape(1, width_dev))
    kept = pl.pallas_call(
        attend_own_kernel,
        out_shape=jax.ShapeDtypeStruct((1, block, 4 * width), bf16),
        in_specs=[whole] * 5,
        out_specs=whole,
        compiler_params=params,
        cost_estimate=pl.CostEstimate(flops=2 * 10**9, bytes_accessed=10**6, transcendentals=10**6),
        name="attention_own_block",
    )(hyena, other, queries, keys, values)
    blocks = [kept[0]] + [exchange(outgoing[i - 1], 2 * i) for i in range(1, seq_count // 2)]
    return pl.pallas_call(
        place_kernel,
        out_shape=[jax.ShapeDtypeStruct((block, width_dev), bf16)] * 2,
        in_specs=[whole] * len(blocks),
        out_specs=[whole, whole],
        compiler_params=params,
        name="placed_blocks",
    )(*blocks)


def on_device(*operands):
    seq_count = lax.axis_size("seq")
    token_ids, embedding, _, medium_filter = operands[:4]
    block = token_ids.shape[0]
    fits = (
        embedding.shape[1] == seq_count * HEAD
        and block == HEAD
        and medium_filter.shape[0] == block
        and seq_count % 8 == 0
        and seq_count & (seq_count - 1) == 0
    )
    return by_head(*operands) if fits else by_position(*operands)


def solution(mesh):
    in_specs = (
        P("seq"),
        P(None, "ch"),
        P(None, "ch"),
        P(None, "ch"),
        P(None, "ch"),
        P(None, "ch"),
        P("ch"),
        P("ch"),
    )
    out_specs = (P("seq", "ch"), P("seq", "ch"))
    return jax.shard_map(
        on_device, mesh=mesh, in_specs=in_specs, out_specs=out_specs, check_vma=False
    )
```

```python
import functools
import math

import jax
import jax.numpy as jnp
import ml_dtypes
import numpy as np
from jax import lax
from jax.experimental import pallas as pl
from jax.experimental.pallas import tpu as pltpu
from jax.sharding import PartitionSpec as P

C = 4096
HEAD = 128


def shifted(value, axis, steps):
    count = lax.axis_size(axis)
    leading, last = (max(0, -steps), min(count, count - steps))
    return lax.ppermute(value, axis, [(source, source + steps) for source in range(leading, last)])


def swapped(shard, axis, apart):
    return lax.ppermute(shard, axis, [(i, i ^ 1 << apart) for i in range(lax.axis_size(axis))])


def from_behind(shard, axis, by):
    size = lax.axis_size(axis)
    return lax.ppermute(shard, axis, [(i, (i + by) % size) for i in range(size)])


def rounded(value):
    return lax.optimization_barrier(value.astype(jnp.bfloat16))


def depthwise_conv(widened, tap_weights, row_count):
    tap_count = tap_weights.shape[0]

    def add_tap(tap_index, running):
        window = lax.dynamic_slice_in_dim(widened, tap_count - 1 - tap_index, row_count, 0)
        return running + tap_weights[tap_index] * window.astype(jnp.float32)

    return lax.fori_loop(
        0, tap_count, add_tap, jnp.zeros((row_count, widened.shape[1]), jnp.float32)
    )


def long_kernel_rows(residue_mine, rate_mine, length):
    positions = jnp.arange(length, dtype=jnp.int32).astype(jnp.float32)
    mode_total = rate_mine.shape[0]

    def add_mode(mode_index, running):
        decay_rate = rate_mine[mode_index]
        mode_weight = (
            residue_mine[mode_index]
            * jnp.sqrt(-jnp.expm1(-2.0 * decay_rate))
            / math.sqrt(mode_total)
        )
        return running + mode_weight[:, None] * jnp.exp(-decay_rate[:, None] * positions[None, :])

    return lax.fori_loop(
        0, mode_total, add_mode, jnp.zeros((rate_mine.shape[1], length), jnp.float32)
    )


def dft_tables(row_size, column_size, period_size):
    row_index = lax.broadcasted_iota(jnp.int32, (row_size, column_size), 0)
    column_index = lax.broadcasted_iota(jnp.int32, (row_size, column_size), 1)
    angles = (row_index * column_index % period_size).astype(jnp.float32) * (
        2.0 * math.pi / period_size
    )
    return (jnp.cos(angles), jnp.sin(angles))


def forward_dft(signal, outer_size, inner_size):
    highest = lax.Precision.HIGHEST
    cos_outer, sin_outer = dft_tables(outer_size // 2, outer_size, outer_size)
    twiddle_cos, twiddle_sin = dft_tables(outer_size, inner_size, outer_size * inner_size)
    cos_inner, sin_inner = dft_tables(inner_size, inner_size, inner_size)
    step_real = jnp.einsum("pab,ak->pkb", signal, cos_outer, precision=highest)
    step_imag = -jnp.einsum("pab,ak->pkb", signal, sin_outer, precision=highest)
    turned_real = step_real * twiddle_cos + step_imag * twiddle_sin
    turned_imag = step_imag * twiddle_cos - step_real * twiddle_sin
    spec_real = jnp.einsum("pkb,bm->pkm", turned_real, cos_inner, precision=highest) + jnp.einsum(
        "pkb,bm->pkm", turned_imag, sin_inner, precision=highest
    )
    spec_imag = jnp.einsum("pkb,bm->pkm", turned_imag, cos_inner, precision=highest) - jnp.einsum(
        "pkb,bm->pkm", turned_real, sin_inner, precision=highest
    )
    return (spec_real, spec_imag)


def inverse_dft(spec_real, spec_imag, outer_size, inner_size):
    highest = lax.Precision.HIGHEST
    cos_outer, sin_outer = dft_tables(outer_size // 2, outer_size, outer_size)
    twiddle_cos, twiddle_sin = dft_tables(outer_size, inner_size, outer_size * inner_size)
    cos_inner, sin_inner = dft_tables(inner_size, inner_size, inner_size)
    back_real = jnp.einsum("pkm,mb->pkb", spec_real, cos_inner, precision=highest) - jnp.einsum(
        "pkm,mb->pkb", spec_imag, sin_inner, precision=highest
    )
    back_imag = jnp.einsum("pkm,mb->pkb", spec_real, sin_inner, precision=highest) + jnp.einsum(
        "pkm,mb->pkb", spec_imag, cos_inner, precision=highest
    )
    turned_real = back_real * twiddle_cos - back_imag * twiddle_sin
    turned_imag = back_real * twiddle_sin + back_imag * twiddle_cos
    signal = jnp.einsum("pkb,ak->pab", turned_real, cos_outer, precision=highest) - jnp.einsum(
        "pkb,ak->pab", turned_imag, sin_outer, precision=highest
    )
    return signal / (outer_size * inner_size)


def attend_block(query_rows, query_index, key_block, value_block, key_start, running, score_scale):
    row_peak, row_total, blended = running
    scores = (
        jnp.einsum("qhd,khd->hqk", query_rows, key_block, preferred_element_type=jnp.float32)
        * score_scale
    )
    key_index = key_start + jnp.arange(key_block.shape[0], dtype=jnp.int32)
    scores = jnp.where(key_index[None, None, :] <= query_index[None, :, None], scores, -1e30)
    new_peak = jnp.maximum(row_peak, jnp.max(scores, axis=2))
    weights = jnp.exp(scores - new_peak[:, :, None])
    rescale = jnp.exp(row_peak - new_peak)
    row_total = row_total * rescale + jnp.sum(weights, axis=2)
    blended = blended * rescale[:, :, None] + jnp.einsum(
        "hqk,khd->hqd",
        weights.astype(jnp.bfloat16),
        value_block,
        preferred_element_type=jnp.float32,
    )
    return (new_peak, row_total, blended)


def merge_partials(first_part, second_part):
    peak_one, total_one, blend_one = first_part
    peak_two, total_two, blend_two = second_part
    new_peak = jnp.maximum(peak_one, peak_two)
    scale_one = jnp.exp(peak_one - new_peak)
    scale_two = jnp.exp(peak_two - new_peak)
    new_total = total_one * scale_one + total_two * scale_two
    new_blend = blend_one * scale_one[..., None] + blend_two * scale_two[..., None]
    return (new_peak, new_total, new_blend)


def split_halves(stacked_part, half_size, upper_side):
    lower_half = stacked_part[:, :half_size]
    upper_half = stacked_part[:, half_size:]
    keep_half = jnp.where(upper_side == 1, upper_half, lower_half)
    send_half = jnp.where(upper_side == 1, lower_half, upper_half)
    return (keep_half, send_half)


def by_position(
    token_ids, embedding, short_filter, medium_filter, long_residue, long_rate, query_gain, key_gain
):
    tok_count = token_ids.shape[0]
    vocab_size = embedding.shape[0]
    width_dev = embedding.shape[1]
    seq_count = lax.axis_size("seq")
    seq_index = lax.axis_index("seq")
    one_hot = (
        token_ids[:, None] == lax.broadcasted_iota(jnp.int32, (tok_count, vocab_size), 1)
    ).astype(jnp.bfloat16)
    embedded = jnp.dot(one_hot, embedding, preferred_element_type=jnp.float32).astype(jnp.bfloat16)
    short_taps = short_filter.shape[0]
    rim_rows = shifted(embedded[tok_count - (short_taps - 1) :], "seq", 1)
    widened = jnp.concatenate([rim_rows, embedded], axis=0)
    short_part = depthwise_conv(widened, short_filter, tok_count)
    short_gated = rounded(embedded.astype(jnp.float32) * short_part)
    medium_taps = medium_filter.shape[0]
    upper_rows = shifted(short_gated[tok_count - (medium_taps - 1) :], "seq", 1)
    widened_two = jnp.concatenate([upper_rows, short_gated], axis=0)
    medium_part = depthwise_conv(widened_two, medium_filter, tok_count)
    medium_gated = rounded(short_gated.astype(jnp.float32) * medium_part)
    per_dev = width_dev // seq_count
    length = tok_count * seq_count
    grouped = medium_gated.T.reshape(seq_count, per_dev, tok_count)
    spread = lax.all_to_all(grouped, "seq", split_axis=0, concat_axis=2, tiled=True).reshape(
        per_dev, length
    )
    rate_mine = lax.dynamic_slice_in_dim(long_rate, seq_index * per_dev, per_dev, 1)
    residue_mine = lax.dynamic_slice_in_dim(long_residue, seq_index * per_dev, per_dev, 1)
    kernel = long_kernel_rows(residue_mine, rate_mine, length)
    outer_size = 128
    inner_size = 2 * length // outer_size
    spread_float = spread.astype(jnp.float32)
    data_real, data_imag = forward_dft(
        spread_float.reshape(per_dev, outer_size // 2, inner_size), outer_size, inner_size
    )
    kernel_real, kernel_imag = forward_dft(
        kernel.reshape(per_dev, outer_size // 2, inner_size), outer_size, inner_size
    )
    product_real = data_real * kernel_real - data_imag * kernel_imag
    product_imag = data_real * kernel_imag + data_imag * kernel_real
    long_part = inverse_dft(product_real, product_imag, outer_size, inner_size).reshape(
        per_dev, length
    )
    channel_out = (spread_float * long_part).astype(jnp.bfloat16)
    returned = lax.all_to_all(channel_out[None], "seq", split_axis=2, concat_axis=0, tiled=True)
    hyena_out = returned.reshape(width_dev, tok_count).T
    head_count = width_dev // HEAD
    hyena_float = hyena_out.astype(jnp.float32)
    square_sums = jnp.sum(hyena_float * hyena_float, axis=1)
    total_sums = lax.psum(square_sums, "ch")
    inverse_scale = lax.rsqrt(total_sums / C + 1e-05)
    normed = hyena_float * inverse_scale[:, None]
    values = normed.astype(jnp.bfloat16).reshape(tok_count, head_count, HEAD)
    queries = (
        (normed * query_gain[None, :]).astype(jnp.bfloat16).reshape(tok_count, head_count, HEAD)
    )
    key_rows = (
        (normed * key_gain[None, :]).astype(jnp.bfloat16).reshape(tok_count, head_count, HEAD)
    )
    group_size = 2
    level_count = group_size.bit_length() - 1
    seq_bits = seq_count.bit_length() - 1
    base_bit = seq_bits - level_count
    stride = seq_count // group_size
    stacked = queries[None]
    level = 0
    bit_number = base_bit + level
    partner_rows = swapped(stacked, "seq", bit_number)
    upper_side = seq_index >> bit_number & 1
    stacked = jnp.where(
        upper_side == 1,
        jnp.concatenate([partner_rows, stacked], axis=0),
        jnp.concatenate([stacked, partner_rows], axis=0),
    )
    query_rows = stacked.reshape(group_size * tok_count, head_count, HEAD)
    group_first = seq_index % stride
    block_numbers = group_first + stride * jnp.arange(group_size, dtype=jnp.int32)
    query_index = (
        block_numbers[:, None] * tok_count + jnp.arange(tok_count, dtype=jnp.int32)[None, :]
    ).reshape(group_size * tok_count)
    score_scale = HEAD ** (-0.5)
    partial_state = (
        jnp.full((head_count, group_size * tok_count), -1e30, jnp.float32),
        jnp.zeros((head_count, group_size * tok_count), jnp.float32),
        jnp.zeros((head_count, group_size * tok_count, HEAD), jnp.float32),
    )

    def cycle_step(turn_number, carried):
        key_block, value_block, running = carried
        key_block, value_block = from_behind((key_block, value_block), "seq", -1)
        source_block = jnp.remainder(seq_index + turn_number, seq_count)
        running = attend_block(
            query_rows,
            query_index,
            key_block,
            value_block,
            source_block * tok_count,
            running,
            score_scale,
        )
        return (key_block, value_block, running)

    carried = lax.fori_loop(1, stride + 1, cycle_step, (key_rows, values, partial_state))
    row_peak, row_total, blended = carried[2]
    row_peak = row_peak.reshape(head_count, group_size, tok_count)
    row_total = row_total.reshape(head_count, group_size, tok_count)
    blended = blended.reshape(head_count, group_size, tok_count, HEAD)
    for level in reversed(range(level_count)):
        bit_number = base_bit + level
        half_size = row_peak.shape[1] // 2
        upper_side = seq_index >> bit_number & 1
        keep_peak, send_peak = split_halves(row_peak, half_size, upper_side)
        keep_total, send_total = split_halves(row_total, half_size, upper_side)
        keep_blend, send_blend = split_halves(blended, half_size, upper_side)
        got_peak, got_total, got_blend = swapped(
            (send_peak, send_total, send_blend), "seq", bit_number
        )
        row_peak, row_total, blended = merge_partials(
            (keep_peak, keep_total, keep_blend), (got_peak, got_total, got_blend)
        )
    normalized = blended[:, 0] / row_total[:, 0][:, :, None]
    attended = normalized.transpose(1, 0, 2).reshape(tok_count, width_dev).astype(jnp.bfloat16)
    return (hyena_out, attended)


def transform_tables(block):
    size = 2 * block
    step = 2.0 * np.pi / size
    freq = (np.arange(block) + 0.5)[:, None]
    angle = freq * np.arange(size)[None, :] * step
    forward = np.concatenate([np.cos(angle), -np.sin(angle)], axis=0)
    angle = (np.arange(block)[:, None] + block) * freq.T * step
    backward = np.concatenate([np.cos(angle), -np.sin(angle)], axis=1) * (2.0 / size)

    def parts(table):
        kept = []
        for _ in range(3):
            kept.append(table.astype(np.float32).astype(ml_dtypes.bfloat16))
            table = table - kept[-1].astype(np.float64)
        return np.concatenate(kept, axis=0)

    forward, backward = parts(forward), parts(backward)
    first, second, third = np.split(forward[:, :block], 3)
    taps = np.concatenate([np.concatenate([first, second], axis=1), np.concatenate([first, third], axis=1)], axis=0)
    return forward, backward, taps


def split_pair(value):
    upper = value.astype(jnp.bfloat16)
    return upper, (value - upper.astype(jnp.float32)).astype(jnp.bfloat16)


def split_three(value):
    upper = value.astype(jnp.bfloat16)
    rest = value - upper.astype(jnp.float32)
    middle = rest.astype(jnp.bfloat16)
    return upper, middle, (rest - middle.astype(jnp.float32)).astype(jnp.bfloat16)


def minus_expm1(value):
    term = value
    series = value
    for order in range(2, 11):
        term = term * value * (-1.0 / order)
        series = series + term
    return jnp.where(value < 0.5, series, 1.0 - jnp.exp(-value))


def dot32(left, right):
    return jnp.dot(left, right, preferred_element_type=jnp.float32)


def far_first(count):
    return [0, *range(count - 1, 0, -1)]


def own_lanes(width):
    return pl.ds(pl.multiple_of(lax.axis_index("seq") * width, width), width)


def fetch_kernel(
    token_ids, residue, rate, medium, table, ids_out, residue_out, rate_out, medium_out, table_out, sems
):
    lanes = own_lanes(medium_out.shape[1])
    copies = [
        pltpu.make_async_copy(source, target, sems.at[i])
        for i, (source, target) in enumerate(
            [
                (token_ids, ids_out),
                (residue.at[:, lanes], residue_out),
                (rate.at[:, lanes], rate_out),
                (medium.at[:, lanes], medium_out),
                (table, table_out),
            ]
        )
    ]
    for copy in copies:
        copy.start()
    for copy in copies:
        copy.wait()


def response_kernel(residue, rate, medium, table, medium_out, long_out):
    block, width = medium.shape
    size = 2 * block
    mode_total = rate.shape[0]
    block_total = long_out.shape[1] // width

    def transformed(signal):
        up, middle, low = split_three(signal)
        return (
            dot32(table[0:size, :], jnp.concatenate([up, up], axis=0))
            + dot32(table[0:size, :], jnp.concatenate([middle, middle], axis=0))
            + dot32(table[size : 2 * size, :], jnp.concatenate([low, up], axis=0))
        )

    medium_out[...] = transformed(medium[...])
    decays = rate[...]
    weights = residue[...] * jnp.sqrt(minus_expm1(2.0 * decays)) / math.sqrt(mode_total)
    modes = [weights * jnp.exp(-decays * float(part * block)) for part in range(block_total)]
    place = lax.broadcasted_iota(jnp.int32, (block, width), 0).astype(jnp.float32)
    rows = 32
    tiles = []
    for first in range(0, block, rows):
        sums = [jnp.zeros((rows, width), jnp.float32) for _ in range(block_total)]
        for mode in range(mode_total):
            shape = jnp.exp(-decays[mode : mode + 1, :] * place[first : first + rows])
            for part in range(block_total):
                sums[part] = sums[part] + modes[part][mode : mode + 1, :] * shape
        tiles.append(jnp.concatenate(sums, axis=1))
    long_out[...] = transformed(jnp.concatenate(tiles, axis=0))


def conv_kernel(*refs, piece_count):
    pieces = refs[:piece_count]
    (embedding, short, medium_resp, long_resp, forward, backward, hyena, sums) = refs[piece_count : piece_count + 8]
    ids, ordered, padded, row_sums = refs[piece_count + 8 :]
    width = padded.shape[1]
    block = width
    size = 2 * block
    length = hyena.shape[0]
    count = length // block
    pair = count // 2
    me = lax.axis_index("seq")
    for i, piece in zip(far_first(piece_count), pieces):
        ids[2 * i : 2 * i + 2, :] = piece[...]
    for b in range(count):
        ordered[b : b + 1, :] = ids[pl.ds(lax.bitwise_xor(me, b), 1), :]
    across = jnp.transpose(ordered[...].astype(jnp.float32), (1, 0)).astype(jnp.int32)
    padded[0:8, :] = jnp.zeros((8, width), jnp.float32)
    table = embedding[:, own_lanes(width)]
    short_taps = short[:, own_lanes(width)]
    vocab = table.shape[0]
    entries = lax.broadcasted_iota(jnp.int32, (block, vocab), 1)
    rows = 16

    def embed(chunk):
        for b in range(chunk * pair, (chunk + 1) * pair):
            chosen = jnp.where(across[:, b : b + 1] == entries, 1.0, 0.0).astype(jnp.bfloat16)
            padded[8 + b * block : 8 + (b + 1) * block, :] = dot32(chosen, table)

    nothing = jnp.zeros((block, width), jnp.bfloat16)
    gated = [{-1: nothing}, {-1: nothing}]
    spectra, products = [{}, {}], [{}, {}]

    def short_gate(chunk):
        for b in range(chunk * pair, (chunk + 1) * pair):
            running = jnp.zeros((block, width), jnp.float32)
            for j in range(short_taps.shape[0]):
                running = running + short_taps[j : j + 1, :] * padded[8 + b * block - j : 8 + (b + 1) * block - j, :]
            signal = padded[8 + b * block : 8 + (b + 1) * block, :] * running
            gated[0][b] = signal.astype(jnp.bfloat16)

    def analyse(turn, chunk):
        span = range(chunk * pair, (chunk + 1) * pair)
        signal = jnp.concatenate(
            [jnp.concatenate([gated[turn][b - 1] for b in span], axis=1)]
            + [jnp.concatenate([gated[turn][b] for b in span], axis=1)],
            axis=0,
        )
        spectrum = (
            dot32(forward[0:size, :], signal)
            + dot32(forward[size : 2 * size, :], signal)
            + dot32(forward[2 * size : 3 * size, :], signal)
        )
        for i, b in enumerate(span):
            spectra[turn][b] = spectrum[:, i * width : (i + 1) * width]

    def multiply(turn, response, chunk):
        columns = []
        for b in range(chunk * pair, (chunk + 1) * pair):
            tiles = [[], []]
            for first in range(0, block, rows):
                upper = slice(first, first + rows)
                lower = slice(block + first, block + first + rows)
                total_real, total_imag = 0.0, 0.0
                for part in range(b + 1 if turn else 1):
                    taps = slice(part * width, (part + 1) * width)
                    real, imag = spectra[turn][b - part][upper], spectra[turn][b - part][lower]
                    filt_real, filt_imag = response[upper, taps], response[lower, taps]
                    total_real = total_real + (real * filt_real - imag * filt_imag)
                    total_imag = total_imag + (real * filt_imag + imag * filt_real)
                tiles[0].append(split_three(total_real))
                tiles[1].append(split_three(total_imag))
            columns.append([jnp.concatenate([tile[i] for tile in tiles[0] + tiles[1]], axis=0) for i in range(3)])
        products[turn][chunk] = [jnp.concatenate([column[i] for column in columns], axis=1) for i in range(3)]

    def synthesise(turn, chunk):
        up, middle, low = products[turn].pop(chunk)
        first, second, third = [backward[i * block : (i + 1) * block, :] for i in range(3)]
        return (
            dot32(first, up)
            + (dot32(second, up) + dot32(first, middle))
            + (dot32(third, up) + dot32(second, middle) + dot32(first, low))
        )

    def gate(turn, chunk):
        out = synthesise(turn, chunk)
        results = []
        for i in range(pair):
            past = gated[turn][chunk * pair + i].astype(jnp.float32)
            results.append((past * out[:, i * width : (i + 1) * width]).astype(jnp.bfloat16))
        return results

    def medium_gate(chunk):
        for i, signal in enumerate(gate(0, chunk)):
            gated[1][chunk * pair + i] = signal

    ones = jnp.ones((size, width), jnp.bfloat16)
    diagonal = lax.broadcasted_iota(jnp.int32, (block, block), 0) == lax.broadcasted_iota(
        jnp.int32, (block, block), 1
    )

    def long_gate(chunk):
        for i, result in enumerate(gate(1, chunk)):
            b = chunk * pair + i
            hyena[b * block : (b + 1) * block, :] = result
            wide = result.astype(jnp.float32)
            spread = dot32(jnp.concatenate(split_pair(wide * wide), axis=1), ones)
            row_sums[b : b + 1, :] = jnp.sum(jnp.where(diagonal, spread, 0.0), axis=0, keepdims=True)

    stages = [
        embed,
        short_gate,
        functools.partial(analyse, 0),
        functools.partial(multiply, 0, medium_resp),
        medium_gate,
        functools.partial(analyse, 1),
        functools.partial(multiply, 1, long_resp),
        long_gate,
    ]
    chunks = count // pair
    for turn in range(chunks + len(stages) - 1):
        for stage in range(len(stages)):
            if 0 <= turn - stage < chunks:
                stages[stage](turn - stage)
    sums[...] = row_sums[...]


def attend_kernel(own, other, sums, query_gain, key_gain, out, queries, keys, values, *, channel_count):
    length, width = own.shape
    count = sums.shape[1]
    block = length // count
    me = lax.axis_index("seq")
    core = lax.rem(me, 2)
    total = jnp.sum(sums[...], axis=0)
    inverse = lax.rsqrt(total / channel_count + 1e-05)
    inverse = jnp.transpose(inverse, (1, 0))
    signals = (own, other)
    gains = []
    for side in range(2):
        lanes = pl.ds(pl.multiple_of(lax.bitwise_xor(me, side) * width, width), width)
        gains.append((query_gain[0:1, lanes], key_gain[0:1, lanes]))

    def normalise(b):
        spans = slice(b * block, (b + 1) * block)
        scale = jnp.broadcast_to(inverse[:, b : b + 1], (block, width))
        for side, signal in enumerate(signals):
            normed = signal[spans, :].astype(jnp.float32) * scale
            values[side, spans, :] = normed.astype(jnp.bfloat16)
            keys[side, spans, :] = (normed * gains[side][1]).astype(jnp.bfloat16)
            queries[side, spans, :] = (normed * gains[side][0]).astype(jnp.bfloat16)

    row_index = lax.broadcasted_iota(jnp.int32, (block, 2 * block), 0) + core * block
    allowed = lax.broadcasted_iota(jnp.int32, (block, 2 * block), 1) <= row_index

    def score(chip, side):
        reach = (chip + 1) * 2 * block
        start = pl.multiple_of((2 * chip + core) * block, block)
        scores = lax.dot_general(
            queries[side, pl.ds(start, block), :],
            keys[side, 0:reach, :],
            (((1,), (1,)), ((), ())),
            preferred_element_type=jnp.float32,
        )
        last = jnp.where(allowed, scores[:, reach - 2 * block :], -1e30)
        return jnp.concatenate([scores[:, : reach - 2 * block], last], axis=1) if chip else last

    def weigh(scores):
        peak = jnp.max(scores, axis=1, keepdims=True)
        weights = jnp.exp2((scores - peak) * (width**-0.5 * math.log2(math.e)))
        return weights.astype(jnp.bfloat16), jnp.sum(weights, axis=1, keepdims=True)

    def blend(chip, side, weights, row_total):
        reach = (chip + 1) * 2 * block
        start = pl.multiple_of((2 * chip + core) * block, block)
        place = lax.bitwise_xor(me // 2, chip)
        half = lax.bitwise_xor(core, side)
        blended = dot32(weights, values[side, 0:reach, :])
        lanes = pl.ds(pl.multiple_of(half * width, width), width)
        out[place, :, lanes] = (blended / row_total).astype(jnp.bfloat16)
        lanes = pl.ds(pl.multiple_of((2 + half) * width, width), width)
        out[place, :, lanes] = signals[side][pl.ds(start, block), :]

    for b in range(count):
        normalise(b)
    chains = [(chip, side) for chip in range(count // 2) for side in range(2)]
    scored, weighed = {}, {}
    for turn in range(len(chains) + 2):
        if turn < len(chains):
            scored[turn] = score(*chains[turn])
        if 0 <= turn - 1 < len(chains):
            weighed[turn - 1] = weigh(scored.pop(turn - 1))
        if 0 <= turn - 2 < len(chains):
            blend(*chains[turn - 2], *weighed.pop(turn - 2))


def place_kernel(*refs):
    blocks, (hyena, attended) = refs[:-2], refs[-2:]
    span = blocks[0].shape[1] // 2
    chip = lax.axis_index("seq") // 2
    for i, block in zip(far_first(len(blocks)), blocks):
        lanes = pl.ds(pl.multiple_of(lax.bitwise_xor(chip, i) * span, span), span)
        attended[:, lanes] = block[:, 0:span]
        hyena[:, lanes] = block[:, span : 2 * span]


def by_head(
    token_ids, embedding, short_filter, medium_filter, long_residue, long_rate, query_gain, key_gain
):
    seq_count = lax.axis_size("seq")
    ch_count = lax.axis_size("ch")
    block = token_ids.shape[0]
    width_dev = embedding.shape[1]
    length = block * seq_count
    width = HEAD
    f32, bf16 = jnp.float32, jnp.bfloat16
    forward, backward, tap_table = transform_tables(block)
    whole = pl.BlockSpec(memory_space=pltpu.VMEM)
    params = pltpu.CompilerParams(vmem_limit_bytes=24 * 1024 * 1024)

    def exchange(value, apart):
        return lax.ppermute(value, "seq", [(i, i ^ apart) for i in range(seq_count)])

    mode_total = long_rate.shape[0]
    in_hbm = pl.BlockSpec(memory_space=pltpu.HBM)

    def fetched(value):
        return pltpu.with_memory_space_constraint(value, pltpu.HBM)

    partner_ids = exchange(token_ids, 1)
    operands = (token_ids, long_residue, long_rate, medium_filter, jnp.asarray(tap_table))
    own_ids, *filters = pl.pallas_call(
        fetch_kernel,
        out_shape=[
            jax.ShapeDtypeStruct((block,), jnp.int32),
            jax.ShapeDtypeStruct((mode_total, width), f32),
            jax.ShapeDtypeStruct((mode_total, width), f32),
            jax.ShapeDtypeStruct((block, width), f32),
            jax.ShapeDtypeStruct(tap_table.shape, bf16),
        ],
        in_specs=[in_hbm] * 5,
        out_specs=[whole] * 5,
        scratch_shapes=[pltpu.SemaphoreType.DMA((5,))],
        compiler_params=params,
        cost_estimate=pl.CostEstimate(flops=10**9, bytes_accessed=2 * 10**6, transcendentals=0),
        name="fetched_operands",
    )(*[fetched(value) for value in operands])
    chip_ids = jnp.stack([own_ids, partner_ids])
    pieces = [chip_ids] + [exchange(chip_ids, 2 * i) for i in far_first(seq_count // 2)[1:]]
    medium_resp, long_resp = pl.pallas_call(
        response_kernel,
        out_shape=[
            jax.ShapeDtypeStruct((2 * block, width), f32),
            jax.ShapeDtypeStruct((2 * block, length), f32),
        ],
        in_specs=[whole] * 4,
        out_specs=[whole] * 2,
        compiler_params=params,
        cost_estimate=pl.CostEstimate(flops=2 * 10**9, bytes_accessed=2 * 10**6, transcendentals=3 * 10**5),
        name="filter_responses",
    )(*filters)

    hyena, square_sums = pl.pallas_call(
        functools.partial(conv_kernel, piece_count=len(pieces)),
        out_shape=[
            jax.ShapeDtypeStruct((length, width), bf16),
            jax.ShapeDtypeStruct((seq_count, block), f32),
        ],
        in_specs=[whole] * (len(pieces) + 6),
        out_specs=[whole, whole],
        scratch_shapes=[
            pltpu.VMEM((seq_count, block), jnp.int32),
            pltpu.VMEM((seq_count, block), jnp.int32),
            pltpu.VMEM((8 + length, width), f32),
            pltpu.VMEM((seq_count, block), f32),
        ],
        compiler_params=params,
        cost_estimate=pl.CostEstimate(flops=2 * 10**9, bytes_accessed=2 * 10**6, transcendentals=0),
        name="gated_convolutions",
    )(*pieces, embedding, short_filter, medium_resp, long_resp, forward, backward)

    other = exchange(hyena, 1)
    devices = seq_count * ch_count
    all_sums = lax.all_to_all(
        jnp.broadcast_to(square_sums[None], (devices, seq_count, block)), ("seq", "ch"), 0, 0, tiled=True
    )
    outgoing = pl.pallas_call(
        functools.partial(attend_kernel, channel_count=width_dev * ch_count),
        out_shape=jax.ShapeDtypeStruct((seq_count // 2, block, 4 * width), bf16),
        in_specs=[whole] * 5,
        out_specs=whole,
        scratch_shapes=[pltpu.VMEM((2, length, width), bf16)] * 3,
        compiler_params=params,
        cost_estimate=pl.CostEstimate(flops=2 * 10**9, bytes_accessed=10**6, transcendentals=10**6),
        name="attention",
    )(hyena, other, all_sums, query_gain.reshape(1, width_dev), key_gain.reshape(1, width_dev))
    blocks = [outgoing[0]] + [exchange(outgoing[i], 2 * i) for i in far_first(seq_count // 2)[1:]]
    return pl.pallas_call(
        place_kernel,
        out_shape=[jax.ShapeDtypeStruct((block, width_dev), bf16)] * 2,
        in_specs=[whole] * len(blocks),
        out_specs=[whole, whole],
        compiler_params=params,
        name="placed_blocks",
    )(*blocks)


def on_device(*operands):
    seq_count = lax.axis_size("seq")
    token_ids, embedding, _, medium_filter = operands[:4]
    block = token_ids.shape[0]
    fits = (
        embedding.shape[1] == seq_count * HEAD
        and block == HEAD
        and medium_filter.shape[0] == block
        and seq_count % 8 == 0
        and seq_count & (seq_count - 1) == 0
    )
    return by_head(*operands) if fits else by_position(*operands)


def solution(mesh):
    in_specs = (
        P("seq"),
        P(None, "ch"),
        P(None, "ch"),
        P(None, "ch"),
        P(None, "ch"),
        P(None, "ch"),
        P("ch"),
        P("ch"),
    )
    out_specs = (P("seq", "ch"), P("seq", "ch"))
    return jax.shard_map(
        on_device, mesh=mesh, in_specs=in_specs, out_specs=out_specs, check_vma=False
    )
```

```python
import functools
import math

import jax
import jax.numpy as jnp
import ml_dtypes
import numpy as np
from jax import lax
from jax.experimental import pallas as pl
from jax.experimental.pallas import tpu as pltpu
from jax.sharding import PartitionSpec as P

C = 4096
HEAD = 128


def shifted(value, axis, steps):
    count = lax.axis_size(axis)
    leading, last = (max(0, -steps), min(count, count - steps))
    return lax.ppermute(value, axis, [(source, source + steps) for source in range(leading, last)])


def swapped(shard, axis, apart):
    return lax.ppermute(shard, axis, [(i, i ^ 1 << apart) for i in range(lax.axis_size(axis))])


def from_behind(shard, axis, by):
    size = lax.axis_size(axis)
    return lax.ppermute(shard, axis, [(i, (i + by) % size) for i in range(size)])


def rounded(value):
    return lax.optimization_barrier(value.astype(jnp.bfloat16))


def depthwise_conv(widened, tap_weights, row_count):
    tap_count = tap_weights.shape[0]

    def add_tap(tap_index, running):
        window = lax.dynamic_slice_in_dim(widened, tap_count - 1 - tap_index, row_count, 0)
        return running + tap_weights[tap_index] * window.astype(jnp.float32)

    return lax.fori_loop(
        0, tap_count, add_tap, jnp.zeros((row_count, widened.shape[1]), jnp.float32)
    )


def long_kernel_rows(residue_mine, rate_mine, length):
    positions = jnp.arange(length, dtype=jnp.int32).astype(jnp.float32)
    mode_total = rate_mine.shape[0]

    def add_mode(mode_index, running):
        decay_rate = rate_mine[mode_index]
        mode_weight = (
            residue_mine[mode_index]
            * jnp.sqrt(-jnp.expm1(-2.0 * decay_rate))
            / math.sqrt(mode_total)
        )
        return running + mode_weight[:, None] * jnp.exp(-decay_rate[:, None] * positions[None, :])

    return lax.fori_loop(
        0, mode_total, add_mode, jnp.zeros((rate_mine.shape[1], length), jnp.float32)
    )


def dft_tables(row_size, column_size, period_size):
    row_index = lax.broadcasted_iota(jnp.int32, (row_size, column_size), 0)
    column_index = lax.broadcasted_iota(jnp.int32, (row_size, column_size), 1)
    angles = (row_index * column_index % period_size).astype(jnp.float32) * (
        2.0 * math.pi / period_size
    )
    return (jnp.cos(angles), jnp.sin(angles))


def forward_dft(signal, outer_size, inner_size):
    highest = lax.Precision.HIGHEST
    cos_outer, sin_outer = dft_tables(outer_size // 2, outer_size, outer_size)
    twiddle_cos, twiddle_sin = dft_tables(outer_size, inner_size, outer_size * inner_size)
    cos_inner, sin_inner = dft_tables(inner_size, inner_size, inner_size)
    step_real = jnp.einsum("pab,ak->pkb", signal, cos_outer, precision=highest)
    step_imag = -jnp.einsum("pab,ak->pkb", signal, sin_outer, precision=highest)
    turned_real = step_real * twiddle_cos + step_imag * twiddle_sin
    turned_imag = step_imag * twiddle_cos - step_real * twiddle_sin
    spec_real = jnp.einsum("pkb,bm->pkm", turned_real, cos_inner, precision=highest) + jnp.einsum(
        "pkb,bm->pkm", turned_imag, sin_inner, precision=highest
    )
    spec_imag = jnp.einsum("pkb,bm->pkm", turned_imag, cos_inner, precision=highest) - jnp.einsum(
        "pkb,bm->pkm", turned_real, sin_inner, precision=highest
    )
    return (spec_real, spec_imag)


def inverse_dft(spec_real, spec_imag, outer_size, inner_size):
    highest = lax.Precision.HIGHEST
    cos_outer, sin_outer = dft_tables(outer_size // 2, outer_size, outer_size)
    twiddle_cos, twiddle_sin = dft_tables(outer_size, inner_size, outer_size * inner_size)
    cos_inner, sin_inner = dft_tables(inner_size, inner_size, inner_size)
    back_real = jnp.einsum("pkm,mb->pkb", spec_real, cos_inner, precision=highest) - jnp.einsum(
        "pkm,mb->pkb", spec_imag, sin_inner, precision=highest
    )
    back_imag = jnp.einsum("pkm,mb->pkb", spec_real, sin_inner, precision=highest) + jnp.einsum(
        "pkm,mb->pkb", spec_imag, cos_inner, precision=highest
    )
    turned_real = back_real * twiddle_cos - back_imag * twiddle_sin
    turned_imag = back_real * twiddle_sin + back_imag * twiddle_cos
    signal = jnp.einsum("pkb,ak->pab", turned_real, cos_outer, precision=highest) - jnp.einsum(
        "pkb,ak->pab", turned_imag, sin_outer, precision=highest
    )
    return signal / (outer_size * inner_size)


def attend_block(query_rows, query_index, key_block, value_block, key_start, running, score_scale):
    row_peak, row_total, blended = running
    scores = (
        jnp.einsum("qhd,khd->hqk", query_rows, key_block, preferred_element_type=jnp.float32)
        * score_scale
    )
    key_index = key_start + jnp.arange(key_block.shape[0], dtype=jnp.int32)
    scores = jnp.where(key_index[None, None, :] <= query_index[None, :, None], scores, -1e30)
    new_peak = jnp.maximum(row_peak, jnp.max(scores, axis=2))
    weights = jnp.exp(scores - new_peak[:, :, None])
    rescale = jnp.exp(row_peak - new_peak)
    row_total = row_total * rescale + jnp.sum(weights, axis=2)
    blended = blended * rescale[:, :, None] + jnp.einsum(
        "hqk,khd->hqd",
        weights.astype(jnp.bfloat16),
        value_block,
        preferred_element_type=jnp.float32,
    )
    return (new_peak, row_total, blended)


def merge_partials(first_part, second_part):
    peak_one, total_one, blend_one = first_part
    peak_two, total_two, blend_two = second_part
    new_peak = jnp.maximum(peak_one, peak_two)
    scale_one = jnp.exp(peak_one - new_peak)
    scale_two = jnp.exp(peak_two - new_peak)
    new_total = total_one * scale_one + total_two * scale_two
    new_blend = blend_one * scale_one[..., None] + blend_two * scale_two[..., None]
    return (new_peak, new_total, new_blend)


def split_halves(stacked_part, half_size, upper_side):
    lower_half = stacked_part[:, :half_size]
    upper_half = stacked_part[:, half_size:]
    keep_half = jnp.where(upper_side == 1, upper_half, lower_half)
    send_half = jnp.where(upper_side == 1, lower_half, upper_half)
    return (keep_half, send_half)


def by_position(
    token_ids, embedding, short_filter, medium_filter, long_residue, long_rate, query_gain, key_gain
):
    tok_count = token_ids.shape[0]
    vocab_size = embedding.shape[0]
    width_dev = embedding.shape[1]
    seq_count = lax.axis_size("seq")
    seq_index = lax.axis_index("seq")
    one_hot = (
        token_ids[:, None] == lax.broadcasted_iota(jnp.int32, (tok_count, vocab_size), 1)
    ).astype(jnp.bfloat16)
    embedded = jnp.dot(one_hot, embedding, preferred_element_type=jnp.float32).astype(jnp.bfloat16)
    short_taps = short_filter.shape[0]
    rim_rows = shifted(embedded[tok_count - (short_taps - 1) :], "seq", 1)
    widened = jnp.concatenate([rim_rows, embedded], axis=0)
    short_part = depthwise_conv(widened, short_filter, tok_count)
    short_gated = rounded(embedded.astype(jnp.float32) * short_part)
    medium_taps = medium_filter.shape[0]
    upper_rows = shifted(short_gated[tok_count - (medium_taps - 1) :], "seq", 1)
    widened_two = jnp.concatenate([upper_rows, short_gated], axis=0)
    medium_part = depthwise_conv(widened_two, medium_filter, tok_count)
    medium_gated = rounded(short_gated.astype(jnp.float32) * medium_part)
    per_dev = width_dev // seq_count
    length = tok_count * seq_count
    grouped = medium_gated.T.reshape(seq_count, per_dev, tok_count)
    spread = lax.all_to_all(grouped, "seq", split_axis=0, concat_axis=2, tiled=True).reshape(
        per_dev, length
    )
    rate_mine = lax.dynamic_slice_in_dim(long_rate, seq_index * per_dev, per_dev, 1)
    residue_mine = lax.dynamic_slice_in_dim(long_residue, seq_index * per_dev, per_dev, 1)
    kernel = long_kernel_rows(residue_mine, rate_mine, length)
    outer_size = 128
    inner_size = 2 * length // outer_size
    spread_float = spread.astype(jnp.float32)
    data_real, data_imag = forward_dft(
        spread_float.reshape(per_dev, outer_size // 2, inner_size), outer_size, inner_size
    )
    kernel_real, kernel_imag = forward_dft(
        kernel.reshape(per_dev, outer_size // 2, inner_size), outer_size, inner_size
    )
    product_real = data_real * kernel_real - data_imag * kernel_imag
    product_imag = data_real * kernel_imag + data_imag * kernel_real
    long_part = inverse_dft(product_real, product_imag, outer_size, inner_size).reshape(
        per_dev, length
    )
    channel_out = (spread_float * long_part).astype(jnp.bfloat16)
    returned = lax.all_to_all(channel_out[None], "seq", split_axis=2, concat_axis=0, tiled=True)
    hyena_out = returned.reshape(width_dev, tok_count).T
    head_count = width_dev // HEAD
    hyena_float = hyena_out.astype(jnp.float32)
    square_sums = jnp.sum(hyena_float * hyena_float, axis=1)
    total_sums = lax.psum(square_sums, "ch")
    inverse_scale = lax.rsqrt(total_sums / C + 1e-05)
    normed = hyena_float * inverse_scale[:, None]
    values = normed.astype(jnp.bfloat16).reshape(tok_count, head_count, HEAD)
    queries = (
        (normed * query_gain[None, :]).astype(jnp.bfloat16).reshape(tok_count, head_count, HEAD)
    )
    key_rows = (
        (normed * key_gain[None, :]).astype(jnp.bfloat16).reshape(tok_count, head_count, HEAD)
    )
    group_size = 2
    level_count = group_size.bit_length() - 1
    seq_bits = seq_count.bit_length() - 1
    base_bit = seq_bits - level_count
    stride = seq_count // group_size
    stacked = queries[None]
    level = 0
    bit_number = base_bit + level
    partner_rows = swapped(stacked, "seq", bit_number)
    upper_side = seq_index >> bit_number & 1
    stacked = jnp.where(
        upper_side == 1,
        jnp.concatenate([partner_rows, stacked], axis=0),
        jnp.concatenate([stacked, partner_rows], axis=0),
    )
    query_rows = stacked.reshape(group_size * tok_count, head_count, HEAD)
    group_first = seq_index % stride
    block_numbers = group_first + stride * jnp.arange(group_size, dtype=jnp.int32)
    query_index = (
        block_numbers[:, None] * tok_count + jnp.arange(tok_count, dtype=jnp.int32)[None, :]
    ).reshape(group_size * tok_count)
    score_scale = HEAD ** (-0.5)
    partial_state = (
        jnp.full((head_count, group_size * tok_count), -1e30, jnp.float32),
        jnp.zeros((head_count, group_size * tok_count), jnp.float32),
        jnp.zeros((head_count, group_size * tok_count, HEAD), jnp.float32),
    )

    def cycle_step(turn_number, carried):
        key_block, value_block, running = carried
        key_block, value_block = from_behind((key_block, value_block), "seq", -1)
        source_block = jnp.remainder(seq_index + turn_number, seq_count)
        running = attend_block(
            query_rows,
            query_index,
            key_block,
            value_block,
            source_block * tok_count,
            running,
            score_scale,
        )
        return (key_block, value_block, running)

    carried = lax.fori_loop(1, stride + 1, cycle_step, (key_rows, values, partial_state))
    row_peak, row_total, blended = carried[2]
    row_peak = row_peak.reshape(head_count, group_size, tok_count)
    row_total = row_total.reshape(head_count, group_size, tok_count)
    blended = blended.reshape(head_count, group_size, tok_count, HEAD)
    for level in reversed(range(level_count)):
        bit_number = base_bit + level
        half_size = row_peak.shape[1] // 2
        upper_side = seq_index >> bit_number & 1
        keep_peak, send_peak = split_halves(row_peak, half_size, upper_side)
        keep_total, send_total = split_halves(row_total, half_size, upper_side)
        keep_blend, send_blend = split_halves(blended, half_size, upper_side)
        got_peak, got_total, got_blend = swapped(
            (send_peak, send_total, send_blend), "seq", bit_number
        )
        row_peak, row_total, blended = merge_partials(
            (keep_peak, keep_total, keep_blend), (got_peak, got_total, got_blend)
        )
    normalized = blended[:, 0] / row_total[:, 0][:, :, None]
    attended = normalized.transpose(1, 0, 2).reshape(tok_count, width_dev).astype(jnp.bfloat16)
    return (hyena_out, attended)


def transform_tables(block):
    size = 2 * block
    step = 2.0 * np.pi / size
    freq = (np.arange(block) + 0.5)[:, None]
    angle = freq * np.arange(size)[None, :] * step
    forward = np.concatenate([np.cos(angle), -np.sin(angle)], axis=0)
    angle = (np.arange(block)[:, None] + block) * freq.T * step
    backward = np.concatenate([np.cos(angle), -np.sin(angle)], axis=1) * (2.0 / size)

    def parts(table):
        kept = []
        for _ in range(3):
            kept.append(table.astype(np.float32).astype(ml_dtypes.bfloat16))
            table = table - kept[-1].astype(np.float64)
        return np.concatenate(kept, axis=0)

    forward, backward = parts(forward), parts(backward)
    first, second, third = np.split(forward[:, :block], 3)
    taps = np.concatenate([np.concatenate([first, second], axis=1), np.concatenate([first, third], axis=1)], axis=0)
    return forward, backward, taps


def split_pair(value):
    upper = value.astype(jnp.bfloat16)
    return upper, (value - upper.astype(jnp.float32)).astype(jnp.bfloat16)


def split_three(value):
    upper = value.astype(jnp.bfloat16)
    rest = value - upper.astype(jnp.float32)
    middle = rest.astype(jnp.bfloat16)
    return upper, middle, (rest - middle.astype(jnp.float32)).astype(jnp.bfloat16)


def minus_expm1(value):
    term = value
    series = value
    for order in range(2, 11):
        term = term * value * (-1.0 / order)
        series = series + term
    return jnp.where(value < 0.5, series, 1.0 - jnp.exp(-value))


def dot32(left, right):
    return jnp.dot(left, right, preferred_element_type=jnp.float32)


def far_first(count):
    return [0, *range(count - 1, 0, -1)]


def own_lanes(width):
    return pl.ds(pl.multiple_of(lax.axis_index("seq") * width, width), width)


def fetch_kernel(
    token_ids, residue, rate, medium, table, ids_out, residue_out, rate_out, medium_out, table_out, sems
):
    lanes = own_lanes(medium_out.shape[1])
    copies = [
        pltpu.make_async_copy(source, target, sems.at[i])
        for i, (source, target) in enumerate(
            [
                (token_ids, ids_out),
                (residue.at[:, lanes], residue_out),
                (rate.at[:, lanes], rate_out),
                (medium.at[:, lanes], medium_out),
                (table, table_out),
            ]
        )
    ]
    for copy in copies:
        copy.start()
    for copy in copies:
        copy.wait()


def response_kernel(residue, rate, medium, table, medium_out, long_out):
    block, width = medium.shape
    size = 2 * block
    mode_total = rate.shape[0]
    block_total = long_out.shape[1] // width

    def transformed(signal):
        up, middle, low = split_three(signal)
        return (
            dot32(table[0:size, :], jnp.concatenate([up, up], axis=0))
            + dot32(table[0:size, :], jnp.concatenate([middle, middle], axis=0))
            + dot32(table[size : 2 * size, :], jnp.concatenate([low, up], axis=0))
        )

    medium_out[...] = transformed(medium[...])
    decays = rate[...]
    weights = residue[...] * jnp.sqrt(minus_expm1(2.0 * decays)) / math.sqrt(mode_total)
    modes = [weights * jnp.exp(-decays * float(part * block)) for part in range(block_total)]
    place = lax.broadcasted_iota(jnp.int32, (block, width), 0).astype(jnp.float32)
    rows = 32
    tiles = []
    for first in range(0, block, rows):
        sums = [jnp.zeros((rows, width), jnp.float32) for _ in range(block_total)]
        for mode in range(mode_total):
            shape = jnp.exp(-decays[mode : mode + 1, :] * place[first : first + rows])
            for part in range(block_total):
                sums[part] = sums[part] + modes[part][mode : mode + 1, :] * shape
        tiles.append(jnp.concatenate(sums, axis=1))
    long_out[...] = transformed(jnp.concatenate(tiles, axis=0))


def conv_kernel(*refs, piece_count):
    pieces = refs[:piece_count]
    (embedding, short, medium_resp, long_resp, forward, backward, hyena, sums) = refs[piece_count : piece_count + 8]
    ids, ordered, padded, row_sums = refs[piece_count + 8 :]
    width = padded.shape[1]
    block = width
    size = 2 * block
    length = hyena.shape[0]
    count = length // block
    pair = count // 2
    me = lax.axis_index("seq")
    for i, piece in zip(far_first(piece_count), pieces):
        ids[2 * i : 2 * i + 2, :] = piece[...]
    for b in range(count):
        ordered[b : b + 1, :] = ids[pl.ds(lax.bitwise_xor(me, b), 1), :]
    across = jnp.transpose(ordered[...].astype(jnp.float32), (1, 0)).astype(jnp.int32)
    padded[0:8, :] = jnp.zeros((8, width), jnp.float32)
    table = embedding[:, own_lanes(width)]
    short_taps = short[:, own_lanes(width)]
    vocab = table.shape[0]
    entries = lax.broadcasted_iota(jnp.int32, (block, vocab), 1)
    rows = 16

    def embed(chunk):
        for b in range(chunk * pair, (chunk + 1) * pair):
            chosen = jnp.where(across[:, b : b + 1] == entries, 1.0, 0.0).astype(jnp.bfloat16)
            padded[8 + b * block : 8 + (b + 1) * block, :] = dot32(chosen, table)

    nothing = jnp.zeros((block, width), jnp.bfloat16)
    gated = [{-1: nothing}, {-1: nothing}]
    spectra, products = [{}, {}], [{}, {}]

    def short_gate(chunk):
        for b in range(chunk * pair, (chunk + 1) * pair):
            running = jnp.zeros((block, width), jnp.float32)
            for j in range(short_taps.shape[0]):
                running = running + short_taps[j : j + 1, :] * padded[8 + b * block - j : 8 + (b + 1) * block - j, :]
            signal = padded[8 + b * block : 8 + (b + 1) * block, :] * running
            gated[0][b] = signal.astype(jnp.bfloat16)

    def analyse(turn, chunk):
        span = range(chunk * pair, (chunk + 1) * pair)
        signal = jnp.concatenate(
            [jnp.concatenate([gated[turn][b - 1] for b in span], axis=1)]
            + [jnp.concatenate([gated[turn][b] for b in span], axis=1)],
            axis=0,
        )
        spectrum = (
            dot32(forward[0:size, :], signal)
            + dot32(forward[size : 2 * size, :], signal)
            + dot32(forward[2 * size : 3 * size, :], signal)
        )
        for i, b in enumerate(span):
            spectra[turn][b] = spectrum[:, i * width : (i + 1) * width]

    def multiply(turn, response, chunk):
        columns = []
        for b in range(chunk * pair, (chunk + 1) * pair):
            tiles = [[], []]
            for first in range(0, block, rows):
                upper = slice(first, first + rows)
                lower = slice(block + first, block + first + rows)
                total_real, total_imag = 0.0, 0.0
                for part in range(b + 1 if turn else 1):
                    taps = slice(part * width, (part + 1) * width)
                    real, imag = spectra[turn][b - part][upper], spectra[turn][b - part][lower]
                    filt_real, filt_imag = response[upper, taps], response[lower, taps]
                    total_real = total_real + (real * filt_real - imag * filt_imag)
                    total_imag = total_imag + (real * filt_imag + imag * filt_real)
                tiles[0].append(split_three(total_real))
                tiles[1].append(split_three(total_imag))
            columns.append([jnp.concatenate([tile[i] for tile in tiles[0] + tiles[1]], axis=0) for i in range(3)])
        products[turn][chunk] = [jnp.concatenate([column[i] for column in columns], axis=1) for i in range(3)]

    def synthesise(turn, chunk):
        up, middle, low = products[turn].pop(chunk)
        first, second, third = [backward[i * block : (i + 1) * block, :] for i in range(3)]
        return (
            dot32(first, up)
            + (dot32(second, up) + dot32(first, middle))
            + (dot32(third, up) + dot32(second, middle) + dot32(first, low))
        )

    def gate(turn, chunk):
        out = synthesise(turn, chunk)
        results = []
        for i in range(pair):
            past = gated[turn][chunk * pair + i].astype(jnp.float32)
            results.append((past * out[:, i * width : (i + 1) * width]).astype(jnp.bfloat16))
        return results

    def medium_gate(chunk):
        for i, signal in enumerate(gate(0, chunk)):
            gated[1][chunk * pair + i] = signal

    ones = jnp.ones((size, width), jnp.bfloat16)
    diagonal = lax.broadcasted_iota(jnp.int32, (block, block), 0) == lax.broadcasted_iota(
        jnp.int32, (block, block), 1
    )

    def long_gate(chunk):
        for i, result in enumerate(gate(1, chunk)):
            b = chunk * pair + i
            hyena[b * block : (b + 1) * block, :] = result
            wide = result.astype(jnp.float32)
            spread = dot32(jnp.concatenate(split_pair(wide * wide), axis=1), ones)
            row_sums[b : b + 1, :] = jnp.sum(jnp.where(diagonal, spread, 0.0), axis=0, keepdims=True)

    stages = [
        embed,
        short_gate,
        functools.partial(analyse, 0),
        functools.partial(multiply, 0, medium_resp),
        medium_gate,
        functools.partial(analyse, 1),
        functools.partial(multiply, 1, long_resp),
        long_gate,
    ]
    chunks = count // pair
    for turn in range(chunks + len(stages) - 1):
        for stage in range(len(stages)):
            if 0 <= turn - stage < chunks:
                stages[stage](turn - stage)
    sums[...] = row_sums[...]


def attend_kernel(own, other, sums, query_gain, key_gain, out, queries, keys, values, *, channel_count):
    length, width = own.shape
    count = sums.shape[1]
    block = length // count
    me = lax.axis_index("seq")
    core = lax.rem(me, 2)
    total = jnp.sum(sums[...], axis=0)
    inverse = lax.rsqrt(total / channel_count + 1e-05)
    inverse = jnp.transpose(inverse, (1, 0))
    signals = (own, other)
    gains = []
    for side in range(2):
        lanes = pl.ds(pl.multiple_of(lax.bitwise_xor(me, side) * width, width), width)
        gains.append((query_gain[0:1, lanes], key_gain[0:1, lanes]))

    def normalise(b):
        spans = slice(b * block, (b + 1) * block)
        scale = jnp.broadcast_to(inverse[:, b : b + 1], (block, width))
        for side, signal in enumerate(signals):
            normed = signal[spans, :].astype(jnp.float32) * scale
            values[side, spans, :] = normed.astype(jnp.bfloat16)
            keys[side, spans, :] = (normed * gains[side][1]).astype(jnp.bfloat16)
            queries[side, spans, :] = (normed * gains[side][0]).astype(jnp.bfloat16)

    row_index = lax.broadcasted_iota(jnp.int32, (block, 2 * block), 0) + core * block
    allowed = lax.broadcasted_iota(jnp.int32, (block, 2 * block), 1) <= row_index

    def score(chip, side):
        reach = (chip + 1) * 2 * block
        start = pl.multiple_of((2 * chip + core) * block, block)
        scores = lax.dot_general(
            queries[side, pl.ds(start, block), :],
            keys[side, 0:reach, :],
            (((1,), (1,)), ((), ())),
            preferred_element_type=jnp.float32,
        )
        last = jnp.where(allowed, scores[:, reach - 2 * block :], -1e30)
        return jnp.concatenate([scores[:, : reach - 2 * block], last], axis=1) if chip else last

    def weigh(scores):
        peak = jnp.max(scores, axis=1, keepdims=True)
        weights = jnp.exp2((scores - peak) * (width**-0.5 * math.log2(math.e)))
        return weights.astype(jnp.bfloat16), jnp.sum(weights, axis=1, keepdims=True)

    def blend(chip, side, weights, row_total):
        reach = (chip + 1) * 2 * block
        place = lax.bitwise_xor(me // 2, chip)
        half = lax.bitwise_xor(core, side)
        blended = dot32(weights, values[side, 0:reach, :])
        lanes = pl.ds(pl.multiple_of(half * width, width), width)
        out[place, :, lanes] = (blended / row_total).astype(jnp.bfloat16)

    for b in range(count):
        normalise(b)
    chains = [(chip, side) for chip in range(count // 2) for side in range(2)]
    scored, weighed = {}, {}
    for turn in range(len(chains) + 2):
        if turn < len(chains):
            scored[turn] = score(*chains[turn])
        if 0 <= turn - 1 < len(chains):
            weighed[turn - 1] = weigh(scored.pop(turn - 1))
        if 0 <= turn - 2 < len(chains):
            blend(*chains[turn - 2], *weighed.pop(turn - 2))


def outgoing_kernel(own, other, out):
    width = own.shape[1]
    block = out.shape[1]
    me = lax.axis_index("seq")
    core = lax.rem(me, 2)
    for i in range(out.shape[0]):
        start = pl.multiple_of((2 * lax.bitwise_xor(me // 2, i) + core) * block, block)
        for side, signal in enumerate((own, other)):
            lanes = pl.ds(pl.multiple_of(lax.bitwise_xor(core, side) * width, width), width)
            out[i, :, lanes] = signal[pl.ds(start, block), :]


def hold_kernel(*refs):
    refs[-1][...] = refs[0][...]


def place_kernel(*refs):
    blocks, out = refs[:-1], refs[-1]
    span = blocks[0].shape[1]
    chip = lax.axis_index("seq") // 2
    for i, block in zip(far_first(len(blocks)), blocks):
        out[:, pl.ds(pl.multiple_of(lax.bitwise_xor(chip, i) * span, span), span)] = block[...]


def by_head(
    token_ids, embedding, short_filter, medium_filter, long_residue, long_rate, query_gain, key_gain
):
    seq_count = lax.axis_size("seq")
    ch_count = lax.axis_size("ch")
    block = token_ids.shape[0]
    width_dev = embedding.shape[1]
    length = block * seq_count
    width = HEAD
    f32, bf16 = jnp.float32, jnp.bfloat16
    forward, backward, tap_table = transform_tables(block)
    whole = pl.BlockSpec(memory_space=pltpu.VMEM)
    params = pltpu.CompilerParams(vmem_limit_bytes=24 * 1024 * 1024)

    def exchange(value, apart):
        return lax.ppermute(value, "seq", [(i, i ^ apart) for i in range(seq_count)])

    mode_total = long_rate.shape[0]
    in_hbm = pl.BlockSpec(memory_space=pltpu.HBM)

    def fetched(value):
        return pltpu.with_memory_space_constraint(value, pltpu.HBM)

    partner_ids = exchange(token_ids, 1)
    operands = (token_ids, long_residue, long_rate, medium_filter, jnp.asarray(tap_table))
    own_ids, *filters = pl.pallas_call(
        fetch_kernel,
        out_shape=[
            jax.ShapeDtypeStruct((block,), jnp.int32),
            jax.ShapeDtypeStruct((mode_total, width), f32),
            jax.ShapeDtypeStruct((mode_total, width), f32),
            jax.ShapeDtypeStruct((block, width), f32),
            jax.ShapeDtypeStruct(tap_table.shape, bf16),
        ],
        in_specs=[in_hbm] * 5,
        out_specs=[whole] * 5,
        scratch_shapes=[pltpu.SemaphoreType.DMA((5,))],
        compiler_params=params,
        cost_estimate=pl.CostEstimate(flops=10**9, bytes_accessed=2 * 10**6, transcendentals=0),
        name="fetched_operands",
    )(*[fetched(value) for value in operands])
    chip_ids = jnp.stack([own_ids, partner_ids])
    pieces = [chip_ids] + [exchange(chip_ids, 2 * i) for i in far_first(seq_count // 2)[1:]]
    medium_resp, long_resp = pl.pallas_call(
        response_kernel,
        out_shape=[
            jax.ShapeDtypeStruct((2 * block, width), f32),
            jax.ShapeDtypeStruct((2 * block, length), f32),
        ],
        in_specs=[whole] * 4,
        out_specs=[whole] * 2,
        compiler_params=params,
        cost_estimate=pl.CostEstimate(flops=2 * 10**9, bytes_accessed=2 * 10**6, transcendentals=3 * 10**5),
        name="filter_responses",
    )(*filters)

    hyena, square_sums = pl.pallas_call(
        functools.partial(conv_kernel, piece_count=len(pieces)),
        out_shape=[
            jax.ShapeDtypeStruct((length, width), bf16),
            jax.ShapeDtypeStruct((seq_count, block), f32),
        ],
        in_specs=[whole] * (len(pieces) + 6),
        out_specs=[whole, whole],
        scratch_shapes=[
            pltpu.VMEM((seq_count, block), jnp.int32),
            pltpu.VMEM((seq_count, block), jnp.int32),
            pltpu.VMEM((8 + length, width), f32),
            pltpu.VMEM((seq_count, block), f32),
        ],
        compiler_params=params,
        cost_estimate=pl.CostEstimate(flops=2 * 10**9, bytes_accessed=2 * 10**6, transcendentals=0),
        name="gated_convolutions",
    )(*pieces, embedding, short_filter, medium_resp, long_resp, forward, backward)

    other = exchange(hyena, 1)
    devices = seq_count * ch_count
    all_sums = lax.all_to_all(
        jnp.broadcast_to(square_sums[None], (devices, seq_count, block)), ("seq", "ch"), 0, 0, tiled=True
    )

    def placed(blocks, name):
        return pl.pallas_call(
            place_kernel,
            out_shape=jax.ShapeDtypeStruct((block, width_dev), bf16),
            in_specs=[whole] * len(blocks),
            out_specs=whole,
            compiler_params=params,
            cost_estimate=pl.CostEstimate(flops=10**9, bytes_accessed=10**6, transcendentals=0),
            name=name,
        )(*blocks)

    def held(value, others):
        return pl.pallas_call(
            hold_kernel,
            out_shape=jax.ShapeDtypeStruct(value.shape, value.dtype),
            in_specs=[whole] + [pl.BlockSpec(memory_space=pl.ANY)] * len(others),
            out_specs=whole,
            compiler_params=params,
            name="held_block",
        )(value, *others)

    order = far_first(seq_count // 2)
    hyena_blocks = pl.pallas_call(
        outgoing_kernel,
        out_shape=jax.ShapeDtypeStruct((seq_count // 2, block, 2 * width), bf16),
        in_specs=[whole, whole],
        out_specs=whole,
        compiler_params=params,
        cost_estimate=pl.CostEstimate(flops=2 * 10**9, bytes_accessed=10**6, transcendentals=0),
        name="hyena_blocks",
    )(hyena, other)
    hyena_parts = [hyena_blocks[0]] + [exchange(hyena_blocks[i], 2 * i) for i in order[1:]]
    outgoing = pl.pallas_call(
        functools.partial(attend_kernel, channel_count=width_dev * ch_count),
        out_shape=jax.ShapeDtypeStruct((seq_count // 2, block, 2 * width), bf16),
        in_specs=[whole] * 5,
        out_specs=whole,
        scratch_shapes=[pltpu.VMEM((2, length, width), bf16)] * 3,
        compiler_params=params,
        cost_estimate=pl.CostEstimate(flops=2 * 10**9, bytes_accessed=10**6, transcendentals=10**6),
        name="attention",
    )(hyena, other, all_sums, query_gain.reshape(1, width_dev), key_gain.reshape(1, width_dev))
    last = held(outgoing[order[-1]], hyena_parts[1:])
    parts = [outgoing[0]] + [exchange(outgoing[i], 2 * i) for i in order[1:-1]] + [exchange(last, 2 * order[-1])]
    return placed(hyena_parts, "placed_hyena"), placed(parts, "placed_attended")


def on_device(*operands):
    seq_count = lax.axis_size("seq")
    token_ids, embedding, _, medium_filter = operands[:4]
    block = token_ids.shape[0]
    fits = (
        embedding.shape[1] == seq_count * HEAD
        and block == HEAD
        and medium_filter.shape[0] == block
        and seq_count % 8 == 0
        and seq_count & (seq_count - 1) == 0
    )
    return by_head(*operands) if fits else by_position(*operands)


def solution(mesh):
    in_specs = (
        P("seq"),
        P(None, "ch"),
        P(None, "ch"),
        P(None, "ch"),
        P(None, "ch"),
        P(None, "ch"),
        P("ch"),
        P("ch"),
    )
    out_specs = (P("seq", "ch"), P("seq", "ch"))
    return jax.shard_map(
        on_device, mesh=mesh, in_specs=in_specs, out_specs=out_specs, check_vma=False
    )
```

```python
import functools
import math

import jax
import jax.numpy as jnp
import ml_dtypes
import numpy as np
from jax import lax
from jax.experimental import pallas as pl
from jax.experimental.pallas import tpu as pltpu
from jax.sharding import PartitionSpec as P

C = 4096
HEAD = 128


def shifted(value, axis, steps):
    count = lax.axis_size(axis)
    leading, last = (max(0, -steps), min(count, count - steps))
    return lax.ppermute(value, axis, [(source, source + steps) for source in range(leading, last)])


def swapped(shard, axis, apart):
    return lax.ppermute(shard, axis, [(i, i ^ 1 << apart) for i in range(lax.axis_size(axis))])


def from_behind(shard, axis, by):
    size = lax.axis_size(axis)
    return lax.ppermute(shard, axis, [(i, (i + by) % size) for i in range(size)])


def rounded(value):
    return lax.optimization_barrier(value.astype(jnp.bfloat16))


def depthwise_conv(widened, tap_weights, row_count):
    tap_count = tap_weights.shape[0]

    def add_tap(tap_index, running):
        window = lax.dynamic_slice_in_dim(widened, tap_count - 1 - tap_index, row_count, 0)
        return running + tap_weights[tap_index] * window.astype(jnp.float32)

    return lax.fori_loop(
        0, tap_count, add_tap, jnp.zeros((row_count, widened.shape[1]), jnp.float32)
    )


def long_kernel_rows(residue_mine, rate_mine, length):
    positions = jnp.arange(length, dtype=jnp.int32).astype(jnp.float32)
    mode_total = rate_mine.shape[0]

    def add_mode(mode_index, running):
        decay_rate = rate_mine[mode_index]
        mode_weight = (
            residue_mine[mode_index]
            * jnp.sqrt(-jnp.expm1(-2.0 * decay_rate))
            / math.sqrt(mode_total)
        )
        return running + mode_weight[:, None] * jnp.exp(-decay_rate[:, None] * positions[None, :])

    return lax.fori_loop(
        0, mode_total, add_mode, jnp.zeros((rate_mine.shape[1], length), jnp.float32)
    )


def dft_tables(row_size, column_size, period_size):
    row_index = lax.broadcasted_iota(jnp.int32, (row_size, column_size), 0)
    column_index = lax.broadcasted_iota(jnp.int32, (row_size, column_size), 1)
    angles = (row_index * column_index % period_size).astype(jnp.float32) * (
        2.0 * math.pi / period_size
    )
    return (jnp.cos(angles), jnp.sin(angles))


def forward_dft(signal, outer_size, inner_size):
    highest = lax.Precision.HIGHEST
    cos_outer, sin_outer = dft_tables(outer_size // 2, outer_size, outer_size)
    twiddle_cos, twiddle_sin = dft_tables(outer_size, inner_size, outer_size * inner_size)
    cos_inner, sin_inner = dft_tables(inner_size, inner_size, inner_size)
    step_real = jnp.einsum("pab,ak->pkb", signal, cos_outer, precision=highest)
    step_imag = -jnp.einsum("pab,ak->pkb", signal, sin_outer, precision=highest)
    turned_real = step_real * twiddle_cos + step_imag * twiddle_sin
    turned_imag = step_imag * twiddle_cos - step_real * twiddle_sin
    spec_real = jnp.einsum("pkb,bm->pkm", turned_real, cos_inner, precision=highest) + jnp.einsum(
        "pkb,bm->pkm", turned_imag, sin_inner, precision=highest
    )
    spec_imag = jnp.einsum("pkb,bm->pkm", turned_imag, cos_inner, precision=highest) - jnp.einsum(
        "pkb,bm->pkm", turned_real, sin_inner, precision=highest
    )
    return (spec_real, spec_imag)


def inverse_dft(spec_real, spec_imag, outer_size, inner_size):
    highest = lax.Precision.HIGHEST
    cos_outer, sin_outer = dft_tables(outer_size // 2, outer_size, outer_size)
    twiddle_cos, twiddle_sin = dft_tables(outer_size, inner_size, outer_size * inner_size)
    cos_inner, sin_inner = dft_tables(inner_size, inner_size, inner_size)
    back_real = jnp.einsum("pkm,mb->pkb", spec_real, cos_inner, precision=highest) - jnp.einsum(
        "pkm,mb->pkb", spec_imag, sin_inner, precision=highest
    )
    back_imag = jnp.einsum("pkm,mb->pkb", spec_real, sin_inner, precision=highest) + jnp.einsum(
        "pkm,mb->pkb", spec_imag, cos_inner, precision=highest
    )
    turned_real = back_real * twiddle_cos - back_imag * twiddle_sin
    turned_imag = back_real * twiddle_sin + back_imag * twiddle_cos
    signal = jnp.einsum("pkb,ak->pab", turned_real, cos_outer, precision=highest) - jnp.einsum(
        "pkb,ak->pab", turned_imag, sin_outer, precision=highest
    )
    return signal / (outer_size * inner_size)


def attend_block(query_rows, query_index, key_block, value_block, key_start, running, score_scale):
    row_peak, row_total, blended = running
    scores = (
        jnp.einsum("qhd,khd->hqk", query_rows, key_block, preferred_element_type=jnp.float32)
        * score_scale
    )
    key_index = key_start + jnp.arange(key_block.shape[0], dtype=jnp.int32)
    scores = jnp.where(key_index[None, None, :] <= query_index[None, :, None], scores, -1e30)
    new_peak = jnp.maximum(row_peak, jnp.max(scores, axis=2))
    weights = jnp.exp(scores - new_peak[:, :, None])
    rescale = jnp.exp(row_peak - new_peak)
    row_total = row_total * rescale + jnp.sum(weights, axis=2)
    blended = blended * rescale[:, :, None] + jnp.einsum(
        "hqk,khd->hqd",
        weights.astype(jnp.bfloat16),
        value_block,
        preferred_element_type=jnp.float32,
    )
    return (new_peak, row_total, blended)


def merge_partials(first_part, second_part):
    peak_one, total_one, blend_one = first_part
    peak_two, total_two, blend_two = second_part
    new_peak = jnp.maximum(peak_one, peak_two)
    scale_one = jnp.exp(peak_one - new_peak)
    scale_two = jnp.exp(peak_two - new_peak)
    new_total = total_one * scale_one + total_two * scale_two
    new_blend = blend_one * scale_one[..., None] + blend_two * scale_two[..., None]
    return (new_peak, new_total, new_blend)


def split_halves(stacked_part, half_size, upper_side):
    lower_half = stacked_part[:, :half_size]
    upper_half = stacked_part[:, half_size:]
    keep_half = jnp.where(upper_side == 1, upper_half, lower_half)
    send_half = jnp.where(upper_side == 1, lower_half, upper_half)
    return (keep_half, send_half)


def by_position(
    token_ids, embedding, short_filter, medium_filter, long_residue, long_rate, query_gain, key_gain
):
    tok_count = token_ids.shape[0]
    vocab_size = embedding.shape[0]
    width_dev = embedding.shape[1]
    seq_count = lax.axis_size("seq")
    seq_index = lax.axis_index("seq")
    one_hot = (
        token_ids[:, None] == lax.broadcasted_iota(jnp.int32, (tok_count, vocab_size), 1)
    ).astype(jnp.bfloat16)
    embedded = jnp.dot(one_hot, embedding, preferred_element_type=jnp.float32).astype(jnp.bfloat16)
    short_taps = short_filter.shape[0]
    rim_rows = shifted(embedded[tok_count - (short_taps - 1) :], "seq", 1)
    widened = jnp.concatenate([rim_rows, embedded], axis=0)
    short_part = depthwise_conv(widened, short_filter, tok_count)
    short_gated = rounded(embedded.astype(jnp.float32) * short_part)
    medium_taps = medium_filter.shape[0]
    upper_rows = shifted(short_gated[tok_count - (medium_taps - 1) :], "seq", 1)
    widened_two = jnp.concatenate([upper_rows, short_gated], axis=0)
    medium_part = depthwise_conv(widened_two, medium_filter, tok_count)
    medium_gated = rounded(short_gated.astype(jnp.float32) * medium_part)
    per_dev = width_dev // seq_count
    length = tok_count * seq_count
    grouped = medium_gated.T.reshape(seq_count, per_dev, tok_count)
    spread = lax.all_to_all(grouped, "seq", split_axis=0, concat_axis=2, tiled=True).reshape(
        per_dev, length
    )
    rate_mine = lax.dynamic_slice_in_dim(long_rate, seq_index * per_dev, per_dev, 1)
    residue_mine = lax.dynamic_slice_in_dim(long_residue, seq_index * per_dev, per_dev, 1)
    kernel = long_kernel_rows(residue_mine, rate_mine, length)
    outer_size = 128
    inner_size = 2 * length // outer_size
    spread_float = spread.astype(jnp.float32)
    data_real, data_imag = forward_dft(
        spread_float.reshape(per_dev, outer_size // 2, inner_size), outer_size, inner_size
    )
    kernel_real, kernel_imag = forward_dft(
        kernel.reshape(per_dev, outer_size // 2, inner_size), outer_size, inner_size
    )
    product_real = data_real * kernel_real - data_imag * kernel_imag
    product_imag = data_real * kernel_imag + data_imag * kernel_real
    long_part = inverse_dft(product_real, product_imag, outer_size, inner_size).reshape(
        per_dev, length
    )
    channel_out = (spread_float * long_part).astype(jnp.bfloat16)
    returned = lax.all_to_all(channel_out[None], "seq", split_axis=2, concat_axis=0, tiled=True)
    hyena_out = returned.reshape(width_dev, tok_count).T
    head_count = width_dev // HEAD
    hyena_float = hyena_out.astype(jnp.float32)
    square_sums = jnp.sum(hyena_float * hyena_float, axis=1)
    total_sums = lax.psum(square_sums, "ch")
    inverse_scale = lax.rsqrt(total_sums / C + 1e-05)
    normed = hyena_float * inverse_scale[:, None]
    values = normed.astype(jnp.bfloat16).reshape(tok_count, head_count, HEAD)
    queries = (
        (normed * query_gain[None, :]).astype(jnp.bfloat16).reshape(tok_count, head_count, HEAD)
    )
    key_rows = (
        (normed * key_gain[None, :]).astype(jnp.bfloat16).reshape(tok_count, head_count, HEAD)
    )
    group_size = 2
    level_count = group_size.bit_length() - 1
    seq_bits = seq_count.bit_length() - 1
    base_bit = seq_bits - level_count
    stride = seq_count // group_size
    stacked = queries[None]
    level = 0
    bit_number = base_bit + level
    partner_rows = swapped(stacked, "seq", bit_number)
    upper_side = seq_index >> bit_number & 1
    stacked = jnp.where(
        upper_side == 1,
        jnp.concatenate([partner_rows, stacked], axis=0),
        jnp.concatenate([stacked, partner_rows], axis=0),
    )
    query_rows = stacked.reshape(group_size * tok_count, head_count, HEAD)
    group_first = seq_index % stride
    block_numbers = group_first + stride * jnp.arange(group_size, dtype=jnp.int32)
    query_index = (
        block_numbers[:, None] * tok_count + jnp.arange(tok_count, dtype=jnp.int32)[None, :]
    ).reshape(group_size * tok_count)
    score_scale = HEAD ** (-0.5)
    partial_state = (
        jnp.full((head_count, group_size * tok_count), -1e30, jnp.float32),
        jnp.zeros((head_count, group_size * tok_count), jnp.float32),
        jnp.zeros((head_count, group_size * tok_count, HEAD), jnp.float32),
    )

    def cycle_step(turn_number, carried):
        key_block, value_block, running = carried
        key_block, value_block = from_behind((key_block, value_block), "seq", -1)
        source_block = jnp.remainder(seq_index + turn_number, seq_count)
        running = attend_block(
            query_rows,
            query_index,
            key_block,
            value_block,
            source_block * tok_count,
            running,
            score_scale,
        )
        return (key_block, value_block, running)

    carried = lax.fori_loop(1, stride + 1, cycle_step, (key_rows, values, partial_state))
    row_peak, row_total, blended = carried[2]
    row_peak = row_peak.reshape(head_count, group_size, tok_count)
    row_total = row_total.reshape(head_count, group_size, tok_count)
    blended = blended.reshape(head_count, group_size, tok_count, HEAD)
    for level in reversed(range(level_count)):
        bit_number = base_bit + level
        half_size = row_peak.shape[1] // 2
        upper_side = seq_index >> bit_number & 1
        keep_peak, send_peak = split_halves(row_peak, half_size, upper_side)
        keep_total, send_total = split_halves(row_total, half_size, upper_side)
        keep_blend, send_blend = split_halves(blended, half_size, upper_side)
        got_peak, got_total, got_blend = swapped(
            (send_peak, send_total, send_blend), "seq", bit_number
        )
        row_peak, row_total, blended = merge_partials(
            (keep_peak, keep_total, keep_blend), (got_peak, got_total, got_blend)
        )
    normalized = blended[:, 0] / row_total[:, 0][:, :, None]
    attended = normalized.transpose(1, 0, 2).reshape(tok_count, width_dev).astype(jnp.bfloat16)
    return (hyena_out, attended)


def transform_tables(block):
    size = 2 * block
    step = 2.0 * np.pi / size
    freq = (np.arange(block) + 0.5)[:, None]
    angle = freq * np.arange(size)[None, :] * step
    forward = np.concatenate([np.cos(angle), -np.sin(angle)], axis=0)
    angle = (np.arange(block)[:, None] + block) * freq.T * step
    backward = np.concatenate([np.cos(angle), -np.sin(angle)], axis=1) * (2.0 / size)

    def parts(table):
        kept = []
        for _ in range(3):
            kept.append(table.astype(np.float32).astype(ml_dtypes.bfloat16))
            table = table - kept[-1].astype(np.float64)
        return np.concatenate(kept, axis=0)

    forward, backward = parts(forward), parts(backward)
    first, second, third = np.split(forward[:, :block], 3)
    taps = np.concatenate([np.concatenate([first, second], axis=1), np.concatenate([first, third], axis=1)], axis=0)
    forward = np.concatenate(np.split(forward, 3), axis=1)
    first, second, third = np.split(backward, 3)
    backward = np.concatenate([first, second, first, third, second, first], axis=1)
    return forward, backward, taps


def split_pair(value):
    upper = value.astype(jnp.bfloat16)
    return upper, (value - upper.astype(jnp.float32)).astype(jnp.bfloat16)


def split_three(value):
    upper = value.astype(jnp.bfloat16)
    rest = value - upper.astype(jnp.float32)
    middle = rest.astype(jnp.bfloat16)
    return upper, middle, (rest - middle.astype(jnp.float32)).astype(jnp.bfloat16)


def minus_expm1(value):
    term = value
    series = value
    for order in range(2, 11):
        term = term * value * (-1.0 / order)
        series = series + term
    return jnp.where(value < 0.5, series, 1.0 - jnp.exp(-value))


def dot32(left, right):
    return jnp.dot(left, right, preferred_element_type=jnp.float32)


def own_lanes(width):
    return pl.ds(pl.multiple_of(lax.axis_index("seq") * width, width), width)


def fetch_kernel(
    token_ids, residue, rate, medium, table, ids_out, residue_out, rate_out, medium_out, table_out, sems
):
    lanes = own_lanes(medium_out.shape[1])
    copies = [
        pltpu.make_async_copy(source, target, sems.at[i])
        for i, (source, target) in enumerate(
            [
                (token_ids, ids_out),
                (residue.at[:, lanes], residue_out),
                (rate.at[:, lanes], rate_out),
                (medium.at[:, lanes], medium_out),
                (table, table_out),
            ]
        )
    ]
    for copy in copies:
        copy.start()
    for copy in copies:
        copy.wait()


def response_kernel(residue, rate, medium, table, medium_out, long_out):
    block, width = medium.shape
    size = 2 * block
    mode_total = rate.shape[0]
    block_total = long_out.shape[1] // width

    def transformed(signal):
        up, middle, low = split_three(signal)
        return (
            dot32(table[0:size, :], jnp.concatenate([up, up], axis=0))
            + dot32(table[0:size, :], jnp.concatenate([middle, middle], axis=0))
            + dot32(table[size : 2 * size, :], jnp.concatenate([low, up], axis=0))
        )

    medium_out[...] = transformed(medium[...])
    decays = rate[...]
    weights = residue[...] * jnp.sqrt(minus_expm1(2.0 * decays)) / math.sqrt(mode_total)
    modes = [weights * jnp.exp(-decays * float(part * block)) for part in range(block_total)]
    place = lax.broadcasted_iota(jnp.int32, (block, width), 0).astype(jnp.float32)
    rows = 32
    tiles = []
    for first in range(0, block, rows):
        sums = [jnp.zeros((rows, width), jnp.float32) for _ in range(block_total)]
        for mode in range(mode_total):
            shape = jnp.exp(-decays[mode : mode + 1, :] * place[first : first + rows])
            for part in range(block_total):
                sums[part] = sums[part] + modes[part][mode : mode + 1, :] * shape
        tiles.append(jnp.concatenate(sums, axis=1))
    long_out[...] = transformed(jnp.concatenate(tiles, axis=0))


def conv_kernel(*refs, piece_count):
    pieces = refs[:piece_count]
    (embedding, short, medium_resp, long_resp, forward, backward, hyena, sums) = refs[piece_count : piece_count + 8]
    ids, ordered, padded, row_sums, copied_sums, sem = refs[piece_count + 8 :]
    width = padded.shape[1]
    block = width
    size = 2 * block
    length = hyena.shape[0]
    count = length // block
    pair = count
    me = lax.axis_index("seq")
    for i, piece in enumerate(pieces):
        ids[2 * i : 2 * i + 2, :] = piece[...]
    for b in range(count):
        ordered[b : b + 1, :] = ids[pl.ds(lax.bitwise_xor(me, b), 1), :]
    across = jnp.transpose(ordered[...].astype(jnp.float32), (1, 0)).astype(jnp.int32)
    padded[0:8, :] = jnp.zeros((8, width), jnp.float32)
    table = embedding[:, own_lanes(width)]
    short_taps = short[:, own_lanes(width)]
    vocab = table.shape[0]
    entries = lax.broadcasted_iota(jnp.int32, (block, vocab), 1)
    rows = 16

    def embed(chunk):
        for b in range(chunk * pair, (chunk + 1) * pair):
            chosen = jnp.where(across[:, b : b + 1] == entries, 1.0, 0.0).astype(jnp.bfloat16)
            padded[8 + b * block : 8 + (b + 1) * block, :] = dot32(chosen, table)

    nothing = jnp.zeros((block, width), jnp.bfloat16)
    gated = [{-1: nothing}, {-1: nothing}]
    spectra, products = [{}, {}], [{}, {}]

    def short_gate(chunk):
        for b in range(chunk * pair, (chunk + 1) * pair):
            running = jnp.zeros((block, width), jnp.float32)
            for j in range(short_taps.shape[0]):
                running = running + short_taps[j : j + 1, :] * padded[8 + b * block - j : 8 + (b + 1) * block - j, :]
            signal = padded[8 + b * block : 8 + (b + 1) * block, :] * running
            gated[0][b] = signal.astype(jnp.bfloat16)

    def analyse(turn, chunk):
        span = range(chunk * pair, (chunk + 1) * pair)
        signal = jnp.concatenate(
            [jnp.concatenate([gated[turn][b - 1] for b in span], axis=1)]
            + [jnp.concatenate([gated[turn][b] for b in span], axis=1)],
            axis=0,
        )
        spectrum = dot32(forward[...], jnp.concatenate([signal] * 3, axis=0))
        for i, b in enumerate(span):
            spectra[turn][b] = spectrum[:, i * width : (i + 1) * width]

    def multiply(turn, response, chunk):
        span = range(chunk * pair, (chunk + 1) * pair)
        sources = range(span[-1] + 1) if turn else span
        tiles = {b: ([], []) for b in span}
        for first in range(0, block, rows):
            sums = {b: ([], []) for b in span}
            for upper in [slice(i, i + 8) for i in range(first, first + rows, 8)]:
                lower = slice(block + upper.start, block + upper.stop)
                data = {b: (spectra[turn][b][upper], spectra[turn][b][lower]) for b in sources}
                filt = [
                    (response[upper, i * width : (i + 1) * width], response[lower, i * width : (i + 1) * width])
                    for i in range(span[-1] + 1 if turn else 1)
                ]
                for b in span:
                    total_real, total_imag = 0.0, 0.0
                    for part in range(b + 1 if turn else 1):
                        (real, imag), (filt_real, filt_imag) = data[b - part], filt[part]
                        total_real = total_real + (real * filt_real - imag * filt_imag)
                        total_imag = total_imag + (real * filt_imag + imag * filt_real)
                    sums[b][0].append(total_real)
                    sums[b][1].append(total_imag)
            for b in span:
                for side in range(2):
                    tiles[b][side].append(split_three(jnp.concatenate(sums[b][side], axis=0)))
        columns = [
            [jnp.concatenate([tile[i] for tile in tiles[b][0] + tiles[b][1]], axis=0) for i in range(3)] for b in span
        ]
        products[turn][chunk] = [jnp.concatenate([column[i] for column in columns], axis=1) for i in range(3)]

    def synthesise(turn, chunk):
        up, middle, low = products[turn].pop(chunk)
        return dot32(backward[...], jnp.concatenate([up, up, middle, up, middle, low], axis=0))

    def gate(turn, chunk):
        out = synthesise(turn, chunk)
        results = []
        for i in range(pair):
            past = gated[turn][chunk * pair + i].astype(jnp.float32)
            results.append((past * out[:, i * width : (i + 1) * width]).astype(jnp.bfloat16))
        return results

    def medium_gate(chunk):
        for i, signal in enumerate(gate(0, chunk)):
            gated[1][chunk * pair + i] = signal

    ones = jnp.ones((size, width), jnp.bfloat16)
    diagonal = lax.broadcasted_iota(jnp.int32, (block, block), 0) == lax.broadcasted_iota(
        jnp.int32, (block, block), 1
    )

    def long_gate(chunk):
        for i, result in enumerate(gate(1, chunk)):
            b = chunk * pair + i
            hyena[b * block : (b + 1) * block, :] = result
            wide = result.astype(jnp.float32)
            spread = dot32(jnp.concatenate(split_pair(wide * wide), axis=1), ones)
            row_sums[b : b + 1, :] = jnp.sum(jnp.where(diagonal, spread, 0.0), axis=0, keepdims=True)

    stages = [
        embed,
        short_gate,
        functools.partial(analyse, 0),
        functools.partial(multiply, 0, medium_resp),
        medium_gate,
        functools.partial(analyse, 1),
        functools.partial(multiply, 1, long_resp),
        long_gate,
    ]
    chunks = count // pair
    for turn in range(chunks + len(stages) - 1):
        for stage in range(len(stages)):
            if 0 <= turn - stage < chunks:
                stages[stage](turn - stage)
    copied_sums[...] = jnp.broadcast_to(row_sums[...][None], copied_sums.shape)
    copy = pltpu.make_async_copy(copied_sums, sums, sem)
    copy.start()
    copy.wait()


def attend_kernel(own, other, sums, query_gain, key_gain, out, queries, keys, values, *, channel_count):
    length, width = own.shape
    count = sums.shape[1]
    block = length // count
    me = lax.axis_index("seq")
    core = lax.rem(me, 2)
    total = jnp.sum(sums[...], axis=0)
    inverse = lax.rsqrt(total / channel_count + 1e-05)
    inverse = jnp.transpose(inverse, (1, 0))
    signals = (own, other)
    gains = []
    for side in range(2):
        lanes = pl.ds(pl.multiple_of(lax.bitwise_xor(me, side) * width, width), width)
        gains.append((query_gain[0:1, lanes], key_gain[0:1, lanes]))

    def normalise(b):
        spans = slice(b * block, (b + 1) * block)
        scale = jnp.broadcast_to(inverse[:, b : b + 1], (block, width))
        for side, signal in enumerate(signals):
            normed = signal[spans, :].astype(jnp.float32) * scale
            values[side, spans, :] = normed.astype(jnp.bfloat16)
            keys[side, spans, :] = (normed * gains[side][1]).astype(jnp.bfloat16)
            queries[side, spans, :] = (normed * gains[side][0]).astype(jnp.bfloat16)

    row_index = lax.broadcasted_iota(jnp.int32, (block, 2 * block), 0) + core * block
    allowed = lax.broadcasted_iota(jnp.int32, (block, 2 * block), 1) <= row_index

    def score(chip, side):
        reach = (chip + 1) * 2 * block
        start = pl.multiple_of((2 * chip + core) * block, block)
        scores = lax.dot_general(
            queries[side, pl.ds(start, block), :],
            keys[side, 0:reach, :],
            (((1,), (1,)), ((), ())),
            preferred_element_type=jnp.float32,
        )
        last = jnp.where(allowed, scores[:, reach - 2 * block :], -1e30)
        return jnp.concatenate([scores[:, : reach - 2 * block], last], axis=1) if chip else last

    def weigh(scores):
        peak = jnp.max(scores, axis=1, keepdims=True)
        weights = jnp.exp2((scores - peak) * (width**-0.5 * math.log2(math.e)))
        return weights.astype(jnp.bfloat16), jnp.sum(weights, axis=1, keepdims=True)

    def blend(chip, side, weights, row_total):
        reach = (chip + 1) * 2 * block
        place = lax.bitwise_xor(me // 2, chip)
        half = lax.bitwise_xor(core, side)
        blended = dot32(weights, values[side, 0:reach, :])
        lanes = pl.ds(pl.multiple_of(half * width, width), width)
        out[place, :, lanes] = (blended / row_total).astype(jnp.bfloat16)

    for b in range(count):
        normalise(b)
    chains = [(chip, side) for chip in range(count // 2) for side in range(2)]
    scored, weighed = {}, {}
    for turn in range(len(chains) + 2):
        if turn < len(chains):
            scored[turn] = score(*chains[turn])
        if 0 <= turn - 1 < len(chains):
            weighed[turn - 1] = weigh(scored.pop(turn - 1))
        if 0 <= turn - 2 < len(chains):
            blend(*chains[turn - 2], *weighed.pop(turn - 2))


def outgoing_kernel(own, other, out):
    width = own.shape[1]
    block = out.shape[1]
    me = lax.axis_index("seq")
    core = lax.rem(me, 2)
    for i in range(out.shape[0]):
        start = pl.multiple_of((2 * lax.bitwise_xor(me // 2, i) + core) * block, block)
        for side, signal in enumerate((own, other)):
            lanes = pl.ds(pl.multiple_of(lax.bitwise_xor(core, side) * width, width), width)
            out[i, :, lanes] = signal[pl.ds(start, block), :]


def hold_kernel(*refs):
    refs[-1][...] = refs[0][...]


def place_kernel(*refs, order):
    blocks, out = refs[:-1], refs[-1]
    span = blocks[0].shape[1]
    chip = lax.axis_index("seq") // 2
    for i, block in zip(order, blocks):
        out[:, pl.ds(pl.multiple_of(lax.bitwise_xor(chip, i) * span, span), span)] = block[...]


def by_head(
    token_ids, embedding, short_filter, medium_filter, long_residue, long_rate, query_gain, key_gain
):
    seq_count = lax.axis_size("seq")
    ch_count = lax.axis_size("ch")
    block = token_ids.shape[0]
    width_dev = embedding.shape[1]
    length = block * seq_count
    width = HEAD
    f32, bf16 = jnp.float32, jnp.bfloat16
    forward, backward, tap_table = transform_tables(block)
    whole = pl.BlockSpec(memory_space=pltpu.VMEM)
    params = pltpu.CompilerParams(vmem_limit_bytes=24 * 1024 * 1024)

    def exchange(value, apart):
        return lax.ppermute(value, "seq", [(i, i ^ apart) for i in range(seq_count)])

    mode_total = long_rate.shape[0]
    in_hbm = pl.BlockSpec(memory_space=pltpu.HBM)

    def fetched(value):
        return pltpu.with_memory_space_constraint(value, pltpu.HBM)

    partner_ids = exchange(token_ids, 1)
    operands = (token_ids, long_residue, long_rate, medium_filter, jnp.asarray(tap_table))
    own_ids, *filters = pl.pallas_call(
        fetch_kernel,
        out_shape=[
            jax.ShapeDtypeStruct((block,), jnp.int32),
            jax.ShapeDtypeStruct((mode_total, width), f32),
            jax.ShapeDtypeStruct((mode_total, width), f32),
            jax.ShapeDtypeStruct((block, width), f32),
            jax.ShapeDtypeStruct(tap_table.shape, bf16),
        ],
        in_specs=[in_hbm] * 5,
        out_specs=[whole] * 5,
        scratch_shapes=[pltpu.SemaphoreType.DMA((5,))],
        compiler_params=params,
        cost_estimate=pl.CostEstimate(flops=10**9, bytes_accessed=2 * 10**6, transcendentals=0),
        name="fetched_operands",
    )(*[fetched(value) for value in operands])
    chip_ids = jnp.stack([own_ids, partner_ids])
    pieces = [chip_ids] + [exchange(chip_ids, 2 * i) for i in range(1, seq_count // 2)]
    medium_resp, long_resp = pl.pallas_call(
        response_kernel,
        out_shape=[
            jax.ShapeDtypeStruct((2 * block, width), f32),
            jax.ShapeDtypeStruct((2 * block, length), f32),
        ],
        in_specs=[whole] * 4,
        out_specs=[whole] * 2,
        compiler_params=params,
        cost_estimate=pl.CostEstimate(flops=2 * 10**9, bytes_accessed=2 * 10**6, transcendentals=3 * 10**5),
        name="filter_responses",
    )(*filters)

    devices = seq_count * ch_count
    hyena, square_sums = pl.pallas_call(
        functools.partial(conv_kernel, piece_count=len(pieces)),
        out_shape=[
            jax.ShapeDtypeStruct((length, width), bf16),
            pltpu.HBM((devices, seq_count, block), f32),
        ],
        in_specs=[whole] * (len(pieces) + 6),
        out_specs=[whole, in_hbm],
        scratch_shapes=[
            pltpu.VMEM((seq_count, block), jnp.int32),
            pltpu.VMEM((seq_count, block), jnp.int32),
            pltpu.VMEM((8 + length, width), f32),
            pltpu.VMEM((seq_count, block), f32),
            pltpu.VMEM((devices, seq_count, block), f32),
            pltpu.SemaphoreType.DMA,
        ],
        compiler_params=params,
        cost_estimate=pl.CostEstimate(flops=2 * 10**9, bytes_accessed=2 * 10**6, transcendentals=0),
        name="gated_convolutions",
    )(*pieces, embedding, short_filter, medium_resp, long_resp, forward, backward)

    other = exchange(hyena, 1)
    all_sums = lax.all_to_all(square_sums, ("seq", "ch"), 0, 0, tiled=True)

    def placed(blocks, name, order):
        return pl.pallas_call(
            functools.partial(place_kernel, order=(0, *order)),
            out_shape=jax.ShapeDtypeStruct((block, width_dev), bf16),
            in_specs=[whole] * len(blocks),
            out_specs=whole,
            compiler_params=params,
            cost_estimate=pl.CostEstimate(flops=10**9, bytes_accessed=10**6, transcendentals=0),
            name=name,
        )(*blocks)

    def held(value, others):
        return pl.pallas_call(
            hold_kernel,
            out_shape=jax.ShapeDtypeStruct(value.shape, value.dtype),
            in_specs=[whole] + [pl.BlockSpec(memory_space=pl.ANY)] * len(others),
            out_specs=whole,
            compiler_params=params,
            name="held_block",
        )(value, *others)

    order = list(range(1, seq_count // 2))
    hyena_blocks = pl.pallas_call(
        outgoing_kernel,
        out_shape=jax.ShapeDtypeStruct((seq_count // 2, block, 2 * width), bf16),
        in_specs=[whole, whole],
        out_specs=whole,
        compiler_params=params,
        cost_estimate=pl.CostEstimate(flops=2 * 10**9, bytes_accessed=10**6, transcendentals=0),
        name="hyena_blocks",
    )(hyena, other)
    hyena_parts = [hyena_blocks[0]] + [exchange(hyena_blocks[i], 2 * i) for i in order]
    outgoing = pl.pallas_call(
        functools.partial(attend_kernel, channel_count=width_dev * ch_count),
        out_shape=jax.ShapeDtypeStruct((seq_count // 2, block, 2 * width), bf16),
        in_specs=[whole] * 5,
        out_specs=whole,
        scratch_shapes=[pltpu.VMEM((2, length, width), bf16)] * 3,
        compiler_params=params,
        cost_estimate=pl.CostEstimate(flops=2 * 10**9, bytes_accessed=10**6, transcendentals=10**6),
        name="attention",
    )(hyena, other, all_sums, query_gain.reshape(1, width_dev), key_gain.reshape(1, width_dev))
    last = held(outgoing[order[0]], hyena_parts[1:])
    parts = [outgoing[0]] + [exchange(outgoing[i], 2 * i) for i in order[:0:-1]] + [exchange(last, 2 * order[0])]
    return placed(hyena_parts, "placed_hyena", order), placed(parts, "placed_attended", order[::-1])


def on_device(*operands):
    seq_count = lax.axis_size("seq")
    token_ids, embedding, _, medium_filter = operands[:4]
    block = token_ids.shape[0]
    fits = (
        embedding.shape[1] == seq_count * HEAD
        and block == HEAD
        and medium_filter.shape[0] == block
        and seq_count % 8 == 0
        and seq_count & (seq_count - 1) == 0
    )
    return by_head(*operands) if fits else by_position(*operands)


def solution(mesh):
    in_specs = (
        P("seq"),
        P(None, "ch"),
        P(None, "ch"),
        P(None, "ch"),
        P(None, "ch"),
        P(None, "ch"),
        P("ch"),
        P("ch"),
    )
    out_specs = (P("seq", "ch"), P("seq", "ch"))
    return jax.shard_map(
        on_device, mesh=mesh, in_specs=in_specs, out_specs=out_specs, check_vma=False
    )
```

```python
import functools
import math

import jax
import jax.numpy as jnp
import ml_dtypes
import numpy as np
from jax import lax
from jax.experimental import pallas as pl
from jax.experimental.pallas import tpu as pltpu
from jax.sharding import PartitionSpec as P

C = 4096
HEAD = 128


def shifted(value, axis, steps):
    count = lax.axis_size(axis)
    leading, last = (max(0, -steps), min(count, count - steps))
    return lax.ppermute(value, axis, [(source, source + steps) for source in range(leading, last)])


def swapped(shard, axis, apart):
    return lax.ppermute(shard, axis, [(i, i ^ 1 << apart) for i in range(lax.axis_size(axis))])


def from_behind(shard, axis, by):
    size = lax.axis_size(axis)
    return lax.ppermute(shard, axis, [(i, (i + by) % size) for i in range(size)])


def rounded(value):
    return lax.optimization_barrier(value.astype(jnp.bfloat16))


def depthwise_conv(widened, tap_weights, row_count):
    tap_count = tap_weights.shape[0]

    def add_tap(tap_index, running):
        window = lax.dynamic_slice_in_dim(widened, tap_count - 1 - tap_index, row_count, 0)
        return running + tap_weights[tap_index] * window.astype(jnp.float32)

    return lax.fori_loop(
        0, tap_count, add_tap, jnp.zeros((row_count, widened.shape[1]), jnp.float32)
    )


def long_kernel_rows(residue_mine, rate_mine, length):
    positions = jnp.arange(length, dtype=jnp.int32).astype(jnp.float32)
    mode_total = rate_mine.shape[0]

    def add_mode(mode_index, running):
        decay_rate = rate_mine[mode_index]
        mode_weight = (
            residue_mine[mode_index]
            * jnp.sqrt(-jnp.expm1(-2.0 * decay_rate))
            / math.sqrt(mode_total)
        )
        return running + mode_weight[:, None] * jnp.exp(-decay_rate[:, None] * positions[None, :])

    return lax.fori_loop(
        0, mode_total, add_mode, jnp.zeros((rate_mine.shape[1], length), jnp.float32)
    )


def dft_tables(row_size, column_size, period_size):
    row_index = lax.broadcasted_iota(jnp.int32, (row_size, column_size), 0)
    column_index = lax.broadcasted_iota(jnp.int32, (row_size, column_size), 1)
    angles = (row_index * column_index % period_size).astype(jnp.float32) * (
        2.0 * math.pi / period_size
    )
    return (jnp.cos(angles), jnp.sin(angles))


def forward_dft(signal, outer_size, inner_size):
    highest = lax.Precision.HIGHEST
    cos_outer, sin_outer = dft_tables(outer_size // 2, outer_size, outer_size)
    twiddle_cos, twiddle_sin = dft_tables(outer_size, inner_size, outer_size * inner_size)
    cos_inner, sin_inner = dft_tables(inner_size, inner_size, inner_size)
    step_real = jnp.einsum("pab,ak->pkb", signal, cos_outer, precision=highest)
    step_imag = -jnp.einsum("pab,ak->pkb", signal, sin_outer, precision=highest)
    turned_real = step_real * twiddle_cos + step_imag * twiddle_sin
    turned_imag = step_imag * twiddle_cos - step_real * twiddle_sin
    spec_real = jnp.einsum("pkb,bm->pkm", turned_real, cos_inner, precision=highest) + jnp.einsum(
        "pkb,bm->pkm", turned_imag, sin_inner, precision=highest
    )
    spec_imag = jnp.einsum("pkb,bm->pkm", turned_imag, cos_inner, precision=highest) - jnp.einsum(
        "pkb,bm->pkm", turned_real, sin_inner, precision=highest
    )
    return (spec_real, spec_imag)


def inverse_dft(spec_real, spec_imag, outer_size, inner_size):
    highest = lax.Precision.HIGHEST
    cos_outer, sin_outer = dft_tables(outer_size // 2, outer_size, outer_size)
    twiddle_cos, twiddle_sin = dft_tables(outer_size, inner_size, outer_size * inner_size)
    cos_inner, sin_inner = dft_tables(inner_size, inner_size, inner_size)
    back_real = jnp.einsum("pkm,mb->pkb", spec_real, cos_inner, precision=highest) - jnp.einsum(
        "pkm,mb->pkb", spec_imag, sin_inner, precision=highest
    )
    back_imag = jnp.einsum("pkm,mb->pkb", spec_real, sin_inner, precision=highest) + jnp.einsum(
        "pkm,mb->pkb", spec_imag, cos_inner, precision=highest
    )
    turned_real = back_real * twiddle_cos - back_imag * twiddle_sin
    turned_imag = back_real * twiddle_sin + back_imag * twiddle_cos
    signal = jnp.einsum("pkb,ak->pab", turned_real, cos_outer, precision=highest) - jnp.einsum(
        "pkb,ak->pab", turned_imag, sin_outer, precision=highest
    )
    return signal / (outer_size * inner_size)


def attend_block(query_rows, query_index, key_block, value_block, key_start, running, score_scale):
    row_peak, row_total, blended = running
    scores = (
        jnp.einsum("qhd,khd->hqk", query_rows, key_block, preferred_element_type=jnp.float32)
        * score_scale
    )
    key_index = key_start + jnp.arange(key_block.shape[0], dtype=jnp.int32)
    scores = jnp.where(key_index[None, None, :] <= query_index[None, :, None], scores, -1e30)
    new_peak = jnp.maximum(row_peak, jnp.max(scores, axis=2))
    weights = jnp.exp(scores - new_peak[:, :, None])
    rescale = jnp.exp(row_peak - new_peak)
    row_total = row_total * rescale + jnp.sum(weights, axis=2)
    blended = blended * rescale[:, :, None] + jnp.einsum(
        "hqk,khd->hqd",
        weights.astype(jnp.bfloat16),
        value_block,
        preferred_element_type=jnp.float32,
    )
    return (new_peak, row_total, blended)


def merge_partials(first_part, second_part):
    peak_one, total_one, blend_one = first_part
    peak_two, total_two, blend_two = second_part
    new_peak = jnp.maximum(peak_one, peak_two)
    scale_one = jnp.exp(peak_one - new_peak)
    scale_two = jnp.exp(peak_two - new_peak)
    new_total = total_one * scale_one + total_two * scale_two
    new_blend = blend_one * scale_one[..., None] + blend_two * scale_two[..., None]
    return (new_peak, new_total, new_blend)


def split_halves(stacked_part, half_size, upper_side):
    lower_half = stacked_part[:, :half_size]
    upper_half = stacked_part[:, half_size:]
    keep_half = jnp.where(upper_side == 1, upper_half, lower_half)
    send_half = jnp.where(upper_side == 1, lower_half, upper_half)
    return (keep_half, send_half)


def by_position(
    token_ids, embedding, short_filter, medium_filter, long_residue, long_rate, query_gain, key_gain
):
    tok_count = token_ids.shape[0]
    vocab_size = embedding.shape[0]
    width_dev = embedding.shape[1]
    seq_count = lax.axis_size("seq")
    seq_index = lax.axis_index("seq")
    one_hot = (
        token_ids[:, None] == lax.broadcasted_iota(jnp.int32, (tok_count, vocab_size), 1)
    ).astype(jnp.bfloat16)
    embedded = jnp.dot(one_hot, embedding, preferred_element_type=jnp.float32).astype(jnp.bfloat16)
    short_taps = short_filter.shape[0]
    rim_rows = shifted(embedded[tok_count - (short_taps - 1) :], "seq", 1)
    widened = jnp.concatenate([rim_rows, embedded], axis=0)
    short_part = depthwise_conv(widened, short_filter, tok_count)
    short_gated = rounded(embedded.astype(jnp.float32) * short_part)
    medium_taps = medium_filter.shape[0]
    upper_rows = shifted(short_gated[tok_count - (medium_taps - 1) :], "seq", 1)
    widened_two = jnp.concatenate([upper_rows, short_gated], axis=0)
    medium_part = depthwise_conv(widened_two, medium_filter, tok_count)
    medium_gated = rounded(short_gated.astype(jnp.float32) * medium_part)
    per_dev = width_dev // seq_count
    length = tok_count * seq_count
    grouped = medium_gated.T.reshape(seq_count, per_dev, tok_count)
    spread = lax.all_to_all(grouped, "seq", split_axis=0, concat_axis=2, tiled=True).reshape(
        per_dev, length
    )
    rate_mine = lax.dynamic_slice_in_dim(long_rate, seq_index * per_dev, per_dev, 1)
    residue_mine = lax.dynamic_slice_in_dim(long_residue, seq_index * per_dev, per_dev, 1)
    kernel = long_kernel_rows(residue_mine, rate_mine, length)
    outer_size = 128
    inner_size = 2 * length // outer_size
    spread_float = spread.astype(jnp.float32)
    data_real, data_imag = forward_dft(
        spread_float.reshape(per_dev, outer_size // 2, inner_size), outer_size, inner_size
    )
    kernel_real, kernel_imag = forward_dft(
        kernel.reshape(per_dev, outer_size // 2, inner_size), outer_size, inner_size
    )
    product_real = data_real * kernel_real - data_imag * kernel_imag
    product_imag = data_real * kernel_imag + data_imag * kernel_real
    long_part = inverse_dft(product_real, product_imag, outer_size, inner_size).reshape(
        per_dev, length
    )
    channel_out = (spread_float * long_part).astype(jnp.bfloat16)
    returned = lax.all_to_all(channel_out[None], "seq", split_axis=2, concat_axis=0, tiled=True)
    hyena_out = returned.reshape(width_dev, tok_count).T
    head_count = width_dev // HEAD
    hyena_float = hyena_out.astype(jnp.float32)
    square_sums = jnp.sum(hyena_float * hyena_float, axis=1)
    total_sums = lax.psum(square_sums, "ch")
    inverse_scale = lax.rsqrt(total_sums / C + 1e-05)
    normed = hyena_float * inverse_scale[:, None]
    values = normed.astype(jnp.bfloat16).reshape(tok_count, head_count, HEAD)
    queries = (
        (normed * query_gain[None, :]).astype(jnp.bfloat16).reshape(tok_count, head_count, HEAD)
    )
    key_rows = (
        (normed * key_gain[None, :]).astype(jnp.bfloat16).reshape(tok_count, head_count, HEAD)
    )
    group_size = 2
    level_count = group_size.bit_length() - 1
    seq_bits = seq_count.bit_length() - 1
    base_bit = seq_bits - level_count
    stride = seq_count // group_size
    stacked = queries[None]
    level = 0
    bit_number = base_bit + level
    partner_rows = swapped(stacked, "seq", bit_number)
    upper_side = seq_index >> bit_number & 1
    stacked = jnp.where(
        upper_side == 1,
        jnp.concatenate([partner_rows, stacked], axis=0),
        jnp.concatenate([stacked, partner_rows], axis=0),
    )
    query_rows = stacked.reshape(group_size * tok_count, head_count, HEAD)
    group_first = seq_index % stride
    block_numbers = group_first + stride * jnp.arange(group_size, dtype=jnp.int32)
    query_index = (
        block_numbers[:, None] * tok_count + jnp.arange(tok_count, dtype=jnp.int32)[None, :]
    ).reshape(group_size * tok_count)
    score_scale = HEAD ** (-0.5)
    partial_state = (
        jnp.full((head_count, group_size * tok_count), -1e30, jnp.float32),
        jnp.zeros((head_count, group_size * tok_count), jnp.float32),
        jnp.zeros((head_count, group_size * tok_count, HEAD), jnp.float32),
    )

    def cycle_step(turn_number, carried):
        key_block, value_block, running = carried
        key_block, value_block = from_behind((key_block, value_block), "seq", -1)
        source_block = jnp.remainder(seq_index + turn_number, seq_count)
        running = attend_block(
            query_rows,
            query_index,
            key_block,
            value_block,
            source_block * tok_count,
            running,
            score_scale,
        )
        return (key_block, value_block, running)

    carried = lax.fori_loop(1, stride + 1, cycle_step, (key_rows, values, partial_state))
    row_peak, row_total, blended = carried[2]
    row_peak = row_peak.reshape(head_count, group_size, tok_count)
    row_total = row_total.reshape(head_count, group_size, tok_count)
    blended = blended.reshape(head_count, group_size, tok_count, HEAD)
    for level in reversed(range(level_count)):
        bit_number = base_bit + level
        half_size = row_peak.shape[1] // 2
        upper_side = seq_index >> bit_number & 1
        keep_peak, send_peak = split_halves(row_peak, half_size, upper_side)
        keep_total, send_total = split_halves(row_total, half_size, upper_side)
        keep_blend, send_blend = split_halves(blended, half_size, upper_side)
        got_peak, got_total, got_blend = swapped(
            (send_peak, send_total, send_blend), "seq", bit_number
        )
        row_peak, row_total, blended = merge_partials(
            (keep_peak, keep_total, keep_blend), (got_peak, got_total, got_blend)
        )
    normalized = blended[:, 0] / row_total[:, 0][:, :, None]
    attended = normalized.transpose(1, 0, 2).reshape(tok_count, width_dev).astype(jnp.bfloat16)
    return (hyena_out, attended)


def transform_tables(block):
    size = 2 * block
    step = 2.0 * np.pi / size
    freq = (np.arange(block) + 0.5)[:, None]
    angle = freq * np.arange(size)[None, :] * step
    forward = np.concatenate([np.cos(angle), -np.sin(angle)], axis=0)
    angle = (np.arange(block)[:, None] + block) * freq.T * step
    backward = np.concatenate([np.cos(angle), -np.sin(angle)], axis=1) * (2.0 / size)

    def parts(table):
        kept = []
        for _ in range(3):
            kept.append(table.astype(np.float32).astype(ml_dtypes.bfloat16))
            table = table - kept[-1].astype(np.float64)
        return np.concatenate(kept, axis=0)

    forward, backward = parts(forward), parts(backward)
    first, second, third = np.split(forward[:, :block], 3)
    taps = np.concatenate([np.concatenate([first, second], axis=1), np.concatenate([first, third], axis=1)], axis=0)
    forward = np.concatenate(np.split(forward, 3), axis=1)
    first, second, third = np.split(backward, 3)
    backward = np.concatenate([first, second, first, third, second, first], axis=1)
    return forward, backward, taps


def split_pair(value):
    upper = value.astype(jnp.bfloat16)
    return upper, (value - upper.astype(jnp.float32)).astype(jnp.bfloat16)


def split_three(value):
    upper = value.astype(jnp.bfloat16)
    rest = value - upper.astype(jnp.float32)
    middle = rest.astype(jnp.bfloat16)
    return upper, middle, (rest - middle.astype(jnp.float32)).astype(jnp.bfloat16)


def minus_expm1(value):
    term = value
    series = value
    for order in range(2, 11):
        term = term * value * (-1.0 / order)
        series = series + term
    return jnp.where(value < 0.5, series, 1.0 - jnp.exp(-value))


def dot32(left, right):
    return jnp.dot(left, right, preferred_element_type=jnp.float32)


def own_lanes(width):
    return pl.ds(pl.multiple_of(lax.axis_index("seq") * width, width), width)


def fetch_kernel(
    token_ids, residue, rate, medium, table, ids_out, residue_out, rate_out, medium_out, table_out, sems
):
    lanes = own_lanes(medium_out.shape[1])
    copies = [
        pltpu.make_async_copy(source, target, sems.at[i])
        for i, (source, target) in enumerate(
            [
                (token_ids, ids_out),
                (residue.at[:, lanes], residue_out),
                (rate.at[:, lanes], rate_out),
                (medium.at[:, lanes], medium_out),
                (table, table_out),
            ]
        )
    ]
    for copy in copies:
        copy.start()
    for copy in copies:
        copy.wait()


def response_kernel(residue, rate, medium, table, medium_out, long_out):
    block, width = medium.shape
    size = 2 * block
    mode_total = rate.shape[0]
    block_total = long_out.shape[1] // width

    def transformed(signal):
        up, middle, low = split_three(signal)
        return (
            dot32(table[0:size, :], jnp.concatenate([up, up], axis=0))
            + dot32(table[0:size, :], jnp.concatenate([middle, middle], axis=0))
            + dot32(table[size : 2 * size, :], jnp.concatenate([low, up], axis=0))
        )

    medium_out[...] = transformed(medium[...])
    decays = rate[...]
    weights = residue[...] * jnp.sqrt(minus_expm1(2.0 * decays)) / math.sqrt(mode_total)
    modes = [weights * jnp.exp(-decays * float(part * block)) for part in range(block_total)]
    place = lax.broadcasted_iota(jnp.int32, (block, width), 0).astype(jnp.float32)
    rows = 32
    tiles = []
    for first in range(0, block, rows):
        sums = [jnp.zeros((rows, width), jnp.float32) for _ in range(block_total)]
        for mode in range(mode_total):
            shape = jnp.exp(-decays[mode : mode + 1, :] * place[first : first + rows])
            for part in range(block_total):
                sums[part] = sums[part] + modes[part][mode : mode + 1, :] * shape
        tiles.append(jnp.concatenate(sums, axis=1))
    long_out[...] = transformed(jnp.concatenate(tiles, axis=0))


def conv_kernel(*refs, piece_count):
    pieces = refs[:piece_count]
    (embedding, short, medium_resp, long_resp, forward, backward, hyena, sums) = refs[piece_count : piece_count + 8]
    ids, ordered, padded, row_sums, copied_sums, sem = refs[piece_count + 8 :]
    width = padded.shape[1]
    block = width
    size = 2 * block
    length = hyena.shape[0]
    count = length // block
    pair = count
    me = lax.axis_index("seq")
    for i, piece in enumerate(pieces):
        ids[2 * i : 2 * i + 2, :] = piece[...]
    for b in range(count):
        ordered[b : b + 1, :] = ids[pl.ds(lax.bitwise_xor(me, b), 1), :]
    across = jnp.transpose(ordered[...].astype(jnp.float32), (1, 0)).astype(jnp.int32)
    padded[0:8, :] = jnp.zeros((8, width), jnp.float32)
    table = embedding[:, own_lanes(width)]
    short_taps = short[:, own_lanes(width)]
    vocab = table.shape[0]
    entries = lax.broadcasted_iota(jnp.int32, (block, vocab), 1)
    rows = 16

    def embed(chunk):
        for b in range(chunk * pair, (chunk + 1) * pair):
            chosen = jnp.where(across[:, b : b + 1] == entries, 1.0, 0.0).astype(jnp.bfloat16)
            padded[8 + b * block : 8 + (b + 1) * block, :] = dot32(chosen, table)

    nothing = jnp.zeros((block, width), jnp.bfloat16)
    gated = [{-1: nothing}, {-1: nothing}]
    spectra, products = [{}, {}], [{}, {}]

    def short_gate(chunk):
        for b in range(chunk * pair, (chunk + 1) * pair):
            running = jnp.zeros((block, width), jnp.float32)
            for j in range(short_taps.shape[0]):
                running = running + short_taps[j : j + 1, :] * padded[8 + b * block - j : 8 + (b + 1) * block - j, :]
            signal = padded[8 + b * block : 8 + (b + 1) * block, :] * running
            gated[0][b] = signal.astype(jnp.bfloat16)

    def analyse(turn, chunk):
        span = range(chunk * pair, (chunk + 1) * pair)
        signal = jnp.concatenate(
            [jnp.concatenate([gated[turn][b - 1] for b in span], axis=1)]
            + [jnp.concatenate([gated[turn][b] for b in span], axis=1)],
            axis=0,
        )
        spectrum = dot32(forward[...], jnp.concatenate([signal] * 3, axis=0))
        for i, b in enumerate(span):
            spectra[turn][b] = spectrum[:, i * width : (i + 1) * width]

    def multiply(turn, response, chunk):
        span = range(chunk * pair, (chunk + 1) * pair)
        sources = range(span[-1] + 1) if turn else span
        tiles = {b: ([], []) for b in span}
        for first in range(0, block, rows):
            sums = {b: ([], []) for b in span}
            for upper in [slice(i, i + 8) for i in range(first, first + rows, 8)]:
                lower = slice(block + upper.start, block + upper.stop)
                data = {b: (spectra[turn][b][upper], spectra[turn][b][lower]) for b in sources}
                filt = [
                    (response[upper, i * width : (i + 1) * width], response[lower, i * width : (i + 1) * width])
                    for i in range(span[-1] + 1 if turn else 1)
                ]
                data = {b: (real, imag, real + imag) for b, (real, imag) in data.items()}
                filt = [(real, imag - real, real + imag) for real, imag in filt]
                for b in span:
                    shared = to_real = to_imag = 0.0
                    for part in range(b + 1 if turn else 1):
                        (real, imag, both), (base, ahead, total) = data[b - part], filt[part]
                        shared = shared + both * base
                        to_imag = to_imag + real * ahead
                        to_real = to_real + imag * total
                    total_real, total_imag = shared - to_real, shared + to_imag
                    sums[b][0].append(total_real)
                    sums[b][1].append(total_imag)
            for b in span:
                for side in range(2):
                    tiles[b][side].append(split_three(jnp.concatenate(sums[b][side], axis=0)))
        columns = [
            [jnp.concatenate([tile[i] for tile in tiles[b][0] + tiles[b][1]], axis=0) for i in range(3)] for b in span
        ]
        products[turn][chunk] = [jnp.concatenate([column[i] for column in columns], axis=1) for i in range(3)]

    def synthesise(turn, chunk):
        up, middle, low = products[turn].pop(chunk)
        return dot32(backward[...], jnp.concatenate([up, up, middle, up, middle, low], axis=0))

    def gate(turn, chunk):
        out = synthesise(turn, chunk)
        results = []
        for i in range(pair):
            past = gated[turn][chunk * pair + i].astype(jnp.float32)
            results.append((past * out[:, i * width : (i + 1) * width]).astype(jnp.bfloat16))
        return results

    def medium_gate(chunk):
        for i, signal in enumerate(gate(0, chunk)):
            gated[1][chunk * pair + i] = signal

    ones = jnp.ones((size, width), jnp.bfloat16)
    diagonal = lax.broadcasted_iota(jnp.int32, (block, block), 0) == lax.broadcasted_iota(
        jnp.int32, (block, block), 1
    )

    def long_gate(chunk):
        for i, result in enumerate(gate(1, chunk)):
            b = chunk * pair + i
            hyena[b * block : (b + 1) * block, :] = result
            wide = result.astype(jnp.float32)
            spread = dot32(jnp.concatenate(split_pair(wide * wide), axis=1), ones)
            row_sums[b : b + 1, :] = jnp.sum(jnp.where(diagonal, spread, 0.0), axis=0, keepdims=True)

    stages = [
        embed,
        short_gate,
        functools.partial(analyse, 0),
        functools.partial(multiply, 0, medium_resp),
        medium_gate,
        functools.partial(analyse, 1),
        functools.partial(multiply, 1, long_resp),
        long_gate,
    ]
    chunks = count // pair
    for turn in range(chunks + len(stages) - 1):
        for stage in range(len(stages)):
            if 0 <= turn - stage < chunks:
                stages[stage](turn - stage)
    copied_sums[...] = jnp.broadcast_to(row_sums[...][None], copied_sums.shape)
    copy = pltpu.make_async_copy(copied_sums, sums, sem)
    copy.start()
    copy.wait()


def attend_kernel(own, other, sums, query_gain, key_gain, out, queries, keys, values, *, channel_count):
    length, width = own.shape
    count = sums.shape[1]
    block = length // count
    me = lax.axis_index("seq")
    core = lax.rem(me, 2)
    total = jnp.sum(sums[...], axis=0)
    inverse = lax.rsqrt(total / channel_count + 1e-05)
    inverse = jnp.transpose(inverse, (1, 0))
    signals = (own, other)
    gains = []
    for side in range(2):
        lanes = pl.ds(pl.multiple_of(lax.bitwise_xor(me, side) * width, width), width)
        gains.append((query_gain[0:1, lanes], key_gain[0:1, lanes]))

    def normalise(b):
        spans = slice(b * block, (b + 1) * block)
        scale = jnp.broadcast_to(inverse[:, b : b + 1], (block, width))
        for side, signal in enumerate(signals):
            normed = signal[spans, :].astype(jnp.float32) * scale
            values[side, spans, :] = normed.astype(jnp.bfloat16)
            keys[side, spans, :] = (normed * gains[side][1]).astype(jnp.bfloat16)
            queries[side, spans, :] = (normed * gains[side][0]).astype(jnp.bfloat16)

    row_index = lax.broadcasted_iota(jnp.int32, (block, 2 * block), 0) + core * block
    allowed = lax.broadcasted_iota(jnp.int32, (block, 2 * block), 1) <= row_index

    def score(chip, side):
        reach = (chip + 1) * 2 * block
        start = pl.multiple_of((2 * chip + core) * block, block)
        scores = lax.dot_general(
            queries[side, pl.ds(start, block), :],
            keys[side, 0:reach, :],
            (((1,), (1,)), ((), ())),
            preferred_element_type=jnp.float32,
        )
        last = jnp.where(allowed, scores[:, reach - 2 * block :], -1e30)
        return jnp.concatenate([scores[:, : reach - 2 * block], last], axis=1) if chip else last

    def weigh(scores):
        peak = jnp.max(scores, axis=1, keepdims=True)
        weights = jnp.exp2((scores - peak) * (width**-0.5 * math.log2(math.e)))
        return weights.astype(jnp.bfloat16), jnp.sum(weights, axis=1, keepdims=True)

    def blend(chip, side, weights, row_total):
        reach = (chip + 1) * 2 * block
        place = lax.bitwise_xor(me // 2, chip)
        half = lax.bitwise_xor(core, side)
        blended = dot32(weights, values[side, 0:reach, :])
        lanes = pl.ds(pl.multiple_of(half * width, width), width)
        out[place, :, lanes] = (blended / row_total).astype(jnp.bfloat16)

    for b in range(count):
        normalise(b)
    chains = [(chip, side) for chip in range(count // 2) for side in range(2)]
    scored, weighed = {}, {}
    for turn in range(len(chains) + 2):
        if turn < len(chains):
            scored[turn] = score(*chains[turn])
        if 0 <= turn - 1 < len(chains):
            weighed[turn - 1] = weigh(scored.pop(turn - 1))
        if 0 <= turn - 2 < len(chains):
            blend(*chains[turn - 2], *weighed.pop(turn - 2))


def outgoing_kernel(own, other, out):
    width = own.shape[1]
    block = out.shape[1]
    me = lax.axis_index("seq")
    core = lax.rem(me, 2)
    for i in range(out.shape[0]):
        start = pl.multiple_of((2 * lax.bitwise_xor(me // 2, i) + core) * block, block)
        for side, signal in enumerate((own, other)):
            lanes = pl.ds(pl.multiple_of(lax.bitwise_xor(core, side) * width, width), width)
            out[i, :, lanes] = signal[pl.ds(start, block), :]


def hold_kernel(*refs):
    refs[-1][...] = refs[0][...]


def place_part_kernel(*refs, order, extra):
    blocks, out, sems = refs[extra:-2], refs[-2], refs[-1]
    span = blocks[0].shape[1]
    chip = lax.axis_index("seq") // 2
    copies = []
    for n, (i, block) in enumerate(zip(order, blocks)):
        lanes = pl.ds(pl.multiple_of(lax.bitwise_xor(chip, i) * span, span), span)
        copies.append(pltpu.make_async_copy(block, out.at[:, lanes], sems.at[n]))
    for copy in copies:
        copy.start()
    for copy in copies:
        copy.wait()


def place_kernel(*refs, order):
    blocks, out = refs[:-1], refs[-1]
    span = blocks[0].shape[1]
    chip = lax.axis_index("seq") // 2
    for i, block in zip(order, blocks):
        out[:, pl.ds(pl.multiple_of(lax.bitwise_xor(chip, i) * span, span), span)] = block[...]


def by_head(
    token_ids, embedding, short_filter, medium_filter, long_residue, long_rate, query_gain, key_gain
):
    seq_count = lax.axis_size("seq")
    ch_count = lax.axis_size("ch")
    block = token_ids.shape[0]
    width_dev = embedding.shape[1]
    length = block * seq_count
    width = HEAD
    f32, bf16 = jnp.float32, jnp.bfloat16
    forward, backward, tap_table = transform_tables(block)
    whole = pl.BlockSpec(memory_space=pltpu.VMEM)
    params = pltpu.CompilerParams(vmem_limit_bytes=24 * 1024 * 1024)

    def exchange(value, apart):
        return lax.ppermute(value, "seq", [(i, i ^ apart) for i in range(seq_count)])

    mode_total = long_rate.shape[0]
    in_hbm = pl.BlockSpec(memory_space=pltpu.HBM)

    def fetched(value):
        return pltpu.with_memory_space_constraint(value, pltpu.HBM)

    partner_ids = exchange(token_ids, 1)
    operands = (token_ids, long_residue, long_rate, medium_filter, jnp.asarray(tap_table))
    own_ids, *filters = pl.pallas_call(
        fetch_kernel,
        out_shape=[
            jax.ShapeDtypeStruct((block,), jnp.int32),
            jax.ShapeDtypeStruct((mode_total, width), f32),
            jax.ShapeDtypeStruct((mode_total, width), f32),
            jax.ShapeDtypeStruct((block, width), f32),
            jax.ShapeDtypeStruct(tap_table.shape, bf16),
        ],
        in_specs=[in_hbm] * 5,
        out_specs=[whole] * 5,
        scratch_shapes=[pltpu.SemaphoreType.DMA((5,))],
        compiler_params=params,
        cost_estimate=pl.CostEstimate(flops=10**9, bytes_accessed=2 * 10**6, transcendentals=0),
        name="fetched_operands",
    )(*[fetched(value) for value in operands])
    chip_ids = jnp.stack([own_ids, partner_ids])
    pieces = [chip_ids] + [exchange(chip_ids, 2 * i) for i in range(1, seq_count // 2)]
    medium_resp, long_resp = pl.pallas_call(
        response_kernel,
        out_shape=[
            jax.ShapeDtypeStruct((2 * block, width), f32),
            jax.ShapeDtypeStruct((2 * block, length), f32),
        ],
        in_specs=[whole] * 4,
        out_specs=[whole] * 2,
        compiler_params=params,
        cost_estimate=pl.CostEstimate(flops=2 * 10**9, bytes_accessed=2 * 10**6, transcendentals=3 * 10**5),
        name="filter_responses",
    )(*filters)

    devices = seq_count * ch_count
    hyena, square_sums = pl.pallas_call(
        functools.partial(conv_kernel, piece_count=len(pieces)),
        out_shape=[
            jax.ShapeDtypeStruct((length, width), bf16),
            pltpu.HBM((devices, seq_count, block), f32),
        ],
        in_specs=[whole] * (len(pieces) + 6),
        out_specs=[whole, in_hbm],
        scratch_shapes=[
            pltpu.VMEM((seq_count, block), jnp.int32),
            pltpu.VMEM((seq_count, block), jnp.int32),
            pltpu.VMEM((8 + length, width), f32),
            pltpu.VMEM((seq_count, block), f32),
            pltpu.VMEM((devices, seq_count, block), f32),
            pltpu.SemaphoreType.DMA,
        ],
        compiler_params=params,
        cost_estimate=pl.CostEstimate(flops=2 * 10**9, bytes_accessed=2 * 10**6, transcendentals=0),
        name="gated_convolutions",
    )(*pieces, embedding, short_filter, medium_resp, long_resp, forward, backward)

    other = exchange(hyena, 1)
    all_sums = lax.all_to_all(square_sums, ("seq", "ch"), 0, 0, tiled=True)

    def placed(blocks, name, order):
        return pl.pallas_call(
            functools.partial(place_kernel, order=(0, *order)),
            out_shape=jax.ShapeDtypeStruct((block, width_dev), bf16),
            in_specs=[whole] * len(blocks),
            out_specs=whole,
            compiler_params=params,
            cost_estimate=pl.CostEstimate(flops=10**9, bytes_accessed=10**6, transcendentals=0),
            name=name,
        )(*blocks)

    def placed_part(blocks, name, order, so_far=()):
        return pl.pallas_call(
            functools.partial(place_part_kernel, order=order, extra=len(so_far)),
            out_shape=jax.ShapeDtypeStruct((block, width_dev), bf16),
            in_specs=[in_hbm] * len(so_far) + [whole] * len(blocks),
            out_specs=in_hbm,
            scratch_shapes=[pltpu.SemaphoreType.DMA((len(blocks),))],
            input_output_aliases={0: 0} if so_far else {},
            compiler_params=params,
            cost_estimate=pl.CostEstimate(flops=10**9, bytes_accessed=10**6, transcendentals=0),
            name=name,
        )(*so_far, *blocks)

    def held(value, others):
        return pl.pallas_call(
            hold_kernel,
            out_shape=jax.ShapeDtypeStruct(value.shape, value.dtype),
            in_specs=[whole] + [pl.BlockSpec(memory_space=pl.ANY)] * len(others),
            out_specs=whole,
            compiler_params=params,
            name="held_block",
        )(value, *others)

    order = list(range(1, seq_count // 2))
    hyena_blocks = pl.pallas_call(
        outgoing_kernel,
        out_shape=jax.ShapeDtypeStruct((seq_count // 2, block, 2 * width), bf16),
        in_specs=[whole, whole],
        out_specs=whole,
        compiler_params=params,
        cost_estimate=pl.CostEstimate(flops=2 * 10**9, bytes_accessed=10**6, transcendentals=0),
        name="hyena_blocks",
    )(hyena, other)
    hyena_parts = [hyena_blocks[0]] + [exchange(hyena_blocks[i], 2 * i) for i in order]
    outgoing = pl.pallas_call(
        functools.partial(attend_kernel, channel_count=width_dev * ch_count),
        out_shape=jax.ShapeDtypeStruct((seq_count // 2, block, 2 * width), bf16),
        in_specs=[whole] * 5,
        out_specs=whole,
        scratch_shapes=[pltpu.VMEM((2, length, width), bf16)] * 3,
        compiler_params=params,
        cost_estimate=pl.CostEstimate(flops=2 * 10**9, bytes_accessed=10**6, transcendentals=10**6),
        name="attention",
    )(hyena, other, all_sums, query_gain.reshape(1, width_dev), key_gain.reshape(1, width_dev))
    last = held(outgoing[order[0]], hyena_parts[1:])
    parts = [outgoing[0]] + [exchange(outgoing[i], 2 * i) for i in order[:0:-1]] + [exchange(last, 2 * order[0])]
    early = placed_part(parts[:-1], "placed_early", (0, *order[:0:-1]))
    attended = placed_part(parts[-1:], "placed_attended", order[:1], (early,))
    return placed(hyena_parts, "placed_hyena", order), attended


def on_device(*operands):
    seq_count = lax.axis_size("seq")
    token_ids, embedding, _, medium_filter = operands[:4]
    block = token_ids.shape[0]
    fits = (
        embedding.shape[1] == seq_count * HEAD
        and block == HEAD
        and medium_filter.shape[0] == block
        and seq_count % 8 == 0
        and seq_count & (seq_count - 1) == 0
    )
    return by_head(*operands) if fits else by_position(*operands)


def solution(mesh):
    in_specs = (
        P("seq"),
        P(None, "ch"),
        P(None, "ch"),
        P(None, "ch"),
        P(None, "ch"),
        P(None, "ch"),
        P("ch"),
        P("ch"),
    )
    out_specs = (P("seq", "ch"), P("seq", "ch"))
    return jax.shard_map(
        on_device, mesh=mesh, in_specs=in_specs, out_specs=out_specs, check_vma=False
    )
```

```python
import functools
import math

import jax
import jax.numpy as jnp
import ml_dtypes
import numpy as np
from jax import lax
from jax.experimental import pallas as pl
from jax.experimental.pallas import tpu as pltpu
from jax.sharding import PartitionSpec as P

C = 4096
HEAD = 128


def shifted(value, axis, steps):
    count = lax.axis_size(axis)
    leading, last = (max(0, -steps), min(count, count - steps))
    return lax.ppermute(value, axis, [(source, source + steps) for source in range(leading, last)])


def swapped(shard, axis, apart):
    return lax.ppermute(shard, axis, [(i, i ^ 1 << apart) for i in range(lax.axis_size(axis))])


def from_behind(shard, axis, by):
    size = lax.axis_size(axis)
    return lax.ppermute(shard, axis, [(i, (i + by) % size) for i in range(size)])


def rounded(value):
    return lax.optimization_barrier(value.astype(jnp.bfloat16))


def depthwise_conv(widened, tap_weights, row_count):
    tap_count = tap_weights.shape[0]

    def add_tap(tap_index, running):
        window = lax.dynamic_slice_in_dim(widened, tap_count - 1 - tap_index, row_count, 0)
        return running + tap_weights[tap_index] * window.astype(jnp.float32)

    return lax.fori_loop(
        0, tap_count, add_tap, jnp.zeros((row_count, widened.shape[1]), jnp.float32)
    )


def long_kernel_rows(residue_mine, rate_mine, length):
    positions = jnp.arange(length, dtype=jnp.int32).astype(jnp.float32)
    mode_total = rate_mine.shape[0]

    def add_mode(mode_index, running):
        decay_rate = rate_mine[mode_index]
        mode_weight = (
            residue_mine[mode_index]
            * jnp.sqrt(-jnp.expm1(-2.0 * decay_rate))
            / math.sqrt(mode_total)
        )
        return running + mode_weight[:, None] * jnp.exp(-decay_rate[:, None] * positions[None, :])

    return lax.fori_loop(
        0, mode_total, add_mode, jnp.zeros((rate_mine.shape[1], length), jnp.float32)
    )


def dft_tables(row_size, column_size, period_size):
    row_index = lax.broadcasted_iota(jnp.int32, (row_size, column_size), 0)
    column_index = lax.broadcasted_iota(jnp.int32, (row_size, column_size), 1)
    angles = (row_index * column_index % period_size).astype(jnp.float32) * (
        2.0 * math.pi / period_size
    )
    return (jnp.cos(angles), jnp.sin(angles))


def forward_dft(signal, outer_size, inner_size):
    highest = lax.Precision.HIGHEST
    cos_outer, sin_outer = dft_tables(outer_size // 2, outer_size, outer_size)
    twiddle_cos, twiddle_sin = dft_tables(outer_size, inner_size, outer_size * inner_size)
    cos_inner, sin_inner = dft_tables(inner_size, inner_size, inner_size)
    step_real = jnp.einsum("pab,ak->pkb", signal, cos_outer, precision=highest)
    step_imag = -jnp.einsum("pab,ak->pkb", signal, sin_outer, precision=highest)
    turned_real = step_real * twiddle_cos + step_imag * twiddle_sin
    turned_imag = step_imag * twiddle_cos - step_real * twiddle_sin
    spec_real = jnp.einsum("pkb,bm->pkm", turned_real, cos_inner, precision=highest) + jnp.einsum(
        "pkb,bm->pkm", turned_imag, sin_inner, precision=highest
    )
    spec_imag = jnp.einsum("pkb,bm->pkm", turned_imag, cos_inner, precision=highest) - jnp.einsum(
        "pkb,bm->pkm", turned_real, sin_inner, precision=highest
    )
    return (spec_real, spec_imag)


def inverse_dft(spec_real, spec_imag, outer_size, inner_size):
    highest = lax.Precision.HIGHEST
    cos_outer, sin_outer = dft_tables(outer_size // 2, outer_size, outer_size)
    twiddle_cos, twiddle_sin = dft_tables(outer_size, inner_size, outer_size * inner_size)
    cos_inner, sin_inner = dft_tables(inner_size, inner_size, inner_size)
    back_real = jnp.einsum("pkm,mb->pkb", spec_real, cos_inner, precision=highest) - jnp.einsum(
        "pkm,mb->pkb", spec_imag, sin_inner, precision=highest
    )
    back_imag = jnp.einsum("pkm,mb->pkb", spec_real, sin_inner, precision=highest) + jnp.einsum(
        "pkm,mb->pkb", spec_imag, cos_inner, precision=highest
    )
    turned_real = back_real * twiddle_cos - back_imag * twiddle_sin
    turned_imag = back_real * twiddle_sin + back_imag * twiddle_cos
    signal = jnp.einsum("pkb,ak->pab", turned_real, cos_outer, precision=highest) - jnp.einsum(
        "pkb,ak->pab", turned_imag, sin_outer, precision=highest
    )
    return signal / (outer_size * inner_size)


def attend_block(query_rows, query_index, key_block, value_block, key_start, running, score_scale):
    row_peak, row_total, blended = running
    scores = (
        jnp.einsum("qhd,khd->hqk", query_rows, key_block, preferred_element_type=jnp.float32)
        * score_scale
    )
    key_index = key_start + jnp.arange(key_block.shape[0], dtype=jnp.int32)
    scores = jnp.where(key_index[None, None, :] <= query_index[None, :, None], scores, -1e30)
    new_peak = jnp.maximum(row_peak, jnp.max(scores, axis=2))
    weights = jnp.exp(scores - new_peak[:, :, None])
    rescale = jnp.exp(row_peak - new_peak)
    row_total = row_total * rescale + jnp.sum(weights, axis=2)
    blended = blended * rescale[:, :, None] + jnp.einsum(
        "hqk,khd->hqd",
        weights.astype(jnp.bfloat16),
        value_block,
        preferred_element_type=jnp.float32,
    )
    return (new_peak, row_total, blended)


def merge_partials(first_part, second_part):
    peak_one, total_one, blend_one = first_part
    peak_two, total_two, blend_two = second_part
    new_peak = jnp.maximum(peak_one, peak_two)
    scale_one = jnp.exp(peak_one - new_peak)
    scale_two = jnp.exp(peak_two - new_peak)
    new_total = total_one * scale_one + total_two * scale_two
    new_blend = blend_one * scale_one[..., None] + blend_two * scale_two[..., None]
    return (new_peak, new_total, new_blend)


def split_halves(stacked_part, half_size, upper_side):
    lower_half = stacked_part[:, :half_size]
    upper_half = stacked_part[:, half_size:]
    keep_half = jnp.where(upper_side == 1, upper_half, lower_half)
    send_half = jnp.where(upper_side == 1, lower_half, upper_half)
    return (keep_half, send_half)


def by_position(
    token_ids, embedding, short_filter, medium_filter, long_residue, long_rate, query_gain, key_gain
):
    tok_count = token_ids.shape[0]
    vocab_size = embedding.shape[0]
    width_dev = embedding.shape[1]
    seq_count = lax.axis_size("seq")
    seq_index = lax.axis_index("seq")
    one_hot = (
        token_ids[:, None] == lax.broadcasted_iota(jnp.int32, (tok_count, vocab_size), 1)
    ).astype(jnp.bfloat16)
    embedded = jnp.dot(one_hot, embedding, preferred_element_type=jnp.float32).astype(jnp.bfloat16)
    short_taps = short_filter.shape[0]
    rim_rows = shifted(embedded[tok_count - (short_taps - 1) :], "seq", 1)
    widened = jnp.concatenate([rim_rows, embedded], axis=0)
    short_part = depthwise_conv(widened, short_filter, tok_count)
    short_gated = rounded(embedded.astype(jnp.float32) * short_part)
    medium_taps = medium_filter.shape[0]
    upper_rows = shifted(short_gated[tok_count - (medium_taps - 1) :], "seq", 1)
    widened_two = jnp.concatenate([upper_rows, short_gated], axis=0)
    medium_part = depthwise_conv(widened_two, medium_filter, tok_count)
    medium_gated = rounded(short_gated.astype(jnp.float32) * medium_part)
    per_dev = width_dev // seq_count
    length = tok_count * seq_count
    grouped = medium_gated.T.reshape(seq_count, per_dev, tok_count)
    spread = lax.all_to_all(grouped, "seq", split_axis=0, concat_axis=2, tiled=True).reshape(
        per_dev, length
    )
    rate_mine = lax.dynamic_slice_in_dim(long_rate, seq_index * per_dev, per_dev, 1)
    residue_mine = lax.dynamic_slice_in_dim(long_residue, seq_index * per_dev, per_dev, 1)
    kernel = long_kernel_rows(residue_mine, rate_mine, length)
    outer_size = 128
    inner_size = 2 * length // outer_size
    spread_float = spread.astype(jnp.float32)
    data_real, data_imag = forward_dft(
        spread_float.reshape(per_dev, outer_size // 2, inner_size), outer_size, inner_size
    )
    kernel_real, kernel_imag = forward_dft(
        kernel.reshape(per_dev, outer_size // 2, inner_size), outer_size, inner_size
    )
    product_real = data_real * kernel_real - data_imag * kernel_imag
    product_imag = data_real * kernel_imag + data_imag * kernel_real
    long_part = inverse_dft(product_real, product_imag, outer_size, inner_size).reshape(
        per_dev, length
    )
    channel_out = (spread_float * long_part).astype(jnp.bfloat16)
    returned = lax.all_to_all(channel_out[None], "seq", split_axis=2, concat_axis=0, tiled=True)
    hyena_out = returned.reshape(width_dev, tok_count).T
    head_count = width_dev // HEAD
    hyena_float = hyena_out.astype(jnp.float32)
    square_sums = jnp.sum(hyena_float * hyena_float, axis=1)
    total_sums = lax.psum(square_sums, "ch")
    inverse_scale = lax.rsqrt(total_sums / C + 1e-05)
    normed = hyena_float * inverse_scale[:, None]
    values = normed.astype(jnp.bfloat16).reshape(tok_count, head_count, HEAD)
    queries = (
        (normed * query_gain[None, :]).astype(jnp.bfloat16).reshape(tok_count, head_count, HEAD)
    )
    key_rows = (
        (normed * key_gain[None, :]).astype(jnp.bfloat16).reshape(tok_count, head_count, HEAD)
    )
    group_size = 2
    level_count = group_size.bit_length() - 1
    seq_bits = seq_count.bit_length() - 1
    base_bit = seq_bits - level_count
    stride = seq_count // group_size
    stacked = queries[None]
    level = 0
    bit_number = base_bit + level
    partner_rows = swapped(stacked, "seq", bit_number)
    upper_side = seq_index >> bit_number & 1
    stacked = jnp.where(
        upper_side == 1,
        jnp.concatenate([partner_rows, stacked], axis=0),
        jnp.concatenate([stacked, partner_rows], axis=0),
    )
    query_rows = stacked.reshape(group_size * tok_count, head_count, HEAD)
    group_first = seq_index % stride
    block_numbers = group_first + stride * jnp.arange(group_size, dtype=jnp.int32)
    query_index = (
        block_numbers[:, None] * tok_count + jnp.arange(tok_count, dtype=jnp.int32)[None, :]
    ).reshape(group_size * tok_count)
    score_scale = HEAD ** (-0.5)
    partial_state = (
        jnp.full((head_count, group_size * tok_count), -1e30, jnp.float32),
        jnp.zeros((head_count, group_size * tok_count), jnp.float32),
        jnp.zeros((head_count, group_size * tok_count, HEAD), jnp.float32),
    )

    def cycle_step(turn_number, carried):
        key_block, value_block, running = carried
        key_block, value_block = from_behind((key_block, value_block), "seq", -1)
        source_block = jnp.remainder(seq_index + turn_number, seq_count)
        running = attend_block(
            query_rows,
            query_index,
            key_block,
            value_block,
            source_block * tok_count,
            running,
            score_scale,
        )
        return (key_block, value_block, running)

    carried = lax.fori_loop(1, stride + 1, cycle_step, (key_rows, values, partial_state))
    row_peak, row_total, blended = carried[2]
    row_peak = row_peak.reshape(head_count, group_size, tok_count)
    row_total = row_total.reshape(head_count, group_size, tok_count)
    blended = blended.reshape(head_count, group_size, tok_count, HEAD)
    for level in reversed(range(level_count)):
        bit_number = base_bit + level
        half_size = row_peak.shape[1] // 2
        upper_side = seq_index >> bit_number & 1
        keep_peak, send_peak = split_halves(row_peak, half_size, upper_side)
        keep_total, send_total = split_halves(row_total, half_size, upper_side)
        keep_blend, send_blend = split_halves(blended, half_size, upper_side)
        got_peak, got_total, got_blend = swapped(
            (send_peak, send_total, send_blend), "seq", bit_number
        )
        row_peak, row_total, blended = merge_partials(
            (keep_peak, keep_total, keep_blend), (got_peak, got_total, got_blend)
        )
    normalized = blended[:, 0] / row_total[:, 0][:, :, None]
    attended = normalized.transpose(1, 0, 2).reshape(tok_count, width_dev).astype(jnp.bfloat16)
    return (hyena_out, attended)


def transform_tables(block):
    size = 2 * block
    step = 2.0 * np.pi / size
    freq = (np.arange(block) + 0.5)[:, None]
    angle = freq * np.arange(size)[None, :] * step
    forward = np.concatenate([np.cos(angle), -np.sin(angle)], axis=0)
    angle = (np.arange(block)[:, None] + block) * freq.T * step
    backward = np.concatenate([np.cos(angle), -np.sin(angle)], axis=1) * (2.0 / size)

    def parts(table):
        kept = []
        for _ in range(3):
            kept.append(table.astype(np.float32).astype(ml_dtypes.bfloat16))
            table = table - kept[-1].astype(np.float64)
        return np.concatenate(kept, axis=0)

    forward, backward = parts(forward), parts(backward)
    first, second, third = np.split(forward[:, :block], 3)
    taps = np.concatenate([np.concatenate([first, second], axis=1), np.concatenate([first, third], axis=1)], axis=0)
    forward = np.concatenate(np.split(forward, 3), axis=1)
    first, second, third = np.split(backward, 3)
    backward = np.concatenate([first, second, first, third, second, first], axis=1)
    return forward, backward, taps


def split_pair(value):
    upper = value.astype(jnp.bfloat16)
    return upper, (value - upper.astype(jnp.float32)).astype(jnp.bfloat16)


def split_three(value):
    upper = value.astype(jnp.bfloat16)
    rest = value - upper.astype(jnp.float32)
    middle = rest.astype(jnp.bfloat16)
    return upper, middle, (rest - middle.astype(jnp.float32)).astype(jnp.bfloat16)


def minus_expm1(value):
    term = value
    series = value
    for order in range(2, 11):
        term = term * value * (-1.0 / order)
        series = series + term
    return jnp.where(value < 0.5, series, 1.0 - jnp.exp(-value))


def dot32(left, right):
    return jnp.dot(left, right, preferred_element_type=jnp.float32)


def own_lanes(width):
    return pl.ds(pl.multiple_of(lax.axis_index("seq") * width, width), width)


def fetch_kernel(
    token_ids, residue, rate, medium, table, ids_out, residue_out, rate_out, medium_out, table_out, sems
):
    lanes = own_lanes(medium_out.shape[1])
    copies = [
        pltpu.make_async_copy(source, target, sems.at[i])
        for i, (source, target) in enumerate(
            [
                (token_ids, ids_out),
                (residue.at[:, lanes], residue_out),
                (rate.at[:, lanes], rate_out),
                (medium.at[:, lanes], medium_out),
                (table, table_out),
            ]
        )
    ]
    for copy in copies:
        copy.start()
    for copy in copies:
        copy.wait()


def response_kernel(residue, rate, medium, table, medium_out, long_out):
    block, width = medium.shape
    size = 2 * block
    mode_total = rate.shape[0]
    block_total = long_out.shape[1] // width

    def transformed(signal):
        up, middle, low = split_three(signal)
        return (
            dot32(table[0:size, :], jnp.concatenate([up, up], axis=0))
            + dot32(table[0:size, :], jnp.concatenate([middle, middle], axis=0))
            + dot32(table[size : 2 * size, :], jnp.concatenate([low, up], axis=0))
        )

    medium_out[...] = transformed(medium[...])
    decays = rate[...]
    weights = residue[...] * jnp.sqrt(minus_expm1(2.0 * decays)) / math.sqrt(mode_total)
    modes = [weights * jnp.exp(-decays * float(part * block)) for part in range(block_total)]
    place = lax.broadcasted_iota(jnp.int32, (block, width), 0).astype(jnp.float32)
    rows = 32
    tiles = []
    for first in range(0, block, rows):
        sums = [jnp.zeros((rows, width), jnp.float32) for _ in range(block_total)]
        for mode in range(mode_total):
            shape = jnp.exp(-decays[mode : mode + 1, :] * place[first : first + rows])
            for part in range(block_total):
                sums[part] = sums[part] + modes[part][mode : mode + 1, :] * shape
        tiles.append(jnp.concatenate(sums, axis=1))
    long_out[...] = transformed(jnp.concatenate(tiles, axis=0))


def conv_kernel(*refs, piece_count):
    pieces = refs[:piece_count]
    (embedding, short, medium_resp, long_resp, forward, backward, hyena, sums) = refs[piece_count : piece_count + 8]
    ids, ordered, padded, row_sums, copied_sums, sem = refs[piece_count + 8 :]
    width = padded.shape[1]
    block = width
    size = 2 * block
    length = hyena.shape[0]
    count = length // block
    pair = count
    me = lax.axis_index("seq")
    for i, piece in enumerate(pieces):
        ids[2 * i : 2 * i + 2, :] = piece[...]
    for b in range(count):
        ordered[b : b + 1, :] = ids[pl.ds(lax.bitwise_xor(me, b), 1), :]
    across = jnp.transpose(ordered[...].astype(jnp.float32), (1, 0)).astype(jnp.int32)
    padded[0:8, :] = jnp.zeros((8, width), jnp.float32)
    table = embedding[:, own_lanes(width)]
    short_taps = short[:, own_lanes(width)]
    vocab = table.shape[0]
    entries = lax.broadcasted_iota(jnp.int32, (block, vocab), 1)
    rows = 16

    def embed(chunk):
        for b in range(chunk * pair, (chunk + 1) * pair):
            chosen = jnp.where(across[:, b : b + 1] == entries, 1.0, 0.0).astype(jnp.bfloat16)
            padded[8 + b * block : 8 + (b + 1) * block, :] = dot32(chosen, table)

    nothing = jnp.zeros((block, width), jnp.bfloat16)
    gated = [{-1: nothing}, {-1: nothing}]
    spectra, products = [{}, {}], [{}, {}]

    def short_gate(chunk):
        for b in range(chunk * pair, (chunk + 1) * pair):
            running = jnp.zeros((block, width), jnp.float32)
            for j in range(short_taps.shape[0]):
                running = running + short_taps[j : j + 1, :] * padded[8 + b * block - j : 8 + (b + 1) * block - j, :]
            signal = padded[8 + b * block : 8 + (b + 1) * block, :] * running
            gated[0][b] = signal.astype(jnp.bfloat16)

    def analyse(turn, chunk):
        span = range(chunk * pair, (chunk + 1) * pair)
        signal = jnp.concatenate(
            [jnp.concatenate([gated[turn][b - 1] for b in span], axis=1)]
            + [jnp.concatenate([gated[turn][b] for b in span], axis=1)],
            axis=0,
        )
        spectrum = dot32(forward[...], jnp.concatenate([signal] * 3, axis=0))
        for i, b in enumerate(span):
            spectra[turn][b] = spectrum[:, i * width : (i + 1) * width]

    def multiply(turn, response, chunk):
        span = range(chunk * pair, (chunk + 1) * pair)
        sources = range(span[-1] + 1) if turn else span
        tiles = {b: ([], []) for b in span}
        for first in range(0, block, rows):
            sums = {b: ([], []) for b in span}
            for upper in [slice(i, i + 8) for i in range(first, first + rows, 8)]:
                lower = slice(block + upper.start, block + upper.stop)
                data = {b: (spectra[turn][b][upper], spectra[turn][b][lower]) for b in sources}
                filt = [
                    (response[upper, i * width : (i + 1) * width], response[lower, i * width : (i + 1) * width])
                    for i in range(span[-1] + 1 if turn else 1)
                ]
                data = {b: (real, imag, real + imag) for b, (real, imag) in data.items()}
                filt = [(real, imag - real, real + imag) for real, imag in filt]
                for b in span:
                    shared = to_real = to_imag = 0.0
                    for part in range(b + 1 if turn else 1):
                        (real, imag, both), (base, ahead, total) = data[b - part], filt[part]
                        shared = shared + both * base
                        to_imag = to_imag + real * ahead
                        to_real = to_real + imag * total
                    total_real, total_imag = shared - to_real, shared + to_imag
                    sums[b][0].append(total_real)
                    sums[b][1].append(total_imag)
            for b in span:
                for side in range(2):
                    tiles[b][side].append(split_three(jnp.concatenate(sums[b][side], axis=0)))
        columns = [
            [jnp.concatenate([tile[i] for tile in tiles[b][0] + tiles[b][1]], axis=0) for i in range(3)] for b in span
        ]
        products[turn][chunk] = [jnp.concatenate([column[i] for column in columns], axis=1) for i in range(3)]

    def synthesise(turn, chunk):
        up, middle, low = products[turn].pop(chunk)
        return dot32(backward[...], jnp.concatenate([up, up, middle, up, middle, low], axis=0))

    def gate(turn, chunk):
        out = synthesise(turn, chunk)
        results = []
        for i in range(pair):
            past = gated[turn][chunk * pair + i].astype(jnp.float32)
            results.append((past * out[:, i * width : (i + 1) * width]).astype(jnp.bfloat16))
        return results

    def medium_gate(chunk):
        for i, signal in enumerate(gate(0, chunk)):
            gated[1][chunk * pair + i] = signal

    ones = jnp.ones((size, width), jnp.bfloat16)
    diagonal = lax.broadcasted_iota(jnp.int32, (block, block), 0) == lax.broadcasted_iota(
        jnp.int32, (block, block), 1
    )

    def long_gate(chunk):
        for i, result in enumerate(gate(1, chunk)):
            b = chunk * pair + i
            hyena[b * block : (b + 1) * block, :] = result
            wide = result.astype(jnp.float32)
            spread = dot32(jnp.concatenate(split_pair(wide * wide), axis=1), ones)
            row_sums[b : b + 1, :] = jnp.sum(jnp.where(diagonal, spread, 0.0), axis=0, keepdims=True)

    stages = [
        embed,
        short_gate,
        functools.partial(analyse, 0),
        functools.partial(multiply, 0, medium_resp),
        medium_gate,
        functools.partial(analyse, 1),
        functools.partial(multiply, 1, long_resp),
        long_gate,
    ]
    chunks = count // pair
    for turn in range(chunks + len(stages) - 1):
        for stage in range(len(stages)):
            if 0 <= turn - stage < chunks:
                stages[stage](turn - stage)
    copied_sums[...] = jnp.broadcast_to(row_sums[...][None], copied_sums.shape)
    copy = pltpu.make_async_copy(copied_sums, sums, sem)
    copy.start()
    copy.wait()


def attend_kernel(own, other, sums, query_gain, key_gain, out, queries, keys, values, *, channel_count):
    length, width = own.shape
    count = sums.shape[1]
    block = length // count
    me = lax.axis_index("seq")
    core = lax.rem(me, 2)
    total = jnp.sum(sums[...], axis=0)
    inverse = lax.rsqrt(total / channel_count + 1e-05)
    inverse = jnp.transpose(inverse, (1, 0))
    signals = (own, other)
    gains = []
    for side in range(2):
        lanes = pl.ds(pl.multiple_of(lax.bitwise_xor(me, side) * width, width), width)
        gains.append((query_gain[0:1, lanes], key_gain[0:1, lanes]))

    def normalise(b):
        spans = slice(b * block, (b + 1) * block)
        scale = jnp.broadcast_to(inverse[:, b : b + 1], (block, width))
        for side, signal in enumerate(signals):
            normed = signal[spans, :].astype(jnp.float32) * scale
            values[side, spans, :] = normed.astype(jnp.bfloat16)
            keys[side, spans, :] = (normed * gains[side][1]).astype(jnp.bfloat16)
            queries[side, spans, :] = (normed * gains[side][0]).astype(jnp.bfloat16)

    row_index = lax.broadcasted_iota(jnp.int32, (block, 2 * block), 0) + core * block
    allowed = lax.broadcasted_iota(jnp.int32, (block, 2 * block), 1) <= row_index

    def score(chip, side):
        reach = (chip + 1) * 2 * block
        start = pl.multiple_of((2 * chip + core) * block, block)
        scores = lax.dot_general(
            queries[side, pl.ds(start, block), :],
            keys[side, 0:reach, :],
            (((1,), (1,)), ((), ())),
            preferred_element_type=jnp.float32,
        )
        last = jnp.where(allowed, scores[:, reach - 2 * block :], -1e30)
        return jnp.concatenate([scores[:, : reach - 2 * block], last], axis=1) if chip else last

    def weigh(scores):
        peak = jnp.max(scores, axis=1, keepdims=True)
        weights = jnp.exp2((scores - peak) * (width**-0.5 * math.log2(math.e)))
        return weights.astype(jnp.bfloat16), jnp.sum(weights, axis=1, keepdims=True)

    def blend(chip, side, weights, row_total):
        reach = (chip + 1) * 2 * block
        place = lax.bitwise_xor(me // 2, chip)
        half = lax.bitwise_xor(core, side)
        blended = dot32(weights, values[side, 0:reach, :])
        lanes = pl.ds(pl.multiple_of(half * width, width), width)
        out[place, :, lanes] = (blended / row_total).astype(jnp.bfloat16)

    for b in range(count):
        normalise(b)
    chains = [(chip, side) for chip in reversed(range(count // 2)) for side in range(2)]
    scored, weighed = {}, {}
    for turn in range(len(chains) + 4):
        if turn < len(chains):
            scored[turn] = score(*chains[turn])
        if 0 <= turn - 2 < len(chains):
            weighed[turn - 2] = weigh(scored.pop(turn - 2))
        if 0 <= turn - 4 < len(chains):
            blend(*chains[turn - 4], *weighed.pop(turn - 4))


def outgoing_kernel(own, other, out):
    width = own.shape[1]
    block = out.shape[1]
    me = lax.axis_index("seq")
    core = lax.rem(me, 2)
    for i in range(out.shape[0]):
        start = pl.multiple_of((2 * lax.bitwise_xor(me // 2, i) + core) * block, block)
        for side, signal in enumerate((own, other)):
            lanes = pl.ds(pl.multiple_of(lax.bitwise_xor(core, side) * width, width), width)
            out[i, :, lanes] = signal[pl.ds(start, block), :]


def hold_kernel(*refs):
    refs[-1][...] = refs[0][...]


def place_part_kernel(*refs, order, extra):
    blocks, out, sems = refs[extra:-2], refs[-2], refs[-1]
    span = blocks[0].shape[1]
    chip = lax.axis_index("seq") // 2
    copies = []
    for n, (i, block) in enumerate(zip(order, blocks)):
        lanes = pl.ds(pl.multiple_of(lax.bitwise_xor(chip, i) * span, span), span)
        copies.append(pltpu.make_async_copy(block, out.at[:, lanes], sems.at[n]))
    for copy in copies:
        copy.start()
    for copy in copies:
        copy.wait()


def place_kernel(*refs, order):
    blocks, out = refs[:-1], refs[-1]
    span = blocks[0].shape[1]
    chip = lax.axis_index("seq") // 2
    for i, block in zip(order, blocks):
        out[:, pl.ds(pl.multiple_of(lax.bitwise_xor(chip, i) * span, span), span)] = block[...]


def by_head(
    token_ids, embedding, short_filter, medium_filter, long_residue, long_rate, query_gain, key_gain
):
    seq_count = lax.axis_size("seq")
    ch_count = lax.axis_size("ch")
    block = token_ids.shape[0]
    width_dev = embedding.shape[1]
    length = block * seq_count
    width = HEAD
    f32, bf16 = jnp.float32, jnp.bfloat16
    forward, backward, tap_table = transform_tables(block)
    whole = pl.BlockSpec(memory_space=pltpu.VMEM)
    params = pltpu.CompilerParams(vmem_limit_bytes=24 * 1024 * 1024)

    def exchange(value, apart):
        return lax.ppermute(value, "seq", [(i, i ^ apart) for i in range(seq_count)])

    mode_total = long_rate.shape[0]
    in_hbm = pl.BlockSpec(memory_space=pltpu.HBM)

    def fetched(value):
        return pltpu.with_memory_space_constraint(value, pltpu.HBM)

    partner_ids = exchange(token_ids, 1)
    operands = (token_ids, long_residue, long_rate, medium_filter, jnp.asarray(tap_table))
    own_ids, *filters = pl.pallas_call(
        fetch_kernel,
        out_shape=[
            jax.ShapeDtypeStruct((block,), jnp.int32),
            jax.ShapeDtypeStruct((mode_total, width), f32),
            jax.ShapeDtypeStruct((mode_total, width), f32),
            jax.ShapeDtypeStruct((block, width), f32),
            jax.ShapeDtypeStruct(tap_table.shape, bf16),
        ],
        in_specs=[in_hbm] * 5,
        out_specs=[whole] * 5,
        scratch_shapes=[pltpu.SemaphoreType.DMA((5,))],
        compiler_params=params,
        cost_estimate=pl.CostEstimate(flops=10**9, bytes_accessed=2 * 10**6, transcendentals=0),
        name="fetched_operands",
    )(*[fetched(value) for value in operands])
    chip_ids = jnp.stack([own_ids, partner_ids])
    pieces = [chip_ids] + [exchange(chip_ids, 2 * i) for i in range(1, seq_count // 2)]
    medium_resp, long_resp = pl.pallas_call(
        response_kernel,
        out_shape=[
            jax.ShapeDtypeStruct((2 * block, width), f32),
            jax.ShapeDtypeStruct((2 * block, length), f32),
        ],
        in_specs=[whole] * 4,
        out_specs=[whole] * 2,
        compiler_params=params,
        cost_estimate=pl.CostEstimate(flops=2 * 10**9, bytes_accessed=2 * 10**6, transcendentals=3 * 10**5),
        name="filter_responses",
    )(*filters)

    devices = seq_count * ch_count
    hyena, square_sums = pl.pallas_call(
        functools.partial(conv_kernel, piece_count=len(pieces)),
        out_shape=[
            jax.ShapeDtypeStruct((length, width), bf16),
            pltpu.HBM((devices, seq_count, block), f32),
        ],
        in_specs=[whole] * (len(pieces) + 6),
        out_specs=[whole, in_hbm],
        scratch_shapes=[
            pltpu.VMEM((seq_count, block), jnp.int32),
            pltpu.VMEM((seq_count, block), jnp.int32),
            pltpu.VMEM((8 + length, width), f32),
            pltpu.VMEM((seq_count, block), f32),
            pltpu.VMEM((devices, seq_count, block), f32),
            pltpu.SemaphoreType.DMA,
        ],
        compiler_params=params,
        cost_estimate=pl.CostEstimate(flops=2 * 10**9, bytes_accessed=2 * 10**6, transcendentals=0),
        name="gated_convolutions",
    )(*pieces, embedding, short_filter, medium_resp, long_resp, forward, backward)

    other = exchange(hyena, 1)
    all_sums = lax.all_to_all(square_sums, ("seq", "ch"), 0, 0, tiled=True)

    def placed(blocks, name, order):
        return pl.pallas_call(
            functools.partial(place_kernel, order=(0, *order)),
            out_shape=jax.ShapeDtypeStruct((block, width_dev), bf16),
            in_specs=[whole] * len(blocks),
            out_specs=whole,
            compiler_params=params,
            cost_estimate=pl.CostEstimate(flops=10**9, bytes_accessed=10**6, transcendentals=0),
            name=name,
        )(*blocks)

    def placed_part(blocks, name, order, so_far=()):
        return pl.pallas_call(
            functools.partial(place_part_kernel, order=order, extra=len(so_far)),
            out_shape=jax.ShapeDtypeStruct((block, width_dev), bf16),
            in_specs=[in_hbm] * len(so_far) + [whole] * len(blocks),
            out_specs=in_hbm,
            scratch_shapes=[pltpu.SemaphoreType.DMA((len(blocks),))],
            input_output_aliases={0: 0} if so_far else {},
            compiler_params=params,
            cost_estimate=pl.CostEstimate(flops=10**9, bytes_accessed=10**6, transcendentals=0),
            name=name,
        )(*so_far, *blocks)

    def held(value, others):
        return pl.pallas_call(
            hold_kernel,
            out_shape=jax.ShapeDtypeStruct(value.shape, value.dtype),
            in_specs=[whole] + [pl.BlockSpec(memory_space=pl.ANY)] * len(others),
            out_specs=whole,
            compiler_params=params,
            name="held_block",
        )(value, *others)

    order = list(range(1, seq_count // 2))
    hyena_blocks = pl.pallas_call(
        outgoing_kernel,
        out_shape=jax.ShapeDtypeStruct((seq_count // 2, block, 2 * width), bf16),
        in_specs=[whole, whole],
        out_specs=whole,
        compiler_params=params,
        cost_estimate=pl.CostEstimate(flops=2 * 10**9, bytes_accessed=10**6, transcendentals=0),
        name="hyena_blocks",
    )(hyena, other)
    hyena_parts = [hyena_blocks[0]] + [exchange(hyena_blocks[i], 2 * i) for i in order]
    outgoing = pl.pallas_call(
        functools.partial(attend_kernel, channel_count=width_dev * ch_count),
        out_shape=jax.ShapeDtypeStruct((seq_count // 2, block, 2 * width), bf16),
        in_specs=[whole] * 5,
        out_specs=whole,
        scratch_shapes=[pltpu.VMEM((2, length, width), bf16)] * 3,
        compiler_params=params,
        cost_estimate=pl.CostEstimate(flops=2 * 10**9, bytes_accessed=10**6, transcendentals=10**6),
        name="attention",
    )(hyena, other, all_sums, query_gain.reshape(1, width_dev), key_gain.reshape(1, width_dev))
    last = held(outgoing[order[0]], hyena_parts[1:])
    parts = [outgoing[0]] + [exchange(outgoing[i], 2 * i) for i in order[:0:-1]] + [exchange(last, 2 * order[0])]
    early = placed_part(parts[:-1], "placed_early", (0, *order[:0:-1]))
    attended = placed_part(parts[-1:], "placed_attended", order[:1], (early,))
    return placed(hyena_parts, "placed_hyena", order), attended


def on_device(*operands):
    seq_count = lax.axis_size("seq")
    token_ids, embedding, _, medium_filter = operands[:4]
    block = token_ids.shape[0]
    fits = (
        embedding.shape[1] == seq_count * HEAD
        and block == HEAD
        and medium_filter.shape[0] == block
        and seq_count % 8 == 0
        and seq_count & (seq_count - 1) == 0
    )
    return by_head(*operands) if fits else by_position(*operands)


def solution(mesh):
    in_specs = (
        P("seq"),
        P(None, "ch"),
        P(None, "ch"),
        P(None, "ch"),
        P(None, "ch"),
        P(None, "ch"),
        P("ch"),
        P("ch"),
    )
    out_specs = (P("seq", "ch"), P("seq", "ch"))
    return jax.shard_map(
        on_device, mesh=mesh, in_specs=in_specs, out_specs=out_specs, check_vma=False
    )
```

```python
import functools
import math

import jax
import jax.numpy as jnp
import ml_dtypes
import numpy as np
from jax import lax
from jax.experimental import pallas as pl
from jax.experimental.pallas import tpu as pltpu
from jax.sharding import PartitionSpec as P

C = 4096
HEAD = 128


def shifted(value, axis, steps):
    count = lax.axis_size(axis)
    leading, last = (max(0, -steps), min(count, count - steps))
    return lax.ppermute(value, axis, [(source, source + steps) for source in range(leading, last)])


def swapped(shard, axis, apart):
    return lax.ppermute(shard, axis, [(i, i ^ 1 << apart) for i in range(lax.axis_size(axis))])


def from_behind(shard, axis, by):
    size = lax.axis_size(axis)
    return lax.ppermute(shard, axis, [(i, (i + by) % size) for i in range(size)])


def rounded(value):
    return lax.optimization_barrier(value.astype(jnp.bfloat16))


def depthwise_conv(widened, tap_weights, row_count):
    tap_count = tap_weights.shape[0]

    def add_tap(tap_index, running):
        window = lax.dynamic_slice_in_dim(widened, tap_count - 1 - tap_index, row_count, 0)
        return running + tap_weights[tap_index] * window.astype(jnp.float32)

    return lax.fori_loop(
        0, tap_count, add_tap, jnp.zeros((row_count, widened.shape[1]), jnp.float32)
    )


def long_kernel_rows(residue_mine, rate_mine, length):
    positions = jnp.arange(length, dtype=jnp.int32).astype(jnp.float32)
    mode_total = rate_mine.shape[0]

    def add_mode(mode_index, running):
        decay_rate = rate_mine[mode_index]
        mode_weight = (
            residue_mine[mode_index]
            * jnp.sqrt(-jnp.expm1(-2.0 * decay_rate))
            / math.sqrt(mode_total)
        )
        return running + mode_weight[:, None] * jnp.exp(-decay_rate[:, None] * positions[None, :])

    return lax.fori_loop(
        0, mode_total, add_mode, jnp.zeros((rate_mine.shape[1], length), jnp.float32)
    )


def dft_tables(row_size, column_size, period_size):
    row_index = lax.broadcasted_iota(jnp.int32, (row_size, column_size), 0)
    column_index = lax.broadcasted_iota(jnp.int32, (row_size, column_size), 1)
    angles = (row_index * column_index % period_size).astype(jnp.float32) * (
        2.0 * math.pi / period_size
    )
    return (jnp.cos(angles), jnp.sin(angles))


def forward_dft(signal, outer_size, inner_size):
    highest = lax.Precision.HIGHEST
    cos_outer, sin_outer = dft_tables(outer_size // 2, outer_size, outer_size)
    twiddle_cos, twiddle_sin = dft_tables(outer_size, inner_size, outer_size * inner_size)
    cos_inner, sin_inner = dft_tables(inner_size, inner_size, inner_size)
    step_real = jnp.einsum("pab,ak->pkb", signal, cos_outer, precision=highest)
    step_imag = -jnp.einsum("pab,ak->pkb", signal, sin_outer, precision=highest)
    turned_real = step_real * twiddle_cos + step_imag * twiddle_sin
    turned_imag = step_imag * twiddle_cos - step_real * twiddle_sin
    spec_real = jnp.einsum("pkb,bm->pkm", turned_real, cos_inner, precision=highest) + jnp.einsum(
        "pkb,bm->pkm", turned_imag, sin_inner, precision=highest
    )
    spec_imag = jnp.einsum("pkb,bm->pkm", turned_imag, cos_inner, precision=highest) - jnp.einsum(
        "pkb,bm->pkm", turned_real, sin_inner, precision=highest
    )
    return (spec_real, spec_imag)


def inverse_dft(spec_real, spec_imag, outer_size, inner_size):
    highest = lax.Precision.HIGHEST
    cos_outer, sin_outer = dft_tables(outer_size // 2, outer_size, outer_size)
    twiddle_cos, twiddle_sin = dft_tables(outer_size, inner_size, outer_size * inner_size)
    cos_inner, sin_inner = dft_tables(inner_size, inner_size, inner_size)
    back_real = jnp.einsum("pkm,mb->pkb", spec_real, cos_inner, precision=highest) - jnp.einsum(
        "pkm,mb->pkb", spec_imag, sin_inner, precision=highest
    )
    back_imag = jnp.einsum("pkm,mb->pkb", spec_real, sin_inner, precision=highest) + jnp.einsum(
        "pkm,mb->pkb", spec_imag, cos_inner, precision=highest
    )
    turned_real = back_real * twiddle_cos - back_imag * twiddle_sin
    turned_imag = back_real * twiddle_sin + back_imag * twiddle_cos
    signal = jnp.einsum("pkb,ak->pab", turned_real, cos_outer, precision=highest) - jnp.einsum(
        "pkb,ak->pab", turned_imag, sin_outer, precision=highest
    )
    return signal / (outer_size * inner_size)


def attend_block(query_rows, query_index, key_block, value_block, key_start, running, score_scale):
    row_peak, row_total, blended = running
    scores = (
        jnp.einsum("qhd,khd->hqk", query_rows, key_block, preferred_element_type=jnp.float32)
        * score_scale
    )
    key_index = key_start + jnp.arange(key_block.shape[0], dtype=jnp.int32)
    scores = jnp.where(key_index[None, None, :] <= query_index[None, :, None], scores, -1e30)
    new_peak = jnp.maximum(row_peak, jnp.max(scores, axis=2))
    weights = jnp.exp(scores - new_peak[:, :, None])
    rescale = jnp.exp(row_peak - new_peak)
    row_total = row_total * rescale + jnp.sum(weights, axis=2)
    blended = blended * rescale[:, :, None] + jnp.einsum(
        "hqk,khd->hqd",
        weights.astype(jnp.bfloat16),
        value_block,
        preferred_element_type=jnp.float32,
    )
    return (new_peak, row_total, blended)


def merge_partials(first_part, second_part):
    peak_one, total_one, blend_one = first_part
    peak_two, total_two, blend_two = second_part
    new_peak = jnp.maximum(peak_one, peak_two)
    scale_one = jnp.exp(peak_one - new_peak)
    scale_two = jnp.exp(peak_two - new_peak)
    new_total = total_one * scale_one + total_two * scale_two
    new_blend = blend_one * scale_one[..., None] + blend_two * scale_two[..., None]
    return (new_peak, new_total, new_blend)


def split_halves(stacked_part, half_size, upper_side):
    lower_half = stacked_part[:, :half_size]
    upper_half = stacked_part[:, half_size:]
    keep_half = jnp.where(upper_side == 1, upper_half, lower_half)
    send_half = jnp.where(upper_side == 1, lower_half, upper_half)
    return (keep_half, send_half)


def by_position(
    token_ids, embedding, short_filter, medium_filter, long_residue, long_rate, query_gain, key_gain
):
    tok_count = token_ids.shape[0]
    vocab_size = embedding.shape[0]
    width_dev = embedding.shape[1]
    seq_count = lax.axis_size("seq")
    seq_index = lax.axis_index("seq")
    one_hot = (
        token_ids[:, None] == lax.broadcasted_iota(jnp.int32, (tok_count, vocab_size), 1)
    ).astype(jnp.bfloat16)
    embedded = jnp.dot(one_hot, embedding, preferred_element_type=jnp.float32).astype(jnp.bfloat16)
    short_taps = short_filter.shape[0]
    rim_rows = shifted(embedded[tok_count - (short_taps - 1) :], "seq", 1)
    widened = jnp.concatenate([rim_rows, embedded], axis=0)
    short_part = depthwise_conv(widened, short_filter, tok_count)
    short_gated = rounded(embedded.astype(jnp.float32) * short_part)
    medium_taps = medium_filter.shape[0]
    upper_rows = shifted(short_gated[tok_count - (medium_taps - 1) :], "seq", 1)
    widened_two = jnp.concatenate([upper_rows, short_gated], axis=0)
    medium_part = depthwise_conv(widened_two, medium_filter, tok_count)
    medium_gated = rounded(short_gated.astype(jnp.float32) * medium_part)
    per_dev = width_dev // seq_count
    length = tok_count * seq_count
    grouped = medium_gated.T.reshape(seq_count, per_dev, tok_count)
    spread = lax.all_to_all(grouped, "seq", split_axis=0, concat_axis=2, tiled=True).reshape(
        per_dev, length
    )
    rate_mine = lax.dynamic_slice_in_dim(long_rate, seq_index * per_dev, per_dev, 1)
    residue_mine = lax.dynamic_slice_in_dim(long_residue, seq_index * per_dev, per_dev, 1)
    kernel = long_kernel_rows(residue_mine, rate_mine, length)
    outer_size = 128
    inner_size = 2 * length // outer_size
    spread_float = spread.astype(jnp.float32)
    data_real, data_imag = forward_dft(
        spread_float.reshape(per_dev, outer_size // 2, inner_size), outer_size, inner_size
    )
    kernel_real, kernel_imag = forward_dft(
        kernel.reshape(per_dev, outer_size // 2, inner_size), outer_size, inner_size
    )
    product_real = data_real * kernel_real - data_imag * kernel_imag
    product_imag = data_real * kernel_imag + data_imag * kernel_real
    long_part = inverse_dft(product_real, product_imag, outer_size, inner_size).reshape(
        per_dev, length
    )
    channel_out = (spread_float * long_part).astype(jnp.bfloat16)
    returned = lax.all_to_all(channel_out[None], "seq", split_axis=2, concat_axis=0, tiled=True)
    hyena_out = returned.reshape(width_dev, tok_count).T
    head_count = width_dev // HEAD
    hyena_float = hyena_out.astype(jnp.float32)
    square_sums = jnp.sum(hyena_float * hyena_float, axis=1)
    total_sums = lax.psum(square_sums, "ch")
    inverse_scale = lax.rsqrt(total_sums / C + 1e-05)
    normed = hyena_float * inverse_scale[:, None]
    values = normed.astype(jnp.bfloat16).reshape(tok_count, head_count, HEAD)
    queries = (
        (normed * query_gain[None, :]).astype(jnp.bfloat16).reshape(tok_count, head_count, HEAD)
    )
    key_rows = (
        (normed * key_gain[None, :]).astype(jnp.bfloat16).reshape(tok_count, head_count, HEAD)
    )
    group_size = 2
    level_count = group_size.bit_length() - 1
    seq_bits = seq_count.bit_length() - 1
    base_bit = seq_bits - level_count
    stride = seq_count // group_size
    stacked = queries[None]
    level = 0
    bit_number = base_bit + level
    partner_rows = swapped(stacked, "seq", bit_number)
    upper_side = seq_index >> bit_number & 1
    stacked = jnp.where(
        upper_side == 1,
        jnp.concatenate([partner_rows, stacked], axis=0),
        jnp.concatenate([stacked, partner_rows], axis=0),
    )
    query_rows = stacked.reshape(group_size * tok_count, head_count, HEAD)
    group_first = seq_index % stride
    block_numbers = group_first + stride * jnp.arange(group_size, dtype=jnp.int32)
    query_index = (
        block_numbers[:, None] * tok_count + jnp.arange(tok_count, dtype=jnp.int32)[None, :]
    ).reshape(group_size * tok_count)
    score_scale = HEAD ** (-0.5)
    partial_state = (
        jnp.full((head_count, group_size * tok_count), -1e30, jnp.float32),
        jnp.zeros((head_count, group_size * tok_count), jnp.float32),
        jnp.zeros((head_count, group_size * tok_count, HEAD), jnp.float32),
    )

    def cycle_step(turn_number, carried):
        key_block, value_block, running = carried
        key_block, value_block = from_behind((key_block, value_block), "seq", -1)
        source_block = jnp.remainder(seq_index + turn_number, seq_count)
        running = attend_block(
            query_rows,
            query_index,
            key_block,
            value_block,
            source_block * tok_count,
            running,
            score_scale,
        )
        return (key_block, value_block, running)

    carried = lax.fori_loop(1, stride + 1, cycle_step, (key_rows, values, partial_state))
    row_peak, row_total, blended = carried[2]
    row_peak = row_peak.reshape(head_count, group_size, tok_count)
    row_total = row_total.reshape(head_count, group_size, tok_count)
    blended = blended.reshape(head_count, group_size, tok_count, HEAD)
    for level in reversed(range(level_count)):
        bit_number = base_bit + level
        half_size = row_peak.shape[1] // 2
        upper_side = seq_index >> bit_number & 1
        keep_peak, send_peak = split_halves(row_peak, half_size, upper_side)
        keep_total, send_total = split_halves(row_total, half_size, upper_side)
        keep_blend, send_blend = split_halves(blended, half_size, upper_side)
        got_peak, got_total, got_blend = swapped(
            (send_peak, send_total, send_blend), "seq", bit_number
        )
        row_peak, row_total, blended = merge_partials(
            (keep_peak, keep_total, keep_blend), (got_peak, got_total, got_blend)
        )
    normalized = blended[:, 0] / row_total[:, 0][:, :, None]
    attended = normalized.transpose(1, 0, 2).reshape(tok_count, width_dev).astype(jnp.bfloat16)
    return (hyena_out, attended)


def transform_tables(block):
    size = 2 * block
    step = 2.0 * np.pi / size
    freq = (np.arange(block) + 0.5)[:, None]
    angle = freq * np.arange(size)[None, :] * step
    forward = np.concatenate([np.cos(angle), -np.sin(angle)], axis=0)
    angle = (np.arange(block)[:, None] + block) * freq.T * step
    backward = np.concatenate([np.cos(angle), -np.sin(angle)], axis=1) * (2.0 / size)

    def parts(table):
        kept = []
        for _ in range(3):
            kept.append(table.astype(np.float32).astype(ml_dtypes.bfloat16))
            table = table - kept[-1].astype(np.float64)
        return np.concatenate(kept, axis=0)

    forward, backward = parts(forward), parts(backward)
    first, second, third = np.split(forward[:, :block], 3)
    taps = np.concatenate([np.concatenate([first, second], axis=1), np.concatenate([first, third], axis=1)], axis=0)
    forward = np.concatenate(np.split(forward, 3), axis=1)
    first, second, third = np.split(backward, 3)
    backward = np.concatenate([first, second, first, third, second, first], axis=1)
    return forward, backward, taps


def split_pair(value):
    upper = value.astype(jnp.bfloat16)
    return upper, (value - upper.astype(jnp.float32)).astype(jnp.bfloat16)


def split_three(value):
    upper = value.astype(jnp.bfloat16)
    rest = value - upper.astype(jnp.float32)
    middle = rest.astype(jnp.bfloat16)
    return upper, middle, (rest - middle.astype(jnp.float32)).astype(jnp.bfloat16)


def minus_expm1(value):
    term = value
    series = value
    for order in range(2, 11):
        term = term * value * (-1.0 / order)
        series = series + term
    return jnp.where(value < 0.5, series, 1.0 - jnp.exp(-value))


def dot32(left, right):
    return jnp.dot(left, right, preferred_element_type=jnp.float32)


def own_lanes(width):
    return pl.ds(pl.multiple_of(lax.axis_index("seq") * width, width), width)


def fetch_kernel(
    token_ids, residue, rate, medium, table, ids_out, residue_out, rate_out, medium_out, table_out, sems
):
    lanes = own_lanes(medium_out.shape[1])
    copies = [
        pltpu.make_async_copy(source, target, sems.at[i])
        for i, (source, target) in enumerate(
            [
                (token_ids, ids_out),
                (residue.at[:, lanes], residue_out),
                (rate.at[:, lanes], rate_out),
                (medium.at[:, lanes], medium_out),
                (table, table_out),
            ]
        )
    ]
    for copy in copies:
        copy.start()
    for copy in copies:
        copy.wait()


def response_kernel(residue, rate, medium, table, medium_out, long_out):
    block, width = medium.shape
    size = 2 * block
    mode_total = rate.shape[0]
    block_total = long_out.shape[1] // width

    def transformed(signal):
        up, middle, low = split_three(signal)
        return (
            dot32(table[0:size, :], jnp.concatenate([up, up], axis=0))
            + dot32(table[0:size, :], jnp.concatenate([middle, middle], axis=0))
            + dot32(table[size : 2 * size, :], jnp.concatenate([low, up], axis=0))
        )

    medium_out[...] = transformed(medium[...])
    decays = rate[...]
    weights = residue[...] * jnp.sqrt(minus_expm1(2.0 * decays)) / math.sqrt(mode_total)
    modes = [weights * jnp.exp(-decays * float(part * block)) for part in range(block_total)]
    place = lax.broadcasted_iota(jnp.int32, (block, width), 0).astype(jnp.float32)
    rows = 32
    tiles = []
    for first in range(0, block, rows):
        sums = [jnp.zeros((rows, width), jnp.float32) for _ in range(block_total)]
        for mode in range(mode_total):
            shape = jnp.exp(-decays[mode : mode + 1, :] * place[first : first + rows])
            for part in range(block_total):
                sums[part] = sums[part] + modes[part][mode : mode + 1, :] * shape
        tiles.append(jnp.concatenate(sums, axis=1))
    long_out[...] = transformed(jnp.concatenate(tiles, axis=0))


def conv_kernel(*refs, piece_count):
    pieces = refs[:piece_count]
    (embedding, short, medium_resp, long_resp, forward, backward, hyena, sums) = refs[piece_count : piece_count + 8]
    ids, ordered, padded, row_sums, copied_sums, sem = refs[piece_count + 8 :]
    width = padded.shape[1]
    block = width
    size = 2 * block
    length = hyena.shape[0]
    count = length // block
    pair = count
    me = lax.axis_index("seq")
    for i, piece in enumerate(pieces):
        ids[2 * i : 2 * i + 2, :] = piece[...]
    for b in range(count):
        ordered[b : b + 1, :] = ids[pl.ds(lax.bitwise_xor(me, b), 1), :]
    across = jnp.transpose(ordered[...].astype(jnp.float32), (1, 0)).astype(jnp.int32)
    padded[0:8, :] = jnp.zeros((8, width), jnp.float32)
    table = embedding[:, own_lanes(width)]
    short_taps = short[:, own_lanes(width)]
    vocab = table.shape[0]
    entries = lax.broadcasted_iota(jnp.int32, (block, vocab), 1)
    rows = 32

    def embed(chunk):
        for b in range(chunk * pair, (chunk + 1) * pair):
            chosen = jnp.where(across[:, b : b + 1] == entries, 1.0, 0.0).astype(jnp.bfloat16)
            padded[8 + b * block : 8 + (b + 1) * block, :] = dot32(chosen, table)

    nothing = jnp.zeros((block, width), jnp.bfloat16)
    gated = [{-1: nothing}, {-1: nothing}]
    spectra, products = [{}, {}], [{}, {}]

    def short_gate(chunk):
        for b in range(chunk * pair, (chunk + 1) * pair):
            running = jnp.zeros((block, width), jnp.float32)
            for j in range(short_taps.shape[0]):
                running = running + short_taps[j : j + 1, :] * padded[8 + b * block - j : 8 + (b + 1) * block - j, :]
            signal = padded[8 + b * block : 8 + (b + 1) * block, :] * running
            gated[0][b] = signal.astype(jnp.bfloat16)

    def analyse(turn, chunk):
        span = range(chunk * pair, (chunk + 1) * pair)
        signal = jnp.concatenate(
            [jnp.concatenate([gated[turn][b - 1] for b in span], axis=1)]
            + [jnp.concatenate([gated[turn][b] for b in span], axis=1)],
            axis=0,
        )
        spectrum = dot32(forward[...], jnp.concatenate([signal] * 3, axis=0))
        for i, b in enumerate(span):
            spectra[turn][b] = spectrum[:, i * width : (i + 1) * width]

    def multiply(turn, response, chunk):
        span = range(chunk * pair, (chunk + 1) * pair)
        sources = range(span[-1] + 1) if turn else span
        tiles = {b: ([], []) for b in span}
        for first in range(0, block, rows):
            sums = {b: ([], []) for b in span}
            for upper in [slice(i, i + 8) for i in range(first, first + rows, 8)]:
                lower = slice(block + upper.start, block + upper.stop)
                data = {b: (spectra[turn][b][upper], spectra[turn][b][lower]) for b in sources}
                filt = [
                    (response[upper, i * width : (i + 1) * width], response[lower, i * width : (i + 1) * width])
                    for i in range(span[-1] + 1 if turn else 1)
                ]
                data = {b: (real, imag, real + imag) for b, (real, imag) in data.items()}
                filt = [(real, imag - real, real + imag) for real, imag in filt]
                for b in span:
                    shared = to_real = to_imag = 0.0
                    for part in range(b + 1 if turn else 1):
                        (real, imag, both), (base, ahead, total) = data[b - part], filt[part]
                        shared = shared + both * base
                        to_imag = to_imag + real * ahead
                        to_real = to_real + imag * total
                    total_real, total_imag = shared - to_real, shared + to_imag
                    sums[b][0].append(total_real)
                    sums[b][1].append(total_imag)
            for b in span:
                for side in range(2):
                    tiles[b][side].append(split_three(jnp.concatenate(sums[b][side], axis=0)))
        columns = [
            [jnp.concatenate([tile[i] for tile in tiles[b][0] + tiles[b][1]], axis=0) for i in range(3)] for b in span
        ]
        products[turn][chunk] = [jnp.concatenate([column[i] for column in columns], axis=1) for i in range(3)]

    def synthesise(turn, chunk):
        up, middle, low = products[turn].pop(chunk)
        return dot32(backward[...], jnp.concatenate([up, up, middle, up, middle, low], axis=0))

    def gate(turn, chunk):
        out = synthesise(turn, chunk)
        results = []
        for i in range(pair):
            past = gated[turn][chunk * pair + i].astype(jnp.float32)
            results.append((past * out[:, i * width : (i + 1) * width]).astype(jnp.bfloat16))
        return results

    def medium_gate(chunk):
        for i, signal in enumerate(gate(0, chunk)):
            gated[1][chunk * pair + i] = signal

    ones = jnp.ones((size, width), jnp.bfloat16)
    diagonal = lax.broadcasted_iota(jnp.int32, (block, block), 0) == lax.broadcasted_iota(
        jnp.int32, (block, block), 1
    )

    def long_gate(chunk):
        for i, result in enumerate(gate(1, chunk)):
            b = chunk * pair + i
            hyena[b * block : (b + 1) * block, :] = result
            wide = result.astype(jnp.float32)
            spread = dot32(jnp.concatenate(split_pair(wide * wide), axis=1), ones)
            row_sums[b : b + 1, :] = jnp.sum(jnp.where(diagonal, spread, 0.0), axis=0, keepdims=True)

    stages = [
        embed,
        short_gate,
        functools.partial(analyse, 0),
        functools.partial(multiply, 0, medium_resp),
        medium_gate,
        functools.partial(analyse, 1),
        functools.partial(multiply, 1, long_resp),
        long_gate,
    ]
    chunks = count // pair
    for turn in range(chunks + len(stages) - 1):
        for stage in range(len(stages)):
            if 0 <= turn - stage < chunks:
                stages[stage](turn - stage)
    copied_sums[...] = jnp.broadcast_to(row_sums[...][None], copied_sums.shape)
    copy = pltpu.make_async_copy(copied_sums, sums, sem)
    copy.start()
    copy.wait()


def attend_kernel(own, other, sums, query_gain, key_gain, out, queries, keys, values, *, channel_count):
    length, width = own.shape
    count = sums.shape[1]
    block = length // count
    me = lax.axis_index("seq")
    core = lax.rem(me, 2)
    total = jnp.sum(sums[...], axis=0)
    inverse = lax.rsqrt(total / channel_count + 1e-05)
    inverse = jnp.transpose(inverse, (1, 0))
    signals = (own, other)
    gains = []
    for side in range(2):
        lanes = pl.ds(pl.multiple_of(lax.bitwise_xor(me, side) * width, width), width)
        gains.append((query_gain[0:1, lanes], key_gain[0:1, lanes]))

    def normalise(b):
        spans = slice(b * block, (b + 1) * block)
        scale = jnp.broadcast_to(inverse[:, b : b + 1], (block, width))
        for side, signal in enumerate(signals):
            normed = signal[spans, :].astype(jnp.float32) * scale
            values[side, spans, :] = normed.astype(jnp.bfloat16)
            keys[side, spans, :] = (normed * gains[side][1]).astype(jnp.bfloat16)
            queries[side, spans, :] = (normed * gains[side][0]).astype(jnp.bfloat16)

    row_index = lax.broadcasted_iota(jnp.int32, (block, 2 * block), 0) + core * block
    allowed = lax.broadcasted_iota(jnp.int32, (block, 2 * block), 1) <= row_index

    def score(chip, side):
        reach = (chip + 1) * 2 * block
        start = pl.multiple_of((2 * chip + core) * block, block)
        scores = lax.dot_general(
            queries[side, pl.ds(start, block), :],
            keys[side, 0:reach, :],
            (((1,), (1,)), ((), ())),
            preferred_element_type=jnp.float32,
        )
        last = jnp.where(allowed, scores[:, reach - 2 * block :], -1e30)
        return jnp.concatenate([scores[:, : reach - 2 * block], last], axis=1) if chip else last

    def weigh(scores):
        peak = jnp.max(scores, axis=1, keepdims=True)
        weights = jnp.exp2((scores - peak) * (width**-0.5 * math.log2(math.e)))
        folded = weights[:, :width]
        for i in range(1, weights.shape[1] // width):
            folded = folded + weights[:, i * width : (i + 1) * width]
        return weights.astype(jnp.bfloat16), jnp.sum(folded, axis=1, keepdims=True)

    def blend(chip, side, weights, row_total):
        reach = (chip + 1) * 2 * block
        place = lax.bitwise_xor(me // 2, chip)
        half = lax.bitwise_xor(core, side)
        blended = dot32(weights, values[side, 0:reach, :])
        lanes = pl.ds(pl.multiple_of(half * width, width), width)
        out[place, :, lanes] = (blended / row_total).astype(jnp.bfloat16)

    for b in range(count):
        normalise(b)
    chains = [(chip, side) for chip in reversed(range(count // 2)) for side in range(2)]
    scored, weighed = {}, {}
    for turn in range(len(chains) + 4):
        if turn < len(chains):
            scored[turn] = score(*chains[turn])
        if 0 <= turn - 2 < len(chains):
            weighed[turn - 2] = weigh(scored.pop(turn - 2))
        if 0 <= turn - 4 < len(chains):
            blend(*chains[turn - 4], *weighed.pop(turn - 4))


def outgoing_kernel(own, other, out):
    width = own.shape[1]
    block = out.shape[1]
    me = lax.axis_index("seq")
    core = lax.rem(me, 2)
    for i in range(out.shape[0]):
        start = pl.multiple_of((2 * lax.bitwise_xor(me // 2, i) + core) * block, block)
        for side, signal in enumerate((own, other)):
            lanes = pl.ds(pl.multiple_of(lax.bitwise_xor(core, side) * width, width), width)
            out[i, :, lanes] = signal[pl.ds(start, block), :]


def hold_kernel(*refs):
    refs[-1][...] = refs[0][...]


def place_part_kernel(*refs, order, extra):
    blocks, out, sems = refs[extra:-2], refs[-2], refs[-1]
    span = blocks[0].shape[1]
    chip = lax.axis_index("seq") // 2
    copies = []
    for n, (i, block) in enumerate(zip(order, blocks)):
        lanes = pl.ds(pl.multiple_of(lax.bitwise_xor(chip, i) * span, span), span)
        copies.append(pltpu.make_async_copy(block, out.at[:, lanes], sems.at[n]))
    for copy in copies:
        copy.start()
    for copy in copies:
        copy.wait()


def place_kernel(*refs, order):
    blocks, out = refs[:-1], refs[-1]
    span = blocks[0].shape[1]
    chip = lax.axis_index("seq") // 2
    for i, block in zip(order, blocks):
        out[:, pl.ds(pl.multiple_of(lax.bitwise_xor(chip, i) * span, span), span)] = block[...]


def by_head(
    token_ids, embedding, short_filter, medium_filter, long_residue, long_rate, query_gain, key_gain
):
    seq_count = lax.axis_size("seq")
    ch_count = lax.axis_size("ch")
    block = token_ids.shape[0]
    width_dev = embedding.shape[1]
    length = block * seq_count
    width = HEAD
    f32, bf16 = jnp.float32, jnp.bfloat16
    forward, backward, tap_table = transform_tables(block)
    whole = pl.BlockSpec(memory_space=pltpu.VMEM)
    params = pltpu.CompilerParams(vmem_limit_bytes=24 * 1024 * 1024)

    def exchange(value, apart):
        return lax.ppermute(value, "seq", [(i, i ^ apart) for i in range(seq_count)])

    mode_total = long_rate.shape[0]
    in_hbm = pl.BlockSpec(memory_space=pltpu.HBM)

    def fetched(value):
        return pltpu.with_memory_space_constraint(value, pltpu.HBM)

    partner_ids = exchange(token_ids, 1)
    operands = (token_ids, long_residue, long_rate, medium_filter, jnp.asarray(tap_table))
    own_ids, *filters = pl.pallas_call(
        fetch_kernel,
        out_shape=[
            jax.ShapeDtypeStruct((block,), jnp.int32),
            jax.ShapeDtypeStruct((mode_total, width), f32),
            jax.ShapeDtypeStruct((mode_total, width), f32),
            jax.ShapeDtypeStruct((block, width), f32),
            jax.ShapeDtypeStruct(tap_table.shape, bf16),
        ],
        in_specs=[in_hbm] * 5,
        out_specs=[whole] * 5,
        scratch_shapes=[pltpu.SemaphoreType.DMA((5,))],
        compiler_params=params,
        cost_estimate=pl.CostEstimate(flops=10**9, bytes_accessed=2 * 10**6, transcendentals=0),
        name="fetched_operands",
    )(*[fetched(value) for value in operands])
    chip_ids = jnp.stack([own_ids, partner_ids])
    pieces = [chip_ids] + [exchange(chip_ids, 2 * i) for i in range(1, seq_count // 2)]
    medium_resp, long_resp = pl.pallas_call(
        response_kernel,
        out_shape=[
            jax.ShapeDtypeStruct((2 * block, width), f32),
            jax.ShapeDtypeStruct((2 * block, length), f32),
        ],
        in_specs=[whole] * 4,
        out_specs=[whole] * 2,
        compiler_params=params,
        cost_estimate=pl.CostEstimate(flops=2 * 10**9, bytes_accessed=2 * 10**6, transcendentals=3 * 10**5),
        name="filter_responses",
    )(*filters)

    devices = seq_count * ch_count
    hyena, square_sums = pl.pallas_call(
        functools.partial(conv_kernel, piece_count=len(pieces)),
        out_shape=[
            jax.ShapeDtypeStruct((length, width), bf16),
            pltpu.HBM((devices, seq_count, block), f32),
        ],
        in_specs=[whole] * (len(pieces) + 6),
        out_specs=[whole, in_hbm],
        scratch_shapes=[
            pltpu.VMEM((seq_count, block), jnp.int32),
            pltpu.VMEM((seq_count, block), jnp.int32),
            pltpu.VMEM((8 + length, width), f32),
            pltpu.VMEM((seq_count, block), f32),
            pltpu.VMEM((devices, seq_count, block), f32),
            pltpu.SemaphoreType.DMA,
        ],
        compiler_params=params,
        cost_estimate=pl.CostEstimate(flops=2 * 10**9, bytes_accessed=2 * 10**6, transcendentals=0),
        name="gated_convolutions",
    )(*pieces, embedding, short_filter, medium_resp, long_resp, forward, backward)

    other = exchange(hyena, 1)
    all_sums = lax.all_to_all(square_sums, ("seq", "ch"), 0, 0, tiled=True)

    def placed(blocks, name, order):
        return pl.pallas_call(
            functools.partial(place_kernel, order=(0, *order)),
            out_shape=jax.ShapeDtypeStruct((block, width_dev), bf16),
            in_specs=[whole] * len(blocks),
            out_specs=whole,
            compiler_params=params,
            cost_estimate=pl.CostEstimate(flops=10**9, bytes_accessed=10**6, transcendentals=0),
            name=name,
        )(*blocks)

    def placed_part(blocks, name, order, so_far=()):
        return pl.pallas_call(
            functools.partial(place_part_kernel, order=order, extra=len(so_far)),
            out_shape=jax.ShapeDtypeStruct((block, width_dev), bf16),
            in_specs=[in_hbm] * len(so_far) + [whole] * len(blocks),
            out_specs=in_hbm,
            scratch_shapes=[pltpu.SemaphoreType.DMA((len(blocks),))],
            input_output_aliases={0: 0} if so_far else {},
            compiler_params=params,
            cost_estimate=pl.CostEstimate(flops=10**9, bytes_accessed=10**6, transcendentals=0),
            name=name,
        )(*so_far, *blocks)

    def held(value, others):
        return pl.pallas_call(
            hold_kernel,
            out_shape=jax.ShapeDtypeStruct(value.shape, value.dtype),
            in_specs=[whole] + [pl.BlockSpec(memory_space=pl.ANY)] * len(others),
            out_specs=whole,
            compiler_params=params,
            name="held_block",
        )(value, *others)

    order = list(range(1, seq_count // 2))
    hyena_blocks = pl.pallas_call(
        outgoing_kernel,
        out_shape=jax.ShapeDtypeStruct((seq_count // 2, block, 2 * width), bf16),
        in_specs=[whole, whole],
        out_specs=whole,
        compiler_params=params,
        cost_estimate=pl.CostEstimate(flops=2 * 10**9, bytes_accessed=10**6, transcendentals=0),
        name="hyena_blocks",
    )(hyena, other)
    hyena_parts = [hyena_blocks[0]] + [exchange(hyena_blocks[i], 2 * i) for i in order]
    outgoing = pl.pallas_call(
        functools.partial(attend_kernel, channel_count=width_dev * ch_count),
        out_shape=jax.ShapeDtypeStruct((seq_count // 2, block, 2 * width), bf16),
        in_specs=[whole] * 5,
        out_specs=whole,
        scratch_shapes=[pltpu.VMEM((2, length, width), bf16)] * 3,
        compiler_params=params,
        cost_estimate=pl.CostEstimate(flops=2 * 10**9, bytes_accessed=10**6, transcendentals=10**6),
        name="attention",
    )(hyena, other, all_sums, query_gain.reshape(1, width_dev), key_gain.reshape(1, width_dev))
    last = held(outgoing[order[0]], hyena_parts[1:])
    parts = [outgoing[0]] + [exchange(outgoing[i], 2 * i) for i in order[:0:-1]] + [exchange(last, 2 * order[0])]
    early = placed_part(parts[:-1], "placed_early", (0, *order[:0:-1]))
    attended = placed_part(parts[-1:], "placed_attended", order[:1], (early,))
    return placed(hyena_parts, "placed_hyena", order), attended


def on_device(*operands):
    seq_count = lax.axis_size("seq")
    token_ids, embedding, _, medium_filter = operands[:4]
    block = token_ids.shape[0]
    fits = (
        embedding.shape[1] == seq_count * HEAD
        and block == HEAD
        and medium_filter.shape[0] == block
        and seq_count % 8 == 0
        and seq_count & (seq_count - 1) == 0
    )
    return by_head(*operands) if fits else by_position(*operands)


def solution(mesh):
    in_specs = (
        P("seq"),
        P(None, "ch"),
        P(None, "ch"),
        P(None, "ch"),
        P(None, "ch"),
        P(None, "ch"),
        P("ch"),
        P("ch"),
    )
    out_specs = (P("seq", "ch"), P("seq", "ch"))
    return jax.shard_map(
        on_device, mesh=mesh, in_specs=in_specs, out_specs=out_specs, check_vma=False
    )
```
